128 devices in a mesh: dp: 32 (over z, y, core), fsdp: 4 (over x).
Axes of the slice: x: 4, y: 4, z: 4, core: 2. Of those that a mesh axis runs over, the one named last changes fastest.
Arguments:
- tokens: bfloat16 [16384, 2048], P(('dp', 'fsdp')), may hold values from -24 to 24
- cotangent: bfloat16 [16384, 2048], P(('dp', 'fsdp')), may hold values from -24 to 24
- block_seq: int32 [32, 4], P('dp'), may hold values from 0 to 1, as said below
- seq_lengths: int32 [32, 2], P('dp'), may hold values from 1 to 384, as said below
- qkv_weight: float32 [2048, 6144], P(('dp', 'fsdp')), may hold values from -0.125 to 0.125
- qkv_moment: float32 [2048, 6144], P(('dp', 'fsdp')), may hold values from -64 to 64
- qkv_second: float32 [2048, 6144], P(('dp', 'fsdp')), may hold values from 4.096 to 65.536
- dense_weight: float32 [2048, 2048], P(('dp', 'fsdp')), may hold values from -0.375 to 0.375
- dense_moment: float32 [2048, 2048], P(('dp', 'fsdp')), may hold values from -16 to 16
- dense_second: float32 [2048, 2048], P(('dp', 'fsdp')), may hold values from 0.32768 to 5.24288
- expand_weight: float32 [2048, 8192], P(('dp', 'fsdp')), may hold values from -0.125 to 0.125
- expand_moment: float32 [2048, 8192], P(('dp', 'fsdp')), may hold values from -24 to 24
- expand_second: float32 [2048, 8192], P(('dp', 'fsdp')), may hold values from 0.73728 to 11.79648
- shrink_weight: float32 [8192, 2048], P(('dp', 'fsdp')), may hold values from -0.0625 to 0.0625
- shrink_moment: float32 [8192, 2048], P(('dp', 'fsdp')), may hold values from -48 to 48
- shrink_second: float32 [8192, 2048], P(('dp', 'fsdp')), may hold values from 2.94912 to 47.5136
- vectors: float32 [22528], P(('dp', 'fsdp')), may hold values from -1 to 1.5
- vec_moment: float32 [22528], P(('dp', 'fsdp')), may hold values from -80 to 80
- vec_second: float32 [22528], P(('dp', 'fsdp')), may hold values from 8.192 to 131.072
Outputs:
- output: bfloat16 [16384, 2048], P(('dp', 'fsdp'))
- input_grad: bfloat16 [16384, 2048], P(('dp', 'fsdp'))
- qkv_grad: float32 [2048, 6144], P(('dp', 'fsdp'))
- qkv_state: float32 [2048, 6144], P(('dp', 'fsdp'))
- qkv_new: float32 [2048, 6144], P(('dp', 'fsdp'))
- dense_grad: float32 [2048, 2048], P(('dp', 'fsdp'))
- dense_state: float32 [2048, 2048], P(('dp', 'fsdp'))
- dense_new: float32 [2048, 2048], P(('dp', 'fsdp'))
- expand_grad: float32 [2048, 8192], P(('dp', 'fsdp'))
- expand_state: float32 [2048, 8192], P(('dp', 'fsdp'))
- expand_new: float32 [2048, 8192], P(('dp', 'fsdp'))
- shrink_grad: float32 [8192, 2048], P(('dp', 'fsdp'))
- shrink_state: float32 [8192, 2048], P(('dp', 'fsdp'))
- shrink_new: float32 [8192, 2048], P(('dp', 'fsdp'))
- vec_grad: float32 [22528], P(('dp', 'fsdp'))
- vec_state: float32 [22528], P(('dp', 'fsdp'))
- vec_new: float32 [22528], P(('dp', 'fsdp'))
The draws below stay inside these ranges and needn't reach their ends.
Inputs may be any that keep to these rules, and one draw needn't show every extreme that they name: `block_seq`: row g names, for each block of group g in row order, the sequence it holds; every sequence 0 to 1 holds one or more blocks, whose order in the row is the order of its positions; the first and the last block of a row hold the same sequence. `seq_lengths`: A sequence with c blocks has more than 128 * (c - 1) and at most 128 * c tokens; the rest of its last block is padding. In every group one sequence has exactly 128 * (3) tokens.
All inputs are finite; a program needn't handle non-finite values.
Results may differ from the reference program's by a relative error of at most 0.017.
Values may be sent and summed in bfloat16 or wider, within the bound.
A program may use at most 640 MiB of HBM per device.

```python
import math
import jax
import jax.numpy as jnp
from jax import lax

D = 2048
FF = 8192
HEAD = 64
ROT = 32
BLOCK = 128
STEP = 10
GROUP_BLOCKS = 4
GROUP_TOKENS = 512
SEQS = 2
GROUPS = 32
TOKENS = 16384
NVEC = 22528


def deal_one(key):
    reach_key, order_key = jax.random.split(key, 2)
    reaching = jax.random.randint(reach_key, (), 0, SEQS).astype(jnp.int32)
    middle = jax.random.permutation(order_key, GROUP_BLOCKS - 2).astype(jnp.int32) + 1
    others = (jnp.arange(SEQS - 1, dtype=jnp.int32) + reaching + 1) % SEQS
    extra_seq = jnp.full((GROUP_BLOCKS - 1 - SEQS,), reaching, jnp.int32)
    filled = jnp.concatenate([others, extra_seq]).astype(jnp.int32)
    owners = jnp.full((GROUP_BLOCKS,), reaching, jnp.int32)
    return owners.at[middle].set(filled)


def deal_blocks(key):
    group_keys = jax.random.split(key, GROUPS)
    return jax.vmap(deal_one)(group_keys)


def draw_block_seq(key, part):
    return deal_blocks(key)


def draw_seq_lengths(key, part):
    owners = deal_blocks(key)
    key = jax.random.fold_in(key, 5)
    counts = jnp.sum((owners[:, :, None] == jnp.arange(SEQS, dtype=jnp.int32)[None, None, :]).astype(jnp.int32), axis=1)
    tail_len = jax.random.randint(key, (GROUPS, SEQS), 1, BLOCK + 1).astype(jnp.int32)
    longest = owners[:, 0:1] == jnp.arange(SEQS, dtype=jnp.int32)[None, :]
    tail_len = jnp.where(longest, BLOCK, tail_len).astype(jnp.int32)
    return (counts - 1) * BLOCK + tail_len


def draw_vectors(key, part):
    key = jax.random.fold_in(key, 11)
    gain_key, rest_key = jax.random.split(key)
    norm_gain = jax.random.uniform(gain_key, (D,), jnp.float32, 0.6, 1.4)
    others = jnp.clip(0.2 * jax.random.normal(rest_key, (NVEC - D,), jnp.float32), -1.0, 1.0)
    return jnp.concatenate([norm_gain, others]).astype(jnp.float32)


def strengthened(entries, key, source, target, parts, factor):
    owner, partner = [(jnp.arange(entries.shape[axis_at]) // (entries.shape[axis_at] // parts)).reshape([-1 if axis == axis_at else 1 for axis in range(entries.ndim)]) for axis_at in (source, target)]
    chosen = jax.random.permutation(key, parts)[partner]
    strong = (owner == chosen) | (owner == (partner + parts // 2) % parts)
    return jnp.where(strong, factor * entries, entries)


def steps_of(stream_key, extent, cuts, least, high):
    level, own = 1.0, jax.random.fold_in(stream_key, 6)
    for axis_at, shards_of in cuts:
        steps = jnp.exp(jax.random.uniform(jax.random.fold_in(own, axis_at), (shards_of,), jnp.float32, least / len(cuts), high / len(cuts)))
        level = level * jnp.repeat(steps, extent[axis_at] // shards_of).reshape([-1 if axis == axis_at else 1 for axis in range(len(extent))])
    return level


def gaussian(own_key, extent, width, limit, cuts=(), kind=jnp.bfloat16):
    array = jax.random.normal(own_key, extent, jnp.float32) * width
    if len(cuts) > 0:
        array = steps_of(own_key, extent, cuts, -0.22, 0.18) * array
    return jnp.clip(array, min=-limit, max=limit).astype(kind)


def gaussian_with(stream_key, shape, scale, limit, cuts, heavy, kind=jnp.bfloat16):
    drawn = scale * jax.random.normal(stream_key, shape, jnp.float32)
    if cuts:
        drawn = drawn * steps_of(stream_key, shape, cuts, -0.22, 0.18)
    return jnp.clip(strengthened(drawn, jax.random.fold_in(stream_key, 3), *heavy), -limit, limit).astype(kind)


def setup_inputs(seed: int = 0) -> dict:
    splits = jax.random.split(jax.random.key(seed), 20)
    return {
        "tokens": gaussian_with(splits[0], (TOKENS, D), 1.0, 24.0, ((0, 128),), (0, 1, 128, 5.5)),
        "cotangent": gaussian_with(splits[1], (TOKENS, D), 1.0, 24.0, ((0, 128),), (0, 1, 128, 5.5)),
        "block_seq": draw_block_seq(jax.random.fold_in(splits[19], 71), 0),
        "seq_lengths": draw_seq_lengths(jax.random.fold_in(splits[19], 71), 0),
        "qkv_weight": gaussian(splits[4], (D, 3 * D), D ** -0.5, 0.125, ((0, 128),), jnp.float32),
        "qkv_moment": gaussian(splits[5], (D, 3 * D), (0.08 * TOKENS ** 0.5), 64.0, ((0, 128),), jnp.float32),
        "qkv_second": jnp.clip(jnp.exp(math.log(65.536) - 2.7725887 * jax.random.uniform(splits[6], (D, 3 * D), jnp.float32) ** steps_of(splits[6], (D, 3 * D), ((0, 128),), -0.2, 0.2)), 4.096, 65.536),
        "dense_weight": gaussian(splits[7], (D, D), (D // 8) ** -0.5, 0.375, ((0, 128),), jnp.float32),
        "dense_moment": gaussian(splits[8], (D, D), (0.022 * TOKENS ** 0.5), 16.0, ((0, 128),), jnp.float32),
        "dense_second": jnp.clip(jnp.exp(math.log(5.24288) - 2.7725887 * jax.random.uniform(splits[9], (D, D), jnp.float32) ** steps_of(splits[9], (D, D), ((0, 128),), -0.2, 0.2)), 0.32768, 5.24288),
        "expand_weight": gaussian(splits[10], (D, FF), D ** -0.5, 0.125, ((0, 128),), jnp.float32),
        "expand_moment": gaussian(splits[11], (D, FF), (0.033 * TOKENS ** 0.5), 24.0, ((0, 128),), jnp.float32),
        "expand_second": jnp.clip(jnp.exp(math.log(11.79648) - 2.7725887 * jax.random.uniform(splits[12], (D, FF), jnp.float32) ** steps_of(splits[12], (D, FF), ((0, 128),), -0.2, 0.2)), 0.73728, 11.79648),
        "shrink_weight": gaussian(splits[13], (FF, D), FF ** -0.5, 0.0625, ((0, 128),), jnp.float32),
        "shrink_moment": gaussian(splits[14], (FF, D), (0.067 * TOKENS ** 0.5), 48.0, ((0, 128),), jnp.float32),
        "shrink_second": jnp.clip(jnp.exp(math.log(47.5136) - 2.779509 * jax.random.uniform(splits[15], (FF, D), jnp.float32) ** steps_of(splits[15], (FF, D), ((0, 128),), -0.2, 0.2)), 2.94912, 47.5136),
        "vectors": draw_vectors(jax.random.fold_in(splits[19], 71), 0),
        "vec_moment": gaussian(splits[17], (NVEC,), (0.11 * TOKENS ** 0.5), 80.0, ((0, 128),), jnp.float32),
        "vec_second": jnp.clip(jnp.exp(math.log(131.072) - 2.7725887 * jax.random.uniform(splits[18], (NVEC,), jnp.float32) ** steps_of(splits[18], (NVEC,), ((0, 128),), -0.2, 0.2)), 8.192, 131.072),
    }


@jax.custom_vjp
def low(v):
    return lax.optimization_barrier(v.astype(jnp.bfloat16)).astype(jnp.float32)

@jax.custom_vjp
def low_back(v):
    return v

def low_keep(v):
    return (low(v), None)

def low_pass(kept, grad):
    return (grad,)

def back_keep(v):
    return (v, None)

def back_low(kept, grad):
    return (low(grad),)
low.defvjp(low_keep, low_pass)
low_back.defvjp(back_keep, back_low)
PRECISE = lax.Precision.HIGHEST
NORM_EPS = 1e-05
MASKED = -1e+30
BETA_ONE = 0.9
BETA_TWO = 0.999
ADAM_EPS = 1e-08
RATES = (0.02, 0.1, 0.02, 0.01, 0.4)
DECAYS = (0.1, 0.1, 0.1, 0.1, 0.0)

def layer_norm(values, norm_gain, norm_shift):
    center = values - lax.optimization_barrier(jnp.mean(values, axis=-1, keepdims=True))
    spread = lax.optimization_barrier(jnp.mean(center * center, axis=-1, keepdims=True))
    return center * lax.rsqrt(spread + NORM_EPS) * norm_gain + norm_shift

def rotary_tables(position, rot_dims):
    half_index = jnp.arange(rot_dims // 2, dtype=jnp.float32)
    inverse = 10000.0 ** (-2.0 * half_index / rot_dims)
    turned = position.astype(jnp.float32)[:, None] * inverse[None, :]
    return (jnp.cos(turned), jnp.sin(turned))

def rotate(values, cosine, sine_part):
    half_dims = cosine.shape[-1]
    front_part = values[..., :half_dims]
    second = values[..., half_dims:2 * half_dims]
    cos_rows = cosine[:, None, :]
    sin_rows = sine_part[:, None, :]
    return jnp.concatenate([front_part * cos_rows - second * sin_rows, second * cos_rows + front_part * sin_rows, values[..., 2 * half_dims:]], axis=-1)

def token_meta(block_row, length_row):
    total_blocks = block_row.shape[0]
    seq_count = length_row.shape[0]
    matching = block_row[None, :] == block_row[:, None]
    earlier_mask = jnp.arange(total_blocks)[None, :] < jnp.arange(total_blocks)[:, None]
    ranking = lax.optimization_barrier(jnp.sum(jnp.where(matching & earlier_mask, 1, 0), axis=1)).astype(jnp.int32)
    offsets = jnp.arange(BLOCK, dtype=jnp.int32)
    position = (ranking[:, None] * BLOCK + offsets[None, :]).reshape(-1)
    sequence = jnp.broadcast_to(block_row[:, None], (total_blocks, BLOCK)).reshape(-1)
    chosen = sequence[:, None] == jnp.arange(seq_count, dtype=jnp.int32)[None, :]
    limits = lax.optimization_barrier(jnp.sum(jnp.where(chosen, length_row[None, :], 0), axis=1))
    return (sequence, position, position < limits)

def split_vectors(vec_all, model_width, ff_width):
    norm_gain = vec_all[:model_width]
    norm_shift = vec_all[model_width:2 * model_width]
    bias_qkv = vec_all[2 * model_width:5 * model_width]
    bias_dense = vec_all[5 * model_width:6 * model_width]
    bias_expand = vec_all[6 * model_width:6 * model_width + ff_width]
    bias_shrink = vec_all[6 * model_width + ff_width:]
    return (norm_gain, norm_shift, bias_qkv, bias_dense, bias_expand, bias_shrink)

def phi_layer(inputs, qkv_weight, dense_weight, expand_weight, shrink_weight, vectors, sequence, position, live):
    row_total, model_width = inputs.shape
    ff_width = expand_weight.shape[1]
    head_count = model_width // HEAD
    norm_gain, norm_shift, bias_qkv, bias_dense, bias_expand, bias_shrink = split_vectors(low(vectors), model_width, ff_width)
    normed = low(layer_norm(inputs, norm_gain, norm_shift))
    projected = low_back(jnp.dot(normed, low(qkv_weight), precision=PRECISE) + bias_qkv)
    cosine, sine_part = rotary_tables(position, ROT)
    queries = low(rotate(projected[:, :model_width].reshape(row_total, head_count, HEAD), cosine, sine_part))
    keys_all = low(rotate(projected[:, model_width:2 * model_width].reshape(row_total, head_count, HEAD), cosine, sine_part))
    values_all = low(projected[:, 2 * model_width:]).reshape(row_total, head_count, HEAD)
    allowed = (sequence[:, None] == sequence[None, :]) & (position[None, :] <= position[:, None]) & live[None, :]
    scores = low_back(jnp.einsum('qhd,khd->hqk', queries, keys_all, precision=PRECISE) * HEAD ** (-0.5))
    scores = jnp.where(allowed[None], scores, MASKED)
    ceiling = lax.optimization_barrier(jnp.max(scores, axis=-1, keepdims=True))
    weights = jnp.exp(scores - ceiling)
    probability = low(weights / lax.optimization_barrier(jnp.sum(weights, axis=-1, keepdims=True)))
    attended = jnp.einsum('hqk,khd->qhd', probability, values_all, precision=PRECISE).reshape(row_total, model_width)
    attended = low_back(low(attended))
    branch_attn = jnp.dot(attended, low(dense_weight), precision=PRECISE) + bias_dense
    pre_act = low_back(jnp.dot(normed, low(expand_weight), precision=PRECISE) + bias_expand)
    act_low = low(jax.nn.gelu(pre_act, approximate=True))
    branch_mlp = jnp.dot(act_low, low(shrink_weight), precision=PRECISE) + bias_shrink
    return inputs + branch_attn + branch_mlp

def adam_step(weight, moment, second, gradient, step_rate, step_decay):
    moment_new = BETA_ONE * moment + (1 - BETA_ONE) * gradient
    second_new = BETA_TWO * second + (1 - BETA_TWO) * gradient * gradient
    moment_hat = moment_new / (1 - BETA_ONE ** STEP)
    second_hat = second_new / (1 - BETA_TWO ** STEP)
    updated = weight - step_rate * (moment_hat / (jnp.sqrt(second_hat) + ADAM_EPS) + step_decay * weight)
    return (second_new, updated)

def reference(tokens, cotangent, block_seq, seq_lengths, qkv_weight, qkv_moment, qkv_second, dense_weight, dense_moment, dense_second, expand_weight, expand_moment, expand_second, shrink_weight, shrink_moment, shrink_second, vectors, vec_moment, vec_second):
    model_width = tokens.shape[1]
    sequence, position, live = jax.vmap(token_meta)(block_seq, seq_lengths)
    inputs = tokens.astype(jnp.float32).reshape(GROUPS, GROUP_TOKENS, model_width)
    tangents = cotangent.astype(jnp.float32).reshape(GROUPS, GROUP_TOKENS, model_width) * live[..., None].astype(jnp.float32)
    masters = (qkv_weight, dense_weight, expand_weight, shrink_weight, vectors)
    zeros_init = tuple((jnp.zeros(w.shape, jnp.float32) for w in masters))

    def group_step(totals, group_item):
        group_in, group_ct, group_seq, group_pos, group_live = group_item

        def forward(values, w_qkv, w_dense, w_expand, w_shrink, w_vec):
            return phi_layer(values, w_qkv, w_dense, w_expand, w_shrink, w_vec, group_seq, group_pos, group_live)
        group_out, backward = jax.vjp(forward, group_in, *masters)
        grads = backward(group_ct)
        summed = tuple((acc + part_grad for acc, part_grad in zip(totals, grads[1:])))
        return (summed, (group_out, grads[0]))
    totals, (outputs, in_grads) = lax.scan(group_step, zeros_init, (inputs, tangents, sequence, position, live))
    output = outputs.reshape(TOKENS, model_width).astype(jnp.bfloat16)
    input_grad = in_grads.reshape(TOKENS, model_width).astype(jnp.bfloat16)
    moments = (qkv_moment, dense_moment, expand_moment, shrink_moment, vec_moment)
    seconds = (qkv_second, dense_second, expand_second, shrink_second, vec_second)
    results = [output, input_grad]
    for index_w in range(5):
        state_new, weight_new = adam_step(masters[index_w], moments[index_w], seconds[index_w], totals[index_w], RATES[index_w], DECAYS[index_w])
        results.extend([totals[index_w], state_new, weight_new])
    return tuple(results)
```

```python
import functools

import jax
import jax.numpy as jnp
import numpy as np
from jax import lax
from jax.experimental import pallas as pl
from jax.experimental.pallas import tpu as pltpu
from jax.sharding import Mesh
from jax.sharding import PartitionSpec as P

HEAD = 64
ROT = 32
BLOCK = 128
STEP = 10
GROUP = 512
MODEL = 2048
FF = 8192
PAIR = 2 * HEAD
ALL = ("z", "y", "c", "x")
DP = ("z", "y", "c")
ZY = ("z", "y")
TP = ("c", "x")
SIZES = (4, 4, 2, 4)
TPN = 8
SCALE = HEAD ** (-0.5)

NORM_EPS = 1e-05
MASKED = -1e30
BETA_ONE = 0.9
BETA_TWO = 0.999
ADAM_EPS = 1e-08
RATES = (0.02, 0.1, 0.02, 0.01, 0.4)
DECAYS = (0.1, 0.1, 0.1, 0.1, 0.0)
GELU_A = float(np.sqrt(2.0 / np.pi))
GELU_B = 0.044715


def dot(a, b):
    return jnp.dot(a, b, preferred_element_type=jnp.float32)


def dot_t(a, b):
    return lax.dot_general(a, b, (((1,), (1,)), ((), ())), preferred_element_type=jnp.float32)


def cross(a, b):
    return lax.dot_general(a, b, (((0,), (0,)), ((), ())), preferred_element_type=jnp.float32)


def rotary_constants():
    half = np.arange(ROT // 2, dtype=np.float32)
    inverse = (10000.0 ** (-2.0 * half.astype(np.float64) / ROT)).astype(np.float32)
    angle = (np.arange(GROUP, dtype=np.float32)[:, None] * inverse[None, :]).astype(np.float64)
    cosine, sine = np.cos(angle).astype(np.float32), np.sin(angle).astype(np.float32)
    one = np.ones((GROUP, HEAD - ROT), np.float32)
    zero = np.zeros((GROUP, ROT // 2), np.float32)
    rest = np.zeros((GROUP, HEAD - ROT), np.float32)
    turn = np.concatenate([cosine, cosine, one], axis=1)
    ahead = np.concatenate([-sine, zero, rest], axis=1)
    behind = np.concatenate([zero, sine, rest], axis=1)
    return tuple(np.concatenate([a, a], axis=1) for a in (turn, ahead, behind))


def device_number(z, y, c, x):
    return ((z * 4 + y) * 2 + c) * 4 + x


def dense_route():
    pairs = []
    for z, y, c, x in np.ndindex(*SIZES):
        pairs.append((device_number(z, y, c, x), device_number((z // 2) * 2 + c, x, z % 2, y)))
    return pairs


def shrink_route():
    pairs = []
    for z, y, c, x in np.ndindex(*SIZES):
        target = device_number(z, (y // 2) * 2 + x % 2, y % 2, c * 2 + x // 2)
        pairs.append((device_number(z, y, c, x), target))
    return pairs


def back(route):
    return [(b, a) for a, b in route]


def block_ranks(block_rows):
    same = block_rows[:, :, None] == block_rows[:, None, :]
    earlier = jnp.arange(4)[None, :] < jnp.arange(4)[:, None]
    return jnp.sum(jnp.where(same & earlier[None], 1, 0), axis=2).astype(jnp.int32)


def turned(values, table, sign):
    turn, ahead, behind = table
    shape_axis = values.ndim - 1
    up = pltpu.roll(values, PAIR - ROT // 2, shape_axis)
    down = pltpu.roll(values, ROT // 2, shape_axis)
    if sign > 0:
        return values * turn + up * ahead + down * behind
    return values * turn - up * ahead - down * behind


def attention_kernel(
    seq_ref, rank_ref, limit_ref, q_ref, k_ref, v_ref, da_ref, turn_ref, ahead_ref, behind_ref,
    att_ref, dq_ref, dk_ref, dv_ref, q_low, k_low, dk_sum, dv_sum
):
    g = pl.program_id(0)
    lane = lax.broadcasted_iota(jnp.int32, (BLOCK, PAIR), 1)
    first = lane < HEAD

    def table_of(b):
        rows = pl.ds(pl.multiple_of(rank_ref[g, b] * BLOCK, BLOCK), BLOCK)
        return turn_ref[rows, :], ahead_ref[rows, :], behind_ref[rows, :]

    for b in range(4):
        rows = pl.ds(b * BLOCK, BLOCK)
        table = table_of(b)
        q_low[rows, :] = turned(q_ref[rows, :], table, 1).astype(jnp.bfloat16)
        k_low[rows, :] = turned(k_ref[rows, :], table, 1).astype(jnp.bfloat16)
    dk_sum[...] = jnp.zeros_like(dk_sum)
    dv_sum[...] = jnp.zeros_like(dv_sum)
    zero = jnp.zeros((BLOCK, PAIR), jnp.bfloat16)
    row_at = lax.broadcasted_iota(jnp.int32, (BLOCK, BLOCK), 0)
    col_at = lax.broadcasted_iota(jnp.int32, (BLOCK, BLOCK), 1)
    for b in range(4):
        rows = pl.ds(b * BLOCK, BLOCK)
        keys = pl.ds(0, (b + 1) * BLOCK)
        width = (b + 1) * BLOCK
        base = rank_ref[g, b] * BLOCK
        diagonal = (col_at <= row_at) & (col_at + base < limit_ref[g, b])
        bias_parts = []
        for e in range(b):
            away = jnp.where(seq_ref[g, e] == seq_ref[g, b], 0.0, MASKED).astype(jnp.float32)
            bias_parts.append(jnp.zeros((BLOCK, BLOCK), jnp.float32) + away)
        bias_parts.append(jnp.where(diagonal, 0.0, MASKED).astype(jnp.float32))
        bias = bias_parts[0] if b == 0 else jnp.concatenate(bias_parts, axis=1)
        q, da, k, v = q_low[rows, :], da_ref[rows, :], k_low[keys, :], v_ref[keys, :]
        qs = [jnp.where(first, q, zero), jnp.where(first, zero, q)]
        das = [jnp.where(first, da, zero), jnp.where(first, zero, da)]
        atts, probs, dss = [], [], []
        for h in range(2):
            s = dot_t(qs[h], k) * SCALE + bias
            top = jnp.max(s, axis=1, keepdims=True)
            w = jnp.exp(s - top)
            p = w * (1.0 / jnp.sum(w, axis=1, keepdims=True))
            p_low = p.astype(jnp.bfloat16)
            atts.append(dot(p_low, v))
            dp = dot_t(das[h], v)
            inner = jnp.sum(p * dp, axis=1, keepdims=True)
            dss.append((p * (dp - inner)).astype(jnp.bfloat16))
            probs.append(p_low)
        att_ref[rows, :] = jnp.where(first, atts[0], atts[1]).astype(jnp.bfloat16)
        dq = jnp.where(first, dot(dss[0], k), dot(dss[1], k)) * SCALE
        dq_ref[rows, :] = turned(dq, table_of(b), -1).astype(jnp.bfloat16)
        dk_sum[keys, :] += cross(jnp.concatenate(dss, axis=0), jnp.concatenate(qs, axis=0))
        dv_sum[keys, :] += cross(jnp.concatenate(probs, axis=0), jnp.concatenate(das, axis=0))
    for b in range(4):
        rows = pl.ds(b * BLOCK, BLOCK)
        dk_ref[rows, :] = turned(dk_sum[rows, :] * SCALE, table_of(b), -1).astype(jnp.bfloat16)
        dv_ref[rows, :] = dv_sum[rows, :].astype(jnp.bfloat16)


def attention(seq, rank, limit, queries, keys, values, d_attended):
    table = rotary_constants()
    whole = pl.BlockSpec((GROUP, PAIR), lambda g, p: (0, 0))
    part = pl.BlockSpec((GROUP, PAIR), lambda g, p: (g, p))
    smem = pl.BlockSpec(memory_space=pltpu.SMEM)
    rows = queries.shape[0]
    out = jax.ShapeDtypeStruct((rows, 2 * PAIR), jnp.bfloat16)
    return pl.pallas_call(
        attention_kernel,
        grid=(rows // GROUP, 2),
        in_specs=[smem, smem, smem, part, part, part, part, whole, whole, whole],
        out_specs=[part] * 4,
        out_shape=[out] * 4,
        scratch_shapes=[
            pltpu.VMEM((GROUP, PAIR), jnp.bfloat16),
            pltpu.VMEM((GROUP, PAIR), jnp.bfloat16),
            pltpu.VMEM((GROUP, PAIR), jnp.float32),
            pltpu.VMEM((GROUP, PAIR), jnp.float32),
        ],
        compiler_params=pltpu.CompilerParams(vmem_limit_bytes=32 * 2**20),
        cost_estimate=pl.CostEstimate(
            flops=2_000_000_000, bytes_accessed=6 * 2**20, transcendentals=2_000_000
        ),
        name="attention",
    )(seq, rank, limit, queries, keys, values, d_attended, *(jnp.asarray(a) for a in table))


def adam_step(weight, moment, second, gradient, step_rate, step_decay):
    moment_new = BETA_ONE * moment + (1 - BETA_ONE) * gradient
    second_new = BETA_TWO * second + (1 - BETA_TWO) * gradient * gradient
    moment_hat = moment_new / (1 - BETA_ONE**STEP)
    second_hat = second_new / (1 - BETA_TWO**STEP)
    updated = weight - step_rate * (
        moment_hat / (jnp.sqrt(second_hat) + ADAM_EPS) + step_decay * weight
    )
    return (second_new, updated)


def columns_out(value, chunks):
    rows = value.shape[0]
    parts = value.reshape(rows, chunks, TPN, PAIR).transpose(2, 0, 1, 3)
    parts = parts.reshape(TPN, rows, chunks * PAIR)
    return lax.all_to_all(parts, TP, split_axis=0, concat_axis=0, tiled=True).reshape(
        TPN * rows, chunks * PAIR
    )


def columns_back(value, chunks):
    rows = value.shape[0] // TPN
    parts = value.reshape(TPN, rows, chunks * PAIR)
    parts = lax.all_to_all(parts, TP, split_axis=0, concat_axis=0, tiled=True)
    parts = parts.reshape(TPN, rows, chunks, PAIR).transpose(1, 2, 0, 3)
    return parts.reshape(rows, chunks * TPN * PAIR)


def own_columns(vector, chunks, t):
    parts = vector.reshape(chunks, TPN, PAIR)
    return lax.dynamic_index_in_dim(parts, t, axis=1, keepdims=False).reshape(chunks * PAIR)


def spread_columns(vector, chunks, t):
    parts = jnp.zeros((chunks, TPN, PAIR), jnp.float32)
    parts = lax.dynamic_update_index_in_dim(parts, vector.reshape(chunks, PAIR), t, axis=1)
    return parts.reshape(-1)


def gathered(value, axes):
    return lax.all_gather(value, axes, axis=0, tiled=True)


def summed(value, axes):
    return lax.psum_scatter(value, axes, scatter_dimension=0, tiled=True)


def shards(
    tokens, cotangent, block_seq, seq_lengths,
    qkv_weight, qkv_moment, qkv_second,
    dense_weight, dense_moment, dense_second,
    expand_weight, expand_moment, expand_second,
    shrink_weight, shrink_moment, shrink_second,
    vectors, vec_moment, vec_second,
):
    t = lax.axis_index("c") * 4 + lax.axis_index("x")
    low = jnp.bfloat16
    vec_all = gathered(vectors.astype(low), ALL).astype(jnp.float32)
    expand_cols = columns_out(expand_weight.astype(low), 8)
    qkv_cols = columns_out(qkv_weight.astype(low), 6)
    dense_rows = lax.ppermute(dense_weight.astype(low), ALL, dense_route())
    shrink_rows = lax.ppermute(shrink_weight.astype(low), ALL, shrink_route())
    w_expand = gathered(expand_cols, ZY)
    w_qkv = gathered(qkv_cols, ZY)
    w_dense = gathered(dense_rows, ZY)
    w_shrink = gathered(shrink_rows, ZY)

    norm_gain, norm_shift = vec_all[:MODEL], vec_all[MODEL : 2 * MODEL]
    bias_qkv = own_columns(vec_all[2 * MODEL : 5 * MODEL], 6, t)
    bias_dense = vec_all[5 * MODEL : 6 * MODEL]
    bias_expand = own_columns(vec_all[6 * MODEL : 6 * MODEL + FF], 8, t)
    bias_shrink = vec_all[6 * MODEL + FF :]

    block_rows = gathered(block_seq, "c")
    length_rows = gathered(seq_lengths, "c")
    ranks = block_ranks(block_rows)
    limits = jnp.where(block_rows == 0, length_rows[:, :1], length_rows[:, 1:])

    c, x = lax.axis_index("c"), lax.axis_index("x")
    my_rank = lax.dynamic_index_in_dim(ranks[c], x, keepdims=False)
    my_limit = lax.dynamic_index_in_dim(limits[c], x, keepdims=False)
    live = my_rank * BLOCK + jnp.arange(BLOCK, dtype=jnp.int32) < my_limit

    inputs = tokens.astype(jnp.float32)
    mean = jnp.mean(inputs, axis=1, keepdims=True)
    center = inputs - mean
    inverse = lax.rsqrt(jnp.mean(center * center, axis=1, keepdims=True) + NORM_EPS)
    xhat = center * inverse
    normed_own = (xhat * norm_gain + norm_shift).astype(low)
    d_out_own = jnp.where(live[:, None], cotangent, jnp.zeros_like(cotangent))
    normed = gathered(normed_own, TP)
    d_out = gathered(d_out_own, TP)

    pre = dot(normed, w_expand) + bias_expand
    inner = jnp.tanh(GELU_A * (pre + GELU_B * (pre * pre * pre)))
    act = (0.5 * pre * (1.0 + inner)).astype(low)
    slope = 0.5 * (1.0 + inner) + 0.5 * pre * (1.0 - inner * inner) * (
        GELU_A * (1.0 + 3.0 * GELU_B * (pre * pre))
    )
    shrink_sum = summed(cross(act, d_out).astype(low), ZY)

    projected = dot(normed, w_qkv) + bias_qkv
    d_attended = dot_t(d_out, w_dense).astype(low)
    attended, d_q, d_k, d_v = attention(
        block_rows, ranks, limits,
        projected[:, : 2 * PAIR],
        projected[:, 2 * PAIR : 4 * PAIR],
        projected[:, 4 * PAIR :].astype(low),
        d_attended,
    )
    dense_sum = summed(cross(attended, d_out).astype(low), ZY)
    d_qkv = jnp.concatenate([d_q, d_k, d_v], axis=1)
    qkv_sum = summed(cross(normed, d_qkv).astype(low), ZY)
    d_pre = (dot_t(d_out, w_shrink) * slope).astype(low)
    expand_sum = summed(cross(normed, d_pre).astype(low), ZY)

    branches = summed((dot(attended, w_dense) + dot(act, w_shrink)).astype(low), TP)
    output = (inputs + (branches.astype(jnp.float32) + (bias_dense + bias_shrink))).astype(low)

    d_normed = summed((dot_t(d_qkv, w_qkv) + dot_t(d_pre, w_expand)).astype(low), TP)
    d_normed = d_normed.astype(jnp.float32)
    e = d_normed * norm_gain
    d_inputs = inverse * (
        e
        - jnp.mean(e, axis=1, keepdims=True)
        - xhat * jnp.mean(e * xhat, axis=1, keepdims=True)
    )
    input_grad = (d_out_own.astype(jnp.float32) + d_inputs).astype(low)

    d_out_sum = jnp.sum(d_out_own, axis=0, dtype=jnp.float32)
    vec_terms = jnp.concatenate(
        [
            jnp.sum(d_normed * xhat, axis=0),
            jnp.sum(d_normed, axis=0),
            spread_columns(jnp.sum(d_qkv, axis=0, dtype=jnp.float32), 6, t),
            d_out_sum,
            spread_columns(jnp.sum(d_pre, axis=0, dtype=jnp.float32), 8, t),
            d_out_sum,
        ]
    )
    vec_grad = summed(vec_terms, ALL)

    shrink_grad = lax.ppermute(shrink_sum, ALL, back(shrink_route())).astype(jnp.float32)
    dense_grad = lax.ppermute(dense_sum, ALL, back(dense_route())).astype(jnp.float32)
    qkv_grad = columns_back(qkv_sum, 6).astype(jnp.float32)
    expand_grad = columns_back(expand_sum, 8).astype(jnp.float32)

    masters = (qkv_weight, dense_weight, expand_weight, shrink_weight, vectors)
    moments = (qkv_moment, dense_moment, expand_moment, shrink_moment, vec_moment)
    seconds = (qkv_second, dense_second, expand_second, shrink_second, vec_second)
    gradients = (qkv_grad, dense_grad, expand_grad, shrink_grad, vec_grad)
    results = [output, input_grad]
    for i in range(5):
        state_new, weight_new = adam_step(
            masters[i], moments[i], seconds[i], gradients[i], RATES[i], DECAYS[i]
        )
        results.extend([gradients[i], state_new, weight_new])
    return tuple(results)


def solution(mesh):
    finer = Mesh(mesh.devices.reshape(*SIZES), ALL)
    whole, group = P(ALL, None), P(DP, None)
    return jax.shard_map(
        shards,
        mesh=finer,
        in_specs=(whole, whole, group, group, *[whole] * 12, *[P(ALL)] * 3),
        out_specs=(*[whole] * 14, *[P(ALL)] * 3),
        check_vma=False,
    )
```

```python
import functools

import jax
import jax.numpy as jnp
import numpy as np
from jax import lax
from jax.experimental import pallas as pl
from jax.experimental.pallas import tpu as pltpu
from jax.sharding import Mesh
from jax.sharding import PartitionSpec as P

HEAD = 64
ROT = 32
BLOCK = 128
STEP = 10
GROUP = 512
MODEL = 2048
FF = 8192
PAIR = 2 * HEAD
ALL = ("z", "y", "c", "x")
DP = ("z", "y", "c")
ZY = ("z", "y")
TP = ("c", "x")
SIZES = (4, 4, 2, 4)
TPN = 8
COPIES = 128
SCALE = HEAD ** (-0.5)

NORM_EPS = 1e-05
MASKED = -1e30
BETA_ONE = 0.9
BETA_TWO = 0.999
ADAM_EPS = 1e-08
RATES = (0.02, 0.1, 0.02, 0.01, 0.4)
DECAYS = (0.1, 0.1, 0.1, 0.1, 0.0)
GELU_A = float(np.sqrt(2.0 / np.pi))
GELU_B = 0.044715


def dot(a, b):
    return jnp.dot(a, b, preferred_element_type=jnp.float32)


def dot_t(a, b):
    return lax.dot_general(a, b, (((1,), (1,)), ((), ())), preferred_element_type=jnp.float32)


def cross(a, b):
    return lax.dot_general(a, b, (((0,), (0,)), ((), ())), preferred_element_type=jnp.float32)


def rotary_constants():
    half = np.arange(ROT // 2, dtype=np.float32)
    inverse = (10000.0 ** (-2.0 * half.astype(np.float64) / ROT)).astype(np.float32)
    angle = (np.arange(GROUP, dtype=np.float32)[:, None] * inverse[None, :]).astype(np.float64)
    cosine, sine = np.cos(angle).astype(np.float32), np.sin(angle).astype(np.float32)
    one = np.ones((GROUP, HEAD - ROT), np.float32)
    zero = np.zeros((GROUP, ROT // 2), np.float32)
    rest = np.zeros((GROUP, HEAD - ROT), np.float32)
    turn = np.concatenate([cosine, cosine, one], axis=1)
    ahead = np.concatenate([-sine, zero, rest], axis=1)
    behind = np.concatenate([zero, sine, rest], axis=1)
    return tuple(np.concatenate([a, a], axis=1) for a in (turn, ahead, behind))


MESH = pl.DeviceIdType.MESH


def other(axis, step):
    size = SIZES[ALL.index(axis)]
    return lax.rem(lax.axis_index(axis) + step + size, size)


class Copies:
    def __init__(self, send, recv):
        self.send, self.recv, self.count, self.open = send, recv, 0, []

    def start(self, src, dst, to):
        at = self.count
        self.count += 1
        copy = pltpu.make_async_remote_copy(
            src_ref=src,
            dst_ref=dst,
            send_sem=self.send.at[at],
            recv_sem=self.recv.at[at],
            device_id=to,
            device_id_type=MESH,
        )
        copy.start()
        self.open.append(copy)
        return copy

    def finish(self):
        for copy in self.open:
            copy.wait_send()
        self.open = []


def enter():
    barrier = pltpu.get_barrier_semaphore()
    for partner in token_partners() + weight_partners() + [dense_partner()]:
        pl.semaphore_signal(barrier, inc=1, device_id=partner, device_id_type=MESH)
    pl.semaphore_wait(barrier, 23)


def token_partners():
    return [{"c": other("c", i), "x": other("x", j)} for i in range(2) for j in range(4) if i + j]


def weight_partners():
    return [{"z": other("z", i), "y": other("y", j)} for i in range(4) for j in range(4) if i + j]


def dense_partner():
    z, y, c, x = (lax.axis_index(a) for a in ALL)
    return {"z": (1 - z // 2) * 2 + c, "y": x, "c": lax.rem(z, 2), "x": y}


def gather_weights(copies, view):
    z, y = lax.axis_index("z"), lax.axis_index("y")
    up, down = {"y": other("y", 1)}, {"y": other("y", -1)}
    far, near = {"z": other("z", 1)}, {"z": other("z", -1)}
    every = slice(None)

    def go(block, to):
        return copies.start(block, block, to)

    a_up, a_down = go(view(z, y, 4), up), go(view(z, y, 4), down)
    b_far, b_near = go(view(z, y, 5), far), go(view(z, y, 5), near)
    yield
    a_up.wait_recv()
    a_up = go(view(z, other("y", -1), 0), up)
    b_far.wait_recv()
    b_far = go(view(other("z", -1), y, 2), far)
    a_down.wait_recv()
    a_down = go(view(z, other("y", 1), 1), down)
    b_near.wait_recv()
    b_near = go(view(other("z", 1), y, 3), near)
    yield
    a_up.wait_recv()
    a_down.wait_recv()
    a_far, a_near = go(view(z, every, 4), far), go(view(z, every, 4), near)
    b_far.wait_recv()
    b_near.wait_recv()
    b_up, b_down = go(view(every, y, 5), up), go(view(every, y, 5), down)
    yield
    a_far.wait_recv()
    a_far = go(view(other("z", -1), every, 0), far)
    b_up.wait_recv()
    b_up = go(view(every, other("y", -1), 2), up)
    a_near.wait_recv()
    a_near = go(view(other("z", 1), every, 1), near)
    b_down.wait_recv()
    b_down = go(view(every, other("y", 1), 3), down)
    yield
    for copy in (a_far, a_near, b_up, b_down):
        copy.wait_recv()


def gather_tokens(copies, ref):
    c, x, across = lax.axis_index("c"), lax.axis_index("x"), other("c", 1)

    def go(block, to):
        return copies.start(block, block, to)

    own = ref.at[c, x]
    right, left, core = go(own, {"x": other("x", 1)}), go(own, {"x": other("x", -1)}), [go(own, {"c": across})]
    yield
    right.wait_recv()
    came = ref.at[c, other("x", -1)]
    right = go(ref.at[c, other("x", -1), pl.ds(0, 64)], {"x": other("x", 1)})
    core.append(go(came, {"c": across}))
    left.wait_recv()
    came = ref.at[c, other("x", 1)]
    left = go(ref.at[c, other("x", 1), pl.ds(64, 64)], {"x": other("x", -1)})
    core.append(go(came, {"c": across}))
    yield
    right.wait_recv()
    left.wait_recv()
    core.append(go(ref.at[c, other("x", 2)], {"c": across}))
    yield
    for copy in core:
        copy.wait_recv()


def gather_vectors(copies, ref):
    z, y, c, x = (lax.axis_index(a) for a in ALL)
    sent = [copies.start(ref.at[z, y, c, x], ref.at[z, y, c, x], to) for to in token_partners()]
    yield
    for copy in sent:
        copy.wait_recv()
    sent = [copies.start(ref.at[z, y], ref.at[z, y], to) for to in weight_partners()]
    yield
    for copy in sent:
        copy.wait_recv()


def expand_to_group(copies, send, ref, width):
    z, y, c, x = (lax.axis_index(a) for a in ALL)
    rows = pl.ds(pl.multiple_of((c * 4 + x) * 16, 16), 16)
    sent = []
    for to in token_partners():
        sent.append(copies.start(send.at[to["c"] * 4 + to["x"]], ref.at[z, y, rows], to))
    ref[z, y, rows] = send[c * 4 + x]
    yield
    for copy in sent:
        copy.wait_recv()


def by_rows(ref, rows):
    quarter = rows // 4

    def view(z, y, part):
        start, size = (part * quarter, quarter) if part < 4 else ((part - 4) * 2 * quarter, 2 * quarter)
        return ref.at[z, y, pl.ds(start, size)]

    return view


def by_columns(ref, columns):
    quarter = columns // 4

    def view(z, y, part):
        start, size = (part * quarter, quarter) if part < 4 else ((part - 4) * 2 * quarter, 2 * quarter)
        return ref.at[z, y, :, pl.ds(start, size)]

    return view


def step(*works):
    for work in works:
        next(work, None)


def row_of(ref, first, count):
    return jnp.concatenate([ref[pl.ds(first + i, 1), :] for i in range(count)], axis=1)


def gather_kernel(
    tokens_ref, d_out_ref, we_send, wq_send, wd_own, ws_own, vec_own,
    we, wq, wd, ws, normed, d_out, vec_rows, vec_all, send, recv,
):
    z, y, c, x = (lax.axis_index(a) for a in ALL)
    copies = Copies(send, recv)
    ws[z, y] = ws_own[...]
    vec_all[z, y, c, x] = vec_own[...]
    d_out[c, x] = d_out_ref[...]
    enter()
    vectors = gather_vectors(copies, vec_all)
    step(vectors)
    shrink = gather_weights(copies, by_rows(ws, 64))
    step(shrink)
    into_expand = expand_to_group(copies, we_send, we, 1024)
    step(into_expand)
    dense_here = copies.start(wd_own, wd.at[dense_partner()["z"], dense_partner()["y"]], dense_partner())
    into_qkv = expand_to_group(copies, wq_send, wq, 768)
    step(into_qkv)
    cotangent = gather_tokens(copies, d_out)
    step(cotangent)
    step(vectors)
    step(into_expand)
    expand = gather_weights(copies, by_rows(we, 128))
    step(expand)
    step(vectors)
    vec_rows[...] = jnp.zeros_like(vec_rows)
    for d in range(128):
        first = (176 * d) // 128
        vec_rows[pl.ds(first, 3), :] += vec_all[d // 32, (d // 8) % 4, (d // 4) % 2, d % 4, pl.ds(0, 3), :]
    values = tokens_ref[...].astype(jnp.float32)
    center = values - jnp.mean(values, axis=1, keepdims=True)
    inverse = lax.rsqrt(jnp.mean(center * center, axis=1, keepdims=True) + NORM_EPS)
    own = center * inverse * row_of(vec_rows, 0, 16) + row_of(vec_rows, 16, 16)
    normed[c, x] = own.astype(jnp.bfloat16)
    forward = gather_tokens(copies, normed)
    step(forward)
    dense_here.wait_recv()
    dense = gather_weights(copies, by_columns(wd, 2048))
    step(dense)
    step(into_qkv)
    qkv = gather_weights(copies, by_rows(wq, 128))
    step(qkv)
    for _ in range(4):
        step(shrink, expand, cotangent, forward, dense, qkv)
    copies.finish()


def gather_all(tokens, d_out, we_send, wq_send, wd_own, ws_own, vec_own):
    low = jnp.bfloat16
    vmem = pl.BlockSpec(memory_space=pltpu.VMEM)
    shapes = [
        ((4, 4, 128, 1024), low), ((4, 4, 128, 768), low), ((4, 4, 16, 2048), low),
        ((4, 4, 64, 2048), low), ((2, 4, 128, 2048), low), ((2, 4, 128, 2048), low),
        ((184, 128), jnp.float32),
    ]
    return pl.pallas_call(
        gather_kernel,
        in_specs=[vmem] * 7,
        out_specs=[vmem] * 7,
        out_shape=[jax.ShapeDtypeStruct(s, t) for s, t in shapes],
        scratch_shapes=[
            pltpu.VMEM((4, 4, 2, 4, 8, 128), jnp.float32),
            pltpu.SemaphoreType.DMA((COPIES,)),
            pltpu.SemaphoreType.DMA((COPIES,)),
        ],
        compiler_params=pltpu.CompilerParams(
            collective_id=0, has_side_effects=True, vmem_limit_bytes=48 * 2**20
        ),
        name="gather_all",
    )(tokens, d_out, we_send, wq_send, wd_own, ws_own, vec_own)


def block_ranks(block_rows):
    same = block_rows[:, :, None] == block_rows[:, None, :]
    earlier = jnp.arange(4)[None, :] < jnp.arange(4)[:, None]
    return jnp.sum(jnp.where(same & earlier[None], 1, 0), axis=2).astype(jnp.int32)


def turned(values, table, sign):
    turn, ahead, behind = table
    shape_axis = values.ndim - 1
    up = pltpu.roll(values, PAIR - ROT // 2, shape_axis)
    down = pltpu.roll(values, ROT // 2, shape_axis)
    if sign > 0:
        return values * turn + up * ahead + down * behind
    return values * turn - up * ahead - down * behind


def attention_kernel(
    seq_ref, rank_ref, limit_ref, q_ref, k_ref, v_ref, da_ref, turn_ref, ahead_ref, behind_ref,
    att_ref, dq_ref, dk_ref, dv_ref, q_low, k_low, dk_sum, dv_sum
):
    g = pl.program_id(0)
    lane = lax.broadcasted_iota(jnp.int32, (BLOCK, PAIR), 1)
    first = lane < HEAD

    def table_of(b):
        rows = pl.ds(pl.multiple_of(rank_ref[g, b] * BLOCK, BLOCK), BLOCK)
        return turn_ref[rows, :], ahead_ref[rows, :], behind_ref[rows, :]

    for b in range(4):
        rows = pl.ds(b * BLOCK, BLOCK)
        table = table_of(b)
        q_low[rows, :] = turned(q_ref[rows, :], table, 1).astype(jnp.bfloat16)
        k_low[rows, :] = turned(k_ref[rows, :], table, 1).astype(jnp.bfloat16)
    dk_sum[...] = jnp.zeros_like(dk_sum)
    dv_sum[...] = jnp.zeros_like(dv_sum)
    zero = jnp.zeros((BLOCK, PAIR), jnp.bfloat16)
    row_at = lax.broadcasted_iota(jnp.int32, (BLOCK, BLOCK), 0)
    col_at = lax.broadcasted_iota(jnp.int32, (BLOCK, BLOCK), 1)
    for b in range(4):
        rows = pl.ds(b * BLOCK, BLOCK)
        keys = pl.ds(0, (b + 1) * BLOCK)
        width = (b + 1) * BLOCK
        base = rank_ref[g, b] * BLOCK
        diagonal = (col_at <= row_at) & (col_at + base < limit_ref[g, b])
        bias_parts = []
        for e in range(b):
            away = jnp.where(seq_ref[g, e] == seq_ref[g, b], 0.0, MASKED).astype(jnp.float32)
            bias_parts.append(jnp.zeros((BLOCK, BLOCK), jnp.float32) + away)
        bias_parts.append(jnp.where(diagonal, 0.0, MASKED).astype(jnp.float32))
        bias = bias_parts[0] if b == 0 else jnp.concatenate(bias_parts, axis=1)
        q, da, k, v = q_low[rows, :], da_ref[rows, :], k_low[keys, :], v_ref[keys, :]
        qs = [jnp.where(first, q, zero), jnp.where(first, zero, q)]
        das = [jnp.where(first, da, zero), jnp.where(first, zero, da)]
        atts, probs, dss = [], [], []
        for h in range(2):
            s = dot_t(qs[h], k) * SCALE + bias
            top = jnp.max(s, axis=1, keepdims=True)
            w = jnp.exp(s - top)
            p = w * (1.0 / jnp.sum(w, axis=1, keepdims=True))
            p_low = p.astype(jnp.bfloat16)
            atts.append(dot(p_low, v))
            dp = dot_t(das[h], v)
            inner = jnp.sum(p * dp, axis=1, keepdims=True)
            dss.append((p * (dp - inner)).astype(jnp.bfloat16))
            probs.append(p_low)
        att_ref[rows, :] = jnp.where(first, atts[0], atts[1]).astype(jnp.bfloat16)
        dq = jnp.where(first, dot(dss[0], k), dot(dss[1], k)) * SCALE
        dq_ref[rows, :] = turned(dq, table_of(b), -1).astype(jnp.bfloat16)
        dk_sum[keys, :] += cross(jnp.concatenate(dss, axis=0), jnp.concatenate(qs, axis=0))
        dv_sum[keys, :] += cross(jnp.concatenate(probs, axis=0), jnp.concatenate(das, axis=0))
    for b in range(4):
        rows = pl.ds(b * BLOCK, BLOCK)
        dk_ref[rows, :] = turned(dk_sum[rows, :] * SCALE, table_of(b), -1).astype(jnp.bfloat16)
        dv_ref[rows, :] = dv_sum[rows, :].astype(jnp.bfloat16)


def attention(seq, rank, limit, queries, keys, values, d_attended):
    table = rotary_constants()
    whole = pl.BlockSpec((GROUP, PAIR), lambda g, p: (0, 0))
    part = pl.BlockSpec((GROUP, PAIR), lambda g, p: (g, p))
    smem = pl.BlockSpec(memory_space=pltpu.SMEM)
    rows = queries.shape[0]
    out = jax.ShapeDtypeStruct((rows, 2 * PAIR), jnp.bfloat16)
    return pl.pallas_call(
        attention_kernel,
        grid=(rows // GROUP, 2),
        in_specs=[smem, smem, smem, part, part, part, part, whole, whole, whole],
        out_specs=[part] * 4,
        out_shape=[out] * 4,
        scratch_shapes=[
            pltpu.VMEM((GROUP, PAIR), jnp.bfloat16),
            pltpu.VMEM((GROUP, PAIR), jnp.bfloat16),
            pltpu.VMEM((GROUP, PAIR), jnp.float32),
            pltpu.VMEM((GROUP, PAIR), jnp.float32),
        ],
        compiler_params=pltpu.CompilerParams(vmem_limit_bytes=32 * 2**20),
        cost_estimate=pl.CostEstimate(
            flops=2_000_000_000, bytes_accessed=6 * 2**20, transcendentals=2_000_000
        ),
        name="attention",
    )(seq, rank, limit, queries, keys, values, d_attended, *(jnp.asarray(a) for a in table))


def adam_step(weight, moment, second, gradient, step_rate, step_decay):
    moment_new = BETA_ONE * moment + (1 - BETA_ONE) * gradient
    second_new = BETA_TWO * second + (1 - BETA_TWO) * gradient * gradient
    moment_hat = moment_new / (1 - BETA_ONE**STEP)
    second_hat = second_new / (1 - BETA_TWO**STEP)
    updated = weight - step_rate * (
        moment_hat / (jnp.sqrt(second_hat) + ADAM_EPS) + step_decay * weight
    )
    return (second_new, updated)


def qkv_out(value):
    lead = value.shape[:-1]
    parts = value.reshape(*lead, 3, 2, TPN, PAIR)[..., ::-1, :, :]
    return jnp.moveaxis(parts, -2, 0).reshape(TPN, *lead, 6 * PAIR)


def qkv_back(parts):
    lead = parts.shape[1:-1]
    parts = jnp.moveaxis(parts.reshape(TPN, *lead, 3, 2, PAIR), 0, -2)[..., ::-1, :, :]
    return parts.reshape(*lead, 3 * MODEL)


def expand_out(value):
    lead = value.shape[:-1]
    parts = value.reshape(*lead, FF // 512, TPN, 64)
    return jnp.moveaxis(parts, -2, 0).reshape(TPN, *lead, FF // TPN)


def expand_back(parts):
    lead = parts.shape[1:-1]
    parts = jnp.moveaxis(parts.reshape(TPN, *lead, FF // 512, 64), 0, -2)
    return parts.reshape(*lead, FF)


def to_group(parts):
    return lax.all_to_all(parts, TP, split_axis=0, concat_axis=0, tiled=True)


def placed(value, t):
    return lax.dynamic_update_index_in_dim(
        jnp.zeros((TPN, value.shape[0]), jnp.float32), value, t, axis=0
    )


def dense_route():
    pairs = []
    for z, y, c, x in np.ndindex(*SIZES):
        target = (((1 - z // 2) * 2 + c) * 4 + x) * 8 + (z % 2) * 4 + y
        pairs.append((((z * 4 + y) * 2 + c) * 4 + x, target))
    return pairs


def gathered(value, axes):
    return lax.all_gather(value, axes, axis=0, tiled=True)


def summed(value, axes):
    return lax.psum_scatter(value, axes, scatter_dimension=0, tiled=True)


def shards(
    tokens, cotangent, block_seq, seq_lengths,
    qkv_weight, qkv_moment, qkv_second,
    dense_weight, dense_moment, dense_second,
    expand_weight, expand_moment, expand_second,
    shrink_weight, shrink_moment, shrink_second,
    vectors, vec_moment, vec_second,
):
    z, y, c, x = (lax.axis_index(a) for a in ALL)
    t = c * 4 + x
    low = jnp.bfloat16
    place = lax.rem(((z * 4 + y) * 8 + t) * 176, 128)
    vec_own = lax.dynamic_update_slice(
        jnp.zeros((1024,), jnp.float32), vectors.astype(low).astype(jnp.float32), (place,)
    ).reshape(8, 128)
    block_rows = gathered(block_seq, "c")
    length_rows = gathered(seq_lengths, "c")
    ranks = block_ranks(block_rows)
    limits = jnp.where(block_rows == 0, length_rows[:, :1], length_rows[:, 1:])

    my_rank = lax.dynamic_index_in_dim(ranks[c], x, keepdims=False)
    my_limit = lax.dynamic_index_in_dim(limits[c], x, keepdims=False)
    live = my_rank * BLOCK + jnp.arange(BLOCK, dtype=jnp.int32) < my_limit

    d_out_own = jnp.where(live[:, None], cotangent, jnp.zeros_like(cotangent))
    w_expand, w_qkv, w_dense, w_shrink, normed, d_out, vec_rows = gather_all(
        tokens,
        d_out_own,
        expand_out(expand_weight.astype(low)),
        qkv_out(qkv_weight.astype(low)),
        dense_weight.astype(low),
        shrink_weight.astype(low),
        vec_own,
    )
    w_expand, w_qkv = w_expand.reshape(MODEL, -1), w_qkv.reshape(MODEL, -1)
    w_dense, w_shrink = w_dense.reshape(-1, MODEL), w_shrink.reshape(-1, MODEL)
    normed, d_out = normed.reshape(-1, MODEL), d_out.reshape(-1, MODEL)
    vec_all = vec_rows[:176].reshape(-1)
    norm_gain = vec_all[:MODEL]
    bias_qkv = qkv_out(vec_all[2 * MODEL : 5 * MODEL])[t]
    bias_dense = vec_all[5 * MODEL : 6 * MODEL]
    bias_expand = expand_out(vec_all[6 * MODEL : 6 * MODEL + FF])[t]
    bias_shrink = vec_all[6 * MODEL + FF :]

    inputs = tokens.astype(jnp.float32)
    mean = jnp.mean(inputs, axis=1, keepdims=True)
    center = inputs - mean
    inverse = lax.rsqrt(jnp.mean(center * center, axis=1, keepdims=True) + NORM_EPS)
    xhat = center * inverse

    pre = dot(normed, w_expand) + bias_expand
    inner = jnp.tanh(GELU_A * (pre + GELU_B * (pre * pre * pre)))
    act = (0.5 * pre * (1.0 + inner)).astype(low)
    slope = 0.5 * (1.0 + inner) + 0.5 * pre * (1.0 - inner * inner) * (
        GELU_A * (1.0 + 3.0 * GELU_B * (pre * pre))
    )
    shrink_sum = summed(cross(act, d_out).astype(low), ZY)

    projected = dot(normed, w_qkv) + bias_qkv
    d_attended = dot_t(d_out, w_dense).astype(low)
    attended, d_q, d_k, d_v = attention(
        block_rows, ranks, limits,
        projected[:, : 2 * PAIR],
        projected[:, 2 * PAIR : 4 * PAIR],
        projected[:, 4 * PAIR :].astype(low),
        d_attended,
    )
    dense_sum = summed(cross(attended, d_out).astype(low), ZY)
    d_qkv = jnp.concatenate([d_q, d_k, d_v], axis=1)
    qkv_sum = summed(cross(normed, d_qkv).astype(low), ZY)
    d_pre = (dot_t(d_out, w_shrink) * slope).astype(low)
    expand_sum = summed(cross(normed, d_pre).astype(low), ZY)

    branches = summed((dot(attended, w_dense) + dot(act, w_shrink)).astype(low), TP)
    output = (inputs + (branches.astype(jnp.float32) + (bias_dense + bias_shrink))).astype(low)

    d_normed = summed((dot_t(d_qkv, w_qkv) + dot_t(d_pre, w_expand)).astype(low), TP)
    d_normed = d_normed.astype(jnp.float32)
    e = d_normed * norm_gain
    d_inputs = inverse * (
        e
        - jnp.mean(e, axis=1, keepdims=True)
        - xhat * jnp.mean(e * xhat, axis=1, keepdims=True)
    )
    input_grad = (d_out_own.astype(jnp.float32) + d_inputs).astype(low)

    d_out_sum = jnp.sum(d_out_own, axis=0, dtype=jnp.float32)
    vec_terms = jnp.concatenate(
        [
            jnp.sum(d_normed * xhat, axis=0),
            jnp.sum(d_normed, axis=0),
            qkv_back(placed(jnp.sum(d_qkv, axis=0, dtype=jnp.float32), t)),
            d_out_sum,
            expand_back(placed(jnp.sum(d_pre, axis=0, dtype=jnp.float32), t)),
            d_out_sum,
        ]
    )
    vec_grad = summed(vec_terms, ALL)

    shrink_grad = shrink_sum.astype(jnp.float32)
    dense_grad = lax.ppermute(dense_sum, ALL, dense_route()).astype(jnp.float32)
    qkv_grad = qkv_back(to_group(qkv_sum.reshape(TPN, 16, -1))).astype(jnp.float32)
    expand_grad = expand_back(to_group(expand_sum.reshape(TPN, 16, -1))).astype(jnp.float32)

    masters = (qkv_weight, dense_weight, expand_weight, shrink_weight, vectors)
    moments = (qkv_moment, dense_moment, expand_moment, shrink_moment, vec_moment)
    seconds = (qkv_second, dense_second, expand_second, shrink_second, vec_second)
    gradients = (qkv_grad, dense_grad, expand_grad, shrink_grad, vec_grad)
    results = [output, input_grad]
    for i in range(5):
        state_new, weight_new = adam_step(
            masters[i], moments[i], seconds[i], gradients[i], RATES[i], DECAYS[i]
        )
        results.extend([gradients[i], state_new, weight_new])
    return tuple(results)


def solution(mesh):
    finer = Mesh(mesh.devices.reshape(*SIZES), ALL)
    whole, group = P(ALL, None), P(DP, None)
    return jax.shard_map(
        shards,
        mesh=finer,
        in_specs=(whole, whole, group, group, *[whole] * 12, *[P(ALL)] * 3),
        out_specs=(*[whole] * 14, *[P(ALL)] * 3),
        check_vma=False,
    )
```

```python
import functools

import jax
import jax.numpy as jnp
import numpy as np
from jax import lax
from jax.experimental import pallas as pl
from jax.experimental.pallas import tpu as pltpu
from jax.sharding import Mesh
from jax.sharding import PartitionSpec as P

HEAD = 64
ROT = 32
BLOCK = 128
STEP = 10
GROUP = 512
MODEL = 2048
FF = 8192
PAIR = 2 * HEAD
ALL = ("z", "y", "c", "x")
DP = ("z", "y", "c")
ZY = ("z", "y")
TP = ("c", "x")
SIZES = (4, 4, 2, 4)
TPN = 8
COPIES = 320
SCALE = HEAD ** (-0.5)

NORM_EPS = 1e-05
MASKED = -1e30
BETA_ONE = 0.9
BETA_TWO = 0.999
ADAM_EPS = 1e-08
RATES = (0.02, 0.1, 0.02, 0.01, 0.4)
DECAYS = (0.1, 0.1, 0.1, 0.1, 0.0)
GELU_A = float(np.sqrt(2.0 / np.pi))
GELU_B = 0.044715


def dot(a, b):
    return jnp.dot(a, b, preferred_element_type=jnp.float32)


def dot_t(a, b):
    return lax.dot_general(a, b, (((1,), (1,)), ((), ())), preferred_element_type=jnp.float32)


def cross(a, b):
    return lax.dot_general(a, b, (((0,), (0,)), ((), ())), preferred_element_type=jnp.float32)


def rotary_constants():
    half = np.arange(ROT // 2, dtype=np.float32)
    inverse = (10000.0 ** (-2.0 * half.astype(np.float64) / ROT)).astype(np.float32)
    angle = (np.arange(GROUP, dtype=np.float32)[:, None] * inverse[None, :]).astype(np.float64)
    cosine, sine = np.cos(angle).astype(np.float32), np.sin(angle).astype(np.float32)
    one = np.ones((GROUP, HEAD - ROT), np.float32)
    zero = np.zeros((GROUP, ROT // 2), np.float32)
    rest = np.zeros((GROUP, HEAD - ROT), np.float32)
    turn = np.concatenate([cosine, cosine, one], axis=1)
    ahead = np.concatenate([-sine, zero, rest], axis=1)
    behind = np.concatenate([zero, sine, rest], axis=1)
    return tuple(np.concatenate([a, a], axis=1) for a in (turn, ahead, behind))


MESH = pl.DeviceIdType.MESH


def other(axis, step):
    size = SIZES[ALL.index(axis)]
    return lax.rem(lax.axis_index(axis) + step + size, size)


class Copies:
    def __init__(self, send, recv):
        self.send, self.recv, self.count, self.open = send, recv, 0, []

    def start(self, src, dst, to):
        at = self.count
        self.count += 1
        copy = pltpu.make_async_remote_copy(
            src_ref=src,
            dst_ref=dst,
            send_sem=self.send.at[at],
            recv_sem=self.recv.at[at],
            device_id=to,
            device_id_type=MESH,
        )
        copy.start()
        self.open.append(copy)
        return copy

    def sent(self, *copies):
        for copy in copies:
            copy.wait_send()
            self.open = [each for each in self.open if each is not copy]

    def finish(self):
        self.sent(*list(self.open))


def enter():
    barrier = pltpu.get_barrier_semaphore()
    for partner in token_partners() + weight_partners() + [dense_partner()]:
        pl.semaphore_signal(barrier, inc=1, device_id=partner, device_id_type=MESH)
    pl.semaphore_wait(barrier, 23)


def token_partners():
    return [{"c": other("c", i), "x": other("x", j)} for i in range(2) for j in range(4) if i + j]


def weight_partners():
    return [{"z": other("z", i), "y": other("y", j)} for i in range(4) for j in range(4) if i + j]


def dense_partner():
    z, y, c, x = (lax.axis_index(a) for a in ALL)
    return {"z": (1 - z // 2) * 2 + c, "y": x, "c": lax.rem(z, 2), "x": y}


def gather_weights(copies, view):
    z, y = lax.axis_index("z"), lax.axis_index("y")
    up, down = {"y": other("y", 1)}, {"y": other("y", -1)}
    far, near = {"z": other("z", 1)}, {"z": other("z", -1)}
    every = slice(None)

    def go(block, to):
        return copies.start(block, block, to)

    a_up, a_down = go(view(z, y, 4), up), go(view(z, y, 4), down)
    b_far, b_near = go(view(z, y, 5), far), go(view(z, y, 5), near)
    yield
    a_up.wait_recv()
    a_up = go(view(z, other("y", -1), 0), up)
    b_far.wait_recv()
    b_far = go(view(other("z", -1), y, 2), far)
    a_down.wait_recv()
    a_down = go(view(z, other("y", 1), 1), down)
    b_near.wait_recv()
    b_near = go(view(other("z", 1), y, 3), near)
    yield
    a_up.wait_recv()
    a_down.wait_recv()
    a_far, a_near = go(view(z, every, 4), far), go(view(z, every, 4), near)
    b_far.wait_recv()
    b_near.wait_recv()
    b_up, b_down = go(view(every, y, 5), up), go(view(every, y, 5), down)
    yield
    a_far.wait_recv()
    a_far = go(view(other("z", -1), every, 0), far)
    b_up.wait_recv()
    b_up = go(view(every, other("y", -1), 2), up)
    a_near.wait_recv()
    a_near = go(view(other("z", 1), every, 1), near)
    b_down.wait_recv()
    b_down = go(view(every, other("y", 1), 3), down)
    yield
    for copy in (a_far, a_near, b_up, b_down):
        copy.wait_recv()


def gather_tokens(copies, ref):
    c, x, across = lax.axis_index("c"), lax.axis_index("x"), other("c", 1)
    mine = []

    def go(block, to):
        mine.append(copies.start(block, block, to))
        return mine[-1]

    own = ref.at[c, x]
    right, left, core = go(own, {"x": other("x", 1)}), go(own, {"x": other("x", -1)}), [go(own, {"c": across})]
    yield
    right.wait_recv()
    came = ref.at[c, other("x", -1)]
    right = go(ref.at[c, other("x", -1), pl.ds(0, 64)], {"x": other("x", 1)})
    core.append(go(came, {"c": across}))
    left.wait_recv()
    came = ref.at[c, other("x", 1)]
    left = go(ref.at[c, other("x", 1), pl.ds(64, 64)], {"x": other("x", -1)})
    core.append(go(came, {"c": across}))
    yield
    right.wait_recv()
    left.wait_recv()
    core.append(go(ref.at[c, other("x", 2)], {"c": across}))
    yield
    for copy in core:
        copy.wait_recv()
    copies.sent(*mine)


def gather_vectors(copies, ref):
    z, y, c, x = (lax.axis_index(a) for a in ALL)
    sent = [copies.start(ref.at[z, y, c, x], ref.at[z, y, c, x], to) for to in token_partners()]
    yield
    for copy in sent:
        copy.wait_recv()
    sent = [copies.start(ref.at[z, y], ref.at[z, y], to) for to in weight_partners()]
    yield
    for copy in sent:
        copy.wait_recv()


def expand_to_group(copies, send, ref, width):
    z, y, c, x = (lax.axis_index(a) for a in ALL)
    rows = pl.ds(pl.multiple_of((c * 4 + x) * 16, 16), 16)
    sent = []
    for to in token_partners():
        sent.append(copies.start(send.at[to["c"] * 4 + to["x"]], ref.at[z, y, rows], to))
    ref[z, y, rows] = send[c * 4 + x]
    yield
    for copy in sent:
        copy.wait_recv()


def by_rows(ref, rows):
    quarter = rows // 4

    def view(z, y, part):
        start, size = (part * quarter, quarter) if part < 4 else ((part - 4) * 2 * quarter, 2 * quarter)
        return ref.at[z, y, pl.ds(start, size)]

    return view


def by_columns(ref, columns):
    quarter = columns // 4

    def view(z, y, part):
        start, size = (part * quarter, quarter) if part < 4 else ((part - 4) * 2 * quarter, 2 * quarter)
        return ref.at[z, y, :, pl.ds(start, size)]

    return view


def step(*works):
    for work in works:
        next(work, None)


def row_of(ref, first, count):
    return jnp.concatenate([ref[pl.ds(first + i, 1), :] for i in range(count)], axis=1)


def ring_sum(copies, axis, block, land, low_part, high_part):
    ahead, behind = other(axis, 1), other(axis, -1)
    up, down = {axis: ahead}, {axis: behind}
    far = other(axis, 2)
    t_low = copies.start(block(far, low_part), land.at[0], up)
    t_high = copies.start(block(far, high_part), land.at[1], down)
    d_high = copies.start(block(ahead, high_part), land.at[3], up)
    d_low = copies.start(block(behind, low_part), land.at[2], down)
    yield
    t_low.wait_recv()
    land[0] = land[0] + block(ahead, low_part)[...]
    p_low = copies.start(land.at[0], land.at[4], up)
    t_high.wait_recv()
    land[1] = land[1] + block(behind, high_part)[...]
    p_high = copies.start(land.at[1], land.at[5], down)
    yield
    for copy in (d_low, d_high, p_low, p_high):
        copy.wait_recv()
    copies.sent(t_low, t_high, d_low, d_high, p_low, p_high)


def three(own, land, high, at=...):
    f32 = jnp.float32
    first, second = land.at[4 + high], land.at[2 + high]
    return own[at].astype(f32) + first[at].astype(f32) + second[at].astype(f32)


def both(first, second):
    while True:
        done = [next(first, 0), next(second, 0)]
        if 0 in done:
            return
        yield


def scatter_weights(copies, view, wide, narrow, give):
    z, y = lax.axis_index("z"), lax.axis_index("y")
    every = slice(None)
    low = jnp.bfloat16
    yield from both(
        ring_sum(copies, "y", lambda i, p: view(every, i, p), wide.at[0], 0, 1),
        ring_sum(copies, "z", lambda i, p: view(i, every, p), wide.at[1], 2, 3),
    )
    for high in range(2):
        own = view(every, y, high)
        for i in range(4):
            own[i] = three(own, wide.at[0], high, i).astype(low)
        own = view(z, every, 2 + high)
        for i in range(4):
            own[i] = three(own, wide.at[1], high, i).astype(low)
    yield from both(
        ring_sum(copies, "z", lambda i, p: view(i, y, p), narrow.at[0], 0, 1),
        ring_sum(copies, "y", lambda i, p: view(z, i, p), narrow.at[1], 2, 3),
    )
    for high in range(2):
        give(high, three(view(z, y, high), narrow.at[0], high))
        give(2 + high, three(view(z, y, 2 + high), narrow.at[1], high))


def scatter_tokens(copies, ref, core_land, land, give, core_free, ring_free, first):
    c, x, across = lax.axis_index("c"), lax.axis_index("x"), other("c", 1)
    if not first:
        pl.semaphore_wait(core_free, 1)
    came = copies.start(ref.at[across], core_land, {"c": across})
    yield
    came.wait_recv()
    for i in range(4):
        ref[c, i] = ref[c, i] + core_land[i]
    if first:
        pl.semaphore_signal(core_free, inc=1, device_id={"c": across}, device_id_type=MESH)
    else:
        pl.semaphore_wait(ring_free, 2)
    yield from ring_sum(copies, "x", lambda i, p: ref.at[c, i, pl.ds(p * 64, 64)], land, 0, 1)
    for high in range(2):
        own = ref.at[c, x, pl.ds(high * 64, 64)]

        def chunk(r, _):
            rows = pl.ds(pl.multiple_of(r * 16, 16), 16)
            give(pl.ds(pl.multiple_of(high * 64 + r * 16, 16), 16), three(own, land, high, rows))
            return 0

        lax.fori_loop(0, 4, chunk, 0)
    if first:
        for way in (1, -1):
            to = {"x": other("x", way)}
            pl.semaphore_signal(ring_free, inc=1, device_id=to, device_id_type=MESH)


def return_to_group(copies, ref, out):
    c, x = lax.axis_index("c"), lax.axis_index("x")
    t = c * 4 + x
    sent = []
    for to in token_partners():
        sent.append(copies.start(ref.at[to["c"] * 4 + to["x"]], out.at[t], to))
    out[t] = ref[t]
    yield
    for copy in sent:
        copy.wait_recv()


def turned(values, table, sign):
    turn, ahead, behind = table
    up = pltpu.roll(values, PAIR - ROT // 2, 1)
    down = pltpu.roll(values, ROT // 2, 1)
    if sign > 0:
        return values * turn + up * ahead + down * behind
    return values * turn - up * ahead - down * behind


def attend(meta, turn_ref, qkv, att, g, p):
    low, f32 = jnp.bfloat16, jnp.float32
    lane = lax.broadcasted_iota(jnp.int32, (BLOCK, PAIR), 1)
    first = lane < HEAD
    zero = jnp.zeros((BLOCK, PAIR), low)
    row_at = lax.broadcasted_iota(jnp.int32, (BLOCK, BLOCK), 0)
    col_at = lax.broadcasted_iota(jnp.int32, (BLOCK, BLOCK), 1)
    cols = [pl.ds(pl.multiple_of(i * 2 * PAIR + p * PAIR, PAIR), PAIR) for i in range(3)]
    d_k = [jnp.zeros((BLOCK, PAIR), f32) for _ in range(4)]
    d_v = [jnp.zeros((BLOCK, PAIR), f32) for _ in range(4)]
    for b in range(4):
        rows, width = pl.ds(b * BLOCK, BLOCK), (b + 1) * BLOCK
        keys = pl.ds(0, width)
        base = meta[:, 4 + b : 5 + b] * BLOCK
        diagonal = (col_at <= row_at) & (col_at.astype(f32) + base < meta[:, 8 + b : 9 + b])
        bias = [
            jnp.where(meta[:, e : e + 1] == meta[:, b : b + 1], 0.0, MASKED)
            + jnp.zeros((BLOCK, BLOCK), f32)
            for e in range(b)
        ]
        bias.append(jnp.where(diagonal, 0.0, MASKED).astype(f32))
        bias = bias[0] if b == 0 else jnp.concatenate(bias, axis=1)
        q, da = qkv[g, rows, cols[0]], att[g, rows, cols[0]]
        k, v = qkv[g, keys, cols[1]], qkv[g, keys, cols[2]]
        qs = [jnp.where(first, q, zero), jnp.where(first, zero, q)]
        das = [jnp.where(first, da, zero), jnp.where(first, zero, da)]
        atts, probs, dss = [], [], []
        for h in range(2):
            s = dot_t(qs[h], k) + bias
            w = jnp.exp(s - jnp.max(s, axis=1, keepdims=True))
            prob = w * (1.0 / jnp.sum(w, axis=1, keepdims=True))
            probs.append(prob.astype(low))
            atts.append(dot(probs[h], v))
            dp = dot_t(das[h], v)
            dss.append((prob * (dp - jnp.sum(prob * dp, axis=1, keepdims=True))).astype(low))
        att[g, rows, cols[0]] = jnp.where(first, atts[0], atts[1]).astype(low)
        dq = jnp.where(first, dot(dss[0], k), dot(dss[1], k)) * SCALE
        qkv[g, rows, cols[0]] = turned(dq, table_of(meta, turn_ref, b), -1).astype(low)
        dk = cross(jnp.concatenate(dss, axis=0), jnp.concatenate(qs, axis=0))
        dv = cross(jnp.concatenate(probs, axis=0), jnp.concatenate(das, axis=0))
        for e in range(b + 1):
            d_k[e] = d_k[e] + dk[e * BLOCK : (e + 1) * BLOCK]
            d_v[e] = d_v[e] + dv[e * BLOCK : (e + 1) * BLOCK]
    for b in range(4):
        rows = pl.ds(b * BLOCK, BLOCK)
        qkv[g, rows, cols[1]] = turned(d_k[b], table_of(meta, turn_ref, b), -1).astype(low)
        qkv[g, rows, cols[2]] = d_v[b].astype(low)


def table_of(meta, turn_ref, b):
    rank = meta[:, 4 + b : 5 + b]
    parts = [turn_ref[:, pl.ds(r * BLOCK, BLOCK), :] for r in range(3)]
    table = jnp.where((rank == 0.0)[None], parts[0], jnp.where((rank == 1.0)[None], parts[1], parts[2]))
    return table[0], table[1], table[2]


def layer_kernel(
    tokens_ref, cot_ref, we_send, wq_send, wd_own, ws_own, vec_own, turn_ref,
    out_ref, ig_ref, ge_out, gq_out, gd_out, gs_out, vec_out,
    we, wq, wd, ws, normed, d_out, act, d_pre, qkv, att,
    ge, gq, gd, gs, tile, bias_e, vec_all, vec_rows,
    wide_e, narrow_e, wide_d, narrow_d, wide_s, narrow_s,
    core_land, ring_land, res_e, res_q, res_d,
    vec_sum, vec_part, vec_came, vec_mine, vec_zy,
    send, recv, core_free, ring_free, wide_free,
):
    low, f32 = jnp.bfloat16, jnp.float32
    z, y, c, x = (lax.axis_index(a) for a in ALL)
    t = c * 4 + x
    copies = Copies(send, recv)
    ws[z, y] = ws_own[...]
    vec_all[z, y, c, x] = vec_own[...]

    own_meta = vec_own[pl.ds(4, 1), :]
    lane = lax.broadcasted_iota(jnp.int32, (1, PAIR), 1)
    own_rank = jnp.sum(jnp.where(lane == 4 + x, own_meta, 0.0), axis=1, keepdims=True)
    own_limit = jnp.sum(jnp.where(lane == 8 + x, own_meta, 0.0), axis=1, keepdims=True)

    def d_out_rows(rows, first):
        row_at = lax.broadcasted_iota(jnp.int32, (16, 1), 0) + first
        live = (row_at.astype(f32) + own_rank * BLOCK < own_limit).astype(f32)
        return cot_ref[rows, :].astype(f32) * live

    def mask_chunk(r, _):
        rows = pl.ds(pl.multiple_of(r * 16, 16), 16)
        d_out[c, x, rows] = d_out_rows(rows, r * 16).astype(low)
        return 0

    lax.fori_loop(0, 8, mask_chunk, 0)
    enter()

    vectors = gather_vectors(copies, vec_all)
    step(vectors)
    shrink = gather_weights(copies, by_rows(ws, 64))
    step(shrink)
    into_expand = expand_to_group(copies, we_send, we, 1024)
    step(into_expand)
    dense_here = copies.start(
        wd_own, wd.at[dense_partner()["z"], dense_partner()["y"]], dense_partner()
    )
    into_qkv = expand_to_group(copies, wq_send, wq, 768)
    step(into_qkv)
    cotangent = gather_tokens(copies, d_out)
    step(cotangent)
    step(vectors)
    step(into_expand)
    expand = gather_weights(copies, by_rows(we, 128))
    step(expand)
    step(shrink)
    step(vectors)
    vec_rows[...] = jnp.zeros_like(vec_rows)
    for d in range(128):
        first = (176 * d) // 128
        vec_rows[pl.ds(first, 3), :] += vec_all[
            d // 32, (d // 8) % 4, (d // 4) % 2, d % 4, pl.ds(0, 3), :
        ]

    def norm_chunk(r, _):
        rows = pl.ds(pl.multiple_of(r * 16, 16), 16)
        values = tokens_ref[rows, :].astype(f32)
        center = values - jnp.mean(values, axis=1, keepdims=True)
        inverse = lax.rsqrt(jnp.mean(center * center, axis=1, keepdims=True) + NORM_EPS)
        own = center * inverse * row_of(vec_rows, 0, 16) + row_of(vec_rows, 16, 16)
        normed[c, x, rows] = own.astype(low)
        return 0

    lax.fori_loop(0, 8, norm_chunk, 0)
    forward = gather_tokens(copies, normed)
    step(forward)
    step(shrink)
    step(expand)
    step(cotangent)
    dense_here.wait_recv()
    dense = gather_weights(copies, by_columns(wd, 2048))
    step(into_qkv)
    qkv_w = gather_weights(copies, by_rows(wq, 128))
    step(expand)
    step(forward)
    step(cotangent)
    step(dense, qkv_w)
    step(shrink)
    step(forward, cotangent)
    step(dense, qkv_w)
    step(expand)
    step(shrink)
    step(dense, qkv_w)
    step(forward)
    step(expand)

    odd = lax.rem(t, 2) == 1
    half = t // 2
    left = lane < HEAD
    bias_e[...] = jnp.zeros_like(bias_e)
    for j in range(8):
        r0 = vec_rows[pl.ds(96 + 8 * j + half, 1), :]
        r1 = vec_rows[pl.ds(100 + 8 * j + half, 1), :]
        even_row = jnp.where(left, r0, pltpu.roll(r1, HEAD, 1))
        odd_row = jnp.where(left, pltpu.roll(r0, HEAD, 1), r1)
        bias_e[pl.ds(0, 1), pl.ds(j * PAIR, PAIR)] = jnp.where(odd, odd_row, even_row)

    def up_tile(i, _):
        g, n = i // 2, lax.rem(i, 2)
        cols = pl.ds(pl.multiple_of(n * 512, 512), 512)
        tile[0] = dot(normed[g].reshape(512, MODEL), we[:, :, :, cols].reshape(MODEL, 512))
        tile[1] = dot_t(d_out[g].reshape(512, MODEL), ws[pl.ds(2 * n, 2)].reshape(512, MODEL))

        def chunk(r, _):
            rows = pl.ds(pl.multiple_of(r * 16, 16), 16)
            pre = tile[0, rows, :] + bias_e[pl.ds(0, 1), cols]
            square = pre * pre
            inner = jnp.tanh(GELU_A * (pre + GELU_B * (square * pre)))
            cover = 0.5 + 0.5 * inner
            act[g, rows, cols] = (pre * cover).astype(low)
            slope = cover + 0.5 * pre * (1.0 - inner * inner) * (
                GELU_A + (3.0 * GELU_A * GELU_B) * square
            )
            d_pre[g, rows, cols] = (tile[1, rows, :] * slope).astype(low)
            return 0

        lax.fori_loop(0, 32, chunk, 0)
        return 0

    lax.fori_loop(0, 2, up_tile, 0)
    step(dense, qkv_w)
    lax.fori_loop(2, 4, up_tile, 0)
    step(dense, qkv_w)

    def shrink_tile(i, _):
        j, n = i // 2, lax.rem(i, 2)
        cols = pl.ds(pl.multiple_of(n * 1024, 1024), 1024)
        mine = act[:, :, pl.ds(pl.multiple_of(j * 512, 512), 512)].reshape(1024, 512)
        term = cross(mine, d_out[:, :, :, cols].reshape(1024, 1024))
        gs[pl.ds(2 * j, 2), :, :, cols] = term.astype(low).reshape(2, 4, 64, 1024)
        return 0

    lax.fori_loop(0, 4, shrink_tile, 0)

    def give_s(part, total):
        gs_out[pl.ds(part * 16, 16), :] = total

    sum_s = scatter_weights(copies, by_rows(gs, 64), wide_s, narrow_s, give_s)
    step(sum_s)

    def grad_tile(left_ref, right_ref, out, width):
        def body(i, _):
            mine = left_ref[:, :, :, pl.ds(pl.multiple_of(i * 512, 512), 512)].reshape(1024, 512)
            term = cross(mine, right_ref[...].reshape(1024, width))
            out[i] = term.astype(low).reshape(4, BLOCK, width)
            return 0

        return body

    expand_tile = grad_tile(normed, d_pre, ge, 1024)
    lax.fori_loop(0, 4, expand_tile, 0)

    def give_e(part, total):
        res_e[pl.ds(2 * part, 2)] = total.astype(low).reshape(2, 16, 1024)

    sum_e = scatter_weights(copies, by_rows(ge, 128), wide_e, narrow_e, give_e)
    step(sum_e)
    step(sum_s)

    def qkv_tile(g, _):
        meta = vec_all[z, y, g, x, pl.ds(4, 1), :]
        projected = dot(normed[g].reshape(512, MODEL), wq[...].reshape(MODEL, 768))
        for p in range(6):
            bias = vec_rows[pl.ds(32 + (p // 2) * 16 + (1 - p % 2) * 8 + t, 1), :]
            for b in range(4):
                rows = pl.ds(b * BLOCK, BLOCK)
                part = projected[b * BLOCK : (b + 1) * BLOCK, p * PAIR : (p + 1) * PAIR] + bias
                if p < 4:
                    part = turned(part, table_of(meta, turn_ref, b), 1)
                part = part.astype(low)
                if p < 2:
                    part = part * jnp.asarray(SCALE, low)
                qkv[g, rows, pl.ds(p * PAIR, PAIR)] = part
        att[g] = dot_t(d_out[g].reshape(512, MODEL), wd[...].reshape(256, MODEL)).astype(low)
        return 0

    lax.fori_loop(0, 2, qkv_tile, 0)
    step(sum_e)
    step(sum_s)

    def attend_tile(i, _):
        g, p = i // 2, lax.rem(i, 2)
        attend(vec_all[z, y, g, x, pl.ds(4, 1), :], turn_ref, qkv, att, g, p)
        return 0

    lax.fori_loop(0, 2, attend_tile, 0)
    step(sum_e)
    step(sum_s)
    lax.fori_loop(2, 4, attend_tile, 0)
    step(sum_s)
    step(sum_e)

    def dense_tile(n, _):
        cols = pl.ds(pl.multiple_of(n * 1024, 1024), 1024)
        term = cross(att[...].reshape(1024, 256), d_out[:, :, :, cols].reshape(1024, 1024))
        gd[:, :, :, cols] = term.astype(low).reshape(4, 4, 16, 1024)
        return 0

    lax.fori_loop(0, 2, dense_tile, 0)

    def give_d(part, total):
        res_d[:, pl.ds(part * 512, 512)] = total.astype(low)

    sum_d = scatter_weights(copies, by_columns(gd, 2048), wide_d, narrow_d, give_d)
    step(sum_d)
    qkv_grad_tile = grad_tile(normed, qkv, gq, 768)
    lax.fori_loop(0, 4, qkv_grad_tile, 0)

    def give_q(part, total):
        res_q[pl.ds(2 * part, 2)] = total.astype(low).reshape(2, 16, 768)

    for _ in sum_e:
        pass
    for axis in ("y", "z"):
        for way in (1, -1):
            to = {axis: other(axis, way)}
            pl.semaphore_signal(wide_free, inc=1, device_id=to, device_id_type=MESH)
    pl.semaphore_wait(wide_free, 4)
    short = pl.ds(0, 768)
    sum_q = scatter_weights(
        copies, by_rows(gq, 128), wide_e.at[:, :, :, :, short], narrow_e.at[:, :, :, short], give_q
    )
    step(sum_q)
    back_e = return_to_group(copies, res_e, ge_out)
    step(back_e)

    for work in (forward, cotangent):
        for _ in work:
            pass

    def down_tile(g):
        def body(i, _):
            cols = pl.ds(pl.multiple_of(i * 512, 512), 512)
            term = dot_t(qkv[g], wq[i].reshape(512, 768)) + dot_t(d_pre[g], we[i].reshape(512, 1024))
            normed[g, :, :, cols] = term.astype(low).reshape(4, BLOCK, 512)
            return 0

        return body

    lax.fori_loop(0, 4, down_tile(1 - c), 0)

    gain = row_of(vec_rows, 0, 16)

    vec_sum[...] = jnp.zeros_like(vec_sum)

    def give_n(rows, total):
        mine = tokens_ref[rows, :].astype(f32)
        middle = mine - jnp.mean(mine, axis=1, keepdims=True)
        spread = lax.rsqrt(jnp.mean(middle * middle, axis=1, keepdims=True) + NORM_EPS)
        xhat = middle * spread
        e = total * gain
        d_in = spread * (
            e - jnp.mean(e, axis=1, keepdims=True) - xhat * jnp.mean(e * xhat, axis=1, keepdims=True)
        )
        dy = d_out_rows(rows, rows.start)
        ig_ref[rows, :] = (dy + d_in).astype(low)
        for i, value in enumerate((total * xhat, total, dy)):
            vec_sum[i] += value[0:8] + value[8:16]

    sum_n = scatter_tokens(copies, normed, core_land, ring_land, give_n, core_free, ring_free, True)
    step(sum_n)
    lax.fori_loop(0, 4, down_tile(c), 0)
    step(sum_d, sum_q)
    step(sum_n)

    def out_tile(g):
        def body(i, _):
            cols = pl.ds(pl.multiple_of(i * 512, 512), 512)
            term = dot(att[g], wd[:, :, :, cols].reshape(256, 512)) + dot(
                act[g], ws[:, :, :, cols].reshape(1024, 512)
            )
            d_out[g, :, :, cols] = term.astype(low).reshape(4, BLOCK, 512)
            return 0

        return body

    lax.fori_loop(0, 4, out_tile(1 - c), 0)
    add_bias = row_of(vec_rows, 80, 16) + row_of(vec_rows, 160, 16)

    def give_o(rows, total):
        out_ref[rows, :] = (tokens_ref[rows, :].astype(f32) + (total + add_bias)).astype(low)

    sum_o = scatter_tokens(copies, d_out, core_land, ring_land, give_o, core_free, ring_free, False)
    step(sum_o)
    step(sum_d, sum_q)
    lax.fori_loop(0, 4, out_tile(c), 0)
    step(sum_n)
    ones = jnp.ones((8, 1024), low)
    vec_mine[...] = jnp.zeros_like(vec_mine)
    vec_mine[pl.ds(3, 1), pl.ds(0, 768)] = dot(ones, qkv[...].reshape(1024, 768))[0:1]
    vec_mine[pl.ds(4, 1), :] = dot(ones, d_pre[...].reshape(1024, 1024))[0:1]
    step(sum_d, sum_q)
    step(sum_n)
    vec_part[...] = jnp.zeros_like(vec_part)
    for i in range(3):
        total = jnp.sum(vec_sum[i], axis=0, keepdims=True)
        for k in range(8):
            vec_part[k, pl.ds(i, 1), :] = total[:, k * 256 : k * 256 + 256]
    sent = []
    for to in token_partners():
        sent.append(copies.start(vec_part.at[to["c"] * 4 + to["x"]], vec_came.at[t], to))
    vec_came[t] = vec_part[t]
    step(sum_o)
    step(sum_d, sum_q)
    back_q = return_to_group(copies, res_q, gq_out)
    step(back_q)
    dense_back = copies.start(res_d, gd_out, dense_partner())
    for copy in sent:
        copy.wait_recv()
    vec_mine[pl.ds(0, 3), pl.ds(0, 256)] = jnp.sum(vec_came[...], axis=0)[0:3]
    vec_zy[z, y] = vec_mine[...]
    sent = [copies.start(vec_mine, vec_zy.at[z, y], to) for to in weight_partners()]
    step(sum_o)
    for copy in sent:
        copy.wait_recv()
    vec_out[c, x] = jnp.sum(vec_zy[...].reshape(16, 8, 1024), axis=0)
    sent = [copies.start(vec_out.at[c, x], vec_out.at[c, x], to) for to in token_partners()]
    step(sum_o)
    step(back_e, back_q)
    dense_back.wait_recv()
    for copy in sent:
        copy.wait_recv()
    for work in (sum_s, sum_e, sum_d, sum_q, sum_n, sum_o, back_e, back_q, vectors, shrink, expand,
                 dense, qkv_w, forward, cotangent, into_expand, into_qkv):
        for _ in work:
            pass
    copies.finish()


def layer(tokens, cotangent, we_send, wq_send, wd_own, ws_own, vec_own):
    low, f32 = jnp.bfloat16, jnp.float32
    vmem = pl.BlockSpec(memory_space=pltpu.VMEM)
    turn = jnp.asarray(np.stack(rotary_constants())[:, : 3 * BLOCK])
    outs = [
        ((BLOCK, MODEL), low), ((BLOCK, MODEL), low), ((8, 16, 1024), low), ((8, 16, 768), low),
        ((16, MODEL), low), ((64, MODEL), f32), ((2, 4, 8, 1024), f32),
    ]
    held = [
        ((4, 4, 128, 1024), low), ((4, 4, 128, 768), low), ((4, 4, 16, 2048), low),
        ((4, 4, 64, 2048), low), ((2, 4, 128, 2048), low), ((2, 4, 128, 2048), low),
        ((2, 512, 1024), low), ((2, 512, 1024), low), ((2, 512, 768), low), ((2, 512, 256), low),
        ((4, 4, 128, 1024), low), ((4, 4, 128, 768), low), ((4, 4, 16, 2048), low),
        ((4, 4, 64, 2048), low), ((2, 512, 512), f32), ((8, 1024), f32),
        ((4, 4, 2, 4, 8, 128), f32), ((184, 128), f32),
        ((2, 6, 4, 32, 1024), low), ((2, 6, 32, 1024), low),
        ((2, 6, 4, 16, 512), low), ((2, 6, 16, 512), low),
        ((2, 6, 4, 16, 2048), low), ((2, 6, 16, 2048), low),
        ((4, 128, 2048), low), ((6, 64, 2048), low),
        ((8, 16, 1024), low), ((8, 16, 768), low), ((16, 2048), low),
        ((3, 8, MODEL), f32), ((8, 8, 256), f32), ((8, 8, 256), f32), ((8, 1024), f32), ((4, 4, 8, 1024), f32),
    ]
    return pl.pallas_call(
        layer_kernel,
        in_specs=[vmem] * 8,
        out_specs=[vmem] * 7,
        out_shape=[jax.ShapeDtypeStruct(s, k) for s, k in outs],
        scratch_shapes=[pltpu.VMEM(s, k) for s, k in held]
        + [
            pltpu.SemaphoreType.DMA((COPIES,)),
            pltpu.SemaphoreType.DMA((COPIES,)),
            pltpu.SemaphoreType.REGULAR,
            pltpu.SemaphoreType.REGULAR,
            pltpu.SemaphoreType.REGULAR,
        ],
        compiler_params=pltpu.CompilerParams(
            collective_id=0, has_side_effects=True, vmem_limit_bytes=64 * 2**20
        ),
        name="layer",
    )(tokens, cotangent, we_send, wq_send, wd_own, ws_own, vec_own, turn)


def adam_step(weight, moment, second, gradient, step_rate, step_decay):
    moment_new = BETA_ONE * moment + (1 - BETA_ONE) * gradient
    second_new = BETA_TWO * second + (1 - BETA_TWO) * gradient * gradient
    moment_hat = moment_new / (1 - BETA_ONE**STEP)
    second_hat = second_new / (1 - BETA_TWO**STEP)
    updated = weight - step_rate * (
        moment_hat / (jnp.sqrt(second_hat) + ADAM_EPS) + step_decay * weight
    )
    return (second_new, updated)


def block_ranks(block_row):
    same = block_row[:, None] == block_row[None, :]
    earlier = jnp.arange(4)[None, :] < jnp.arange(4)[:, None]
    return jnp.sum(jnp.where(same & earlier, 1, 0), axis=1)


def qkv_out(value):
    lead = value.shape[:-1]
    parts = value.reshape(*lead, 3, 2, TPN, PAIR)[..., ::-1, :, :]
    return jnp.moveaxis(parts, -2, 0).reshape(TPN, *lead, 6 * PAIR)


def qkv_back(parts):
    lead = parts.shape[1:-1]
    parts = jnp.moveaxis(parts.reshape(TPN, *lead, 3, 2, PAIR), 0, -2)[..., ::-1, :, :]
    return parts.reshape(*lead, 3 * MODEL)


def expand_out(value):
    lead = value.shape[:-1]
    parts = value.reshape(*lead, FF // 512, TPN, 64)
    return jnp.moveaxis(parts, -2, 0).reshape(TPN, *lead, FF // TPN)


def expand_back(parts):
    lead = parts.shape[1:-1]
    parts = jnp.moveaxis(parts.reshape(TPN, *lead, FF // 512, 64), 0, -2)
    return parts.reshape(*lead, FF)


def to_group(parts):
    return lax.all_to_all(parts, TP, split_axis=0, concat_axis=0, tiled=True)


def placed(value, t):
    return lax.dynamic_update_index_in_dim(
        jnp.zeros((TPN, value.shape[0]), jnp.float32), value, t, axis=0
    )


def dense_route():
    pairs = []
    for z, y, c, x in np.ndindex(*SIZES):
        target = (((1 - z // 2) * 2 + c) * 4 + x) * 8 + (z % 2) * 4 + y
        pairs.append((((z * 4 + y) * 2 + c) * 4 + x, target))
    return pairs


def gathered(value, axes):
    return lax.all_gather(value, axes, axis=0, tiled=True)


def summed(value, axes):
    return lax.psum_scatter(value, axes, scatter_dimension=0, tiled=True)


def shards(
    tokens, cotangent, block_seq, seq_lengths,
    qkv_weight, qkv_moment, qkv_second,
    dense_weight, dense_moment, dense_second,
    expand_weight, expand_moment, expand_second,
    shrink_weight, shrink_moment, shrink_second,
    vectors, vec_moment, vec_second,
):
    z, y, c, x = (lax.axis_index(a) for a in ALL)
    t = c * 4 + x
    low = jnp.bfloat16
    place = ((z * 4 + y) * 8 + t) * 176
    block_row = block_seq[0]
    limits = jnp.where(block_row == 0, seq_lengths[0, 0], seq_lengths[0, 1])
    meta = jnp.concatenate([block_row, block_ranks(block_row), limits]).astype(jnp.float32)
    vec_own = jnp.zeros((1024,), jnp.float32).at[512 : 512 + 12].set(meta)
    vec_own = lax.dynamic_update_slice(
        vec_own, vectors.astype(low).astype(jnp.float32), (lax.rem(place, 128),)
    ).reshape(8, 128)
    output, input_grad, expand_back_rows, qkv_back_rows, dense_rows, shrink_grad, vec_sums = layer(
        tokens,
        cotangent,
        expand_out(expand_weight.astype(low)),
        qkv_out(qkv_weight.astype(low)),
        dense_weight.astype(low),
        shrink_weight.astype(low),
        vec_own,
    )
    expand_grad = expand_back(expand_back_rows).astype(jnp.float32)
    qkv_grad = qkv_back(qkv_back_rows).astype(jnp.float32)
    dense_grad = dense_rows.astype(jnp.float32)
    sums = vec_sums.reshape(TPN, 8, 1024)
    d_out_sum = sums[:, 2, :256].reshape(-1)
    vec_terms = jnp.concatenate(
        [
            sums[:, 0, :256].reshape(-1),
            sums[:, 1, :256].reshape(-1),
            qkv_back(sums[:, 3, :768]),
            d_out_sum,
            expand_back(sums[:, 4]),
            d_out_sum,
        ]
    )
    vec_grad = lax.dynamic_slice(vec_terms, (place,), (176,))

    masters = (qkv_weight, dense_weight, expand_weight, shrink_weight, vectors)
    moments = (qkv_moment, dense_moment, expand_moment, shrink_moment, vec_moment)
    seconds = (qkv_second, dense_second, expand_second, shrink_second, vec_second)
    gradients = (qkv_grad, dense_grad, expand_grad, shrink_grad, vec_grad)
    results = [output, input_grad]
    for i in range(5):
        state_new, weight_new = adam_step(
            masters[i], moments[i], seconds[i], gradients[i], RATES[i], DECAYS[i]
        )
        results.extend([gradients[i], state_new, weight_new])
    return tuple(results)


def solution(mesh):
    finer = Mesh(mesh.devices.reshape(*SIZES), ALL)
    whole, group = P(ALL, None), P(DP, None)
    return jax.shard_map(
        shards,
        mesh=finer,
        in_specs=(whole, whole, group, group, *[whole] * 12, *[P(ALL)] * 3),
        out_specs=(*[whole] * 14, *[P(ALL)] * 3),
        check_vma=False,
    )
```

```python
import functools

import jax
import jax.numpy as jnp
import numpy as np
from jax import lax
from jax.experimental import pallas as pl
from jax.experimental.pallas import tpu as pltpu
from jax.sharding import Mesh
from jax.sharding import PartitionSpec as P

HEAD = 64
ROT = 32
BLOCK = 128
STEP = 10
GROUP = 512
MODEL = 2048
FF = 8192
PAIR = 2 * HEAD
ALL = ("z", "y", "c", "x")
DP = ("z", "y", "c")
ZY = ("z", "y")
TP = ("c", "x")
SIZES = (4, 4, 2, 4)
TPN = 8
COPIES = 480
SCHEDULE = (
    "to_q", "to_d", "s", "d", "tok", "q", "d", "s", "vec", "cot", "vec_rows", "q", "norm_own",
    "d", "d", "q", "q", "cot", "s", "s", "q", "d", "norm_sides", "to_e", "norm_far", "qkv0",
    "e", "qkv1", "att0", "to_d", "s", "e", "att1", "att2", "to_q", "e", "att3", "e", "grad_d",
    "e", "to_e", "grad_q0", "grad_q1", "tok", "sum_q", "up0", "up1", "sum_d", "up2", "sum_q",
    "e", "up3", "vec", "grad_e0", "sum_d", "vec", "sum_e0", "grad_e1", "s", "sum_e1", "downa0",
    "n0", "downb0", "downa1", "n0", "n1", "tok", "sum_q", "downb1", "cot", "grad_s0", "sum_q",
    "sum_e0", "sum_e1", "n0", "n1", "q", "d", "e", "d", "e", "grad_s1", "sum_q", "sum_d",
    "outa0", "o0", "sum_s0", "cot", "outb0", "back_q", "sum_s1", "n1", "sum_d", "outa1", "o1",
    "outb1", "back_d", "o0", "sum_e0", "sum_e1", "sum_s1", "back_q", "o1", "sum_e0", "col_sums",
    "norm_back", "sum_e0", "sum_e1", "q", "sum_s0", "o0", "e", "s", "d", "vec_back", "sum_s1",
    "o1", "sum_s1", "sum_d", "back_e", "back_d", "vec_back", "sum_s0", "n1", "e", "s",
    "vec_back", "n0", "o0", "sum_s1", "sum_e0", "sum_s0", "o1", "sum_s0", "cot", "back_e",
    "vec_back", "sum_q", "sum_d", "vec_back",
)
SCALE = HEAD ** (-0.5)

NORM_EPS = 1e-05
MASKED = -1e30
BETA_ONE = 0.9
BETA_TWO = 0.999
ADAM_EPS = 1e-08
RATES = (0.02, 0.1, 0.02, 0.01, 0.4)
DECAYS = (0.1, 0.1, 0.1, 0.1, 0.0)
GELU_A = float(np.sqrt(2.0 / np.pi))
GELU_B = 0.044715


def dot(a, b):
    return jnp.dot(a, b, preferred_element_type=jnp.float32)


def dot_t(a, b):
    return lax.dot_general(a, b, (((1,), (1,)), ((), ())), preferred_element_type=jnp.float32)


def cross(a, b):
    return lax.dot_general(a, b, (((0,), (0,)), ((), ())), preferred_element_type=jnp.float32)


def rotary_constants():
    half = np.arange(ROT // 2, dtype=np.float32)
    inverse = (10000.0 ** (-2.0 * half.astype(np.float64) / ROT)).astype(np.float32)
    angle = (np.arange(GROUP, dtype=np.float32)[:, None] * inverse[None, :]).astype(np.float64)
    cosine, sine = np.cos(angle).astype(np.float32), np.sin(angle).astype(np.float32)
    one = np.ones((GROUP, HEAD - ROT), np.float32)
    zero = np.zeros((GROUP, ROT // 2), np.float32)
    rest = np.zeros((GROUP, HEAD - ROT), np.float32)
    turn = np.concatenate([cosine, cosine, one], axis=1)
    ahead = np.concatenate([-sine, zero, rest], axis=1)
    behind = np.concatenate([zero, sine, rest], axis=1)
    return tuple(np.concatenate([a, a], axis=1) for a in (turn, ahead, behind))


MESH = pl.DeviceIdType.MESH


def other(axis, step):
    size = SIZES[ALL.index(axis)]
    return lax.rem(lax.axis_index(axis) + step + size, size)


class Copy:
    def __init__(self, copy):
        self.copy, self.here, self.gone = copy, False, False

    def arrive(self):
        if not self.here:
            self.copy.wait_recv()
        self.here = True

    def leave(self):
        if not self.gone:
            self.copy.wait_send()
        self.gone = True


class Copies:
    def __init__(self, send, recv):
        self.send, self.recv, self.all = send, recv, []

    def start(self, src, dst, to):
        at = len(self.all)
        copy = pltpu.make_async_remote_copy(
            src_ref=src,
            dst_ref=dst,
            send_sem=self.send.at[at],
            recv_sem=self.recv.at[at],
            device_id=to,
            device_id_type=MESH,
        )
        copy.start()
        self.all.append(Copy(copy))
        return self.all[-1]

    def finish(self):
        for copy in self.all:
            copy.leave()


def greet():
    barrier = pltpu.get_barrier_semaphore()
    for partner in token_partners() + weight_partners() + [dense_partner()]:
        pl.semaphore_signal(barrier, inc=1, device_id=partner, device_id_type=MESH)


def enter():
    pl.semaphore_wait(pltpu.get_barrier_semaphore(), 23)


def token_partners():
    return [{"c": other("c", i), "x": other("x", j)} for i in range(2) for j in range(4) if i + j]


def weight_partners():
    return [{"z": other("z", i), "y": other("y", j)} for i in range(4) for j in range(4) if i + j]


def dense_partner():
    z, y, c, x = (lax.axis_index(a) for a in ALL)
    return {"z": (1 - z // 2) * 2 + c, "y": x, "c": lax.rem(z, 2), "x": y}


def gather_weights(copies, view):
    z, y = lax.axis_index("z"), lax.axis_index("y")
    z_up, z_down, y_up, y_down = other("z", 1), other("z", -1), other("y", 1), other("y", -1)
    z_far, y_far = other("z", 2), other("y", 2)
    up, down, far, near = {"y": y_up}, {"y": y_down}, {"z": z_up}, {"z": z_down}

    def go(block, to):
        return copies.start(block, block, to)

    a_up, a_down = go(view(z, y, 4), up), go(view(z, y, 4), down)
    b_up, b_down = go(view(z, y, 5), far), go(view(z, y, 5), near)
    a_own = go(view(z, y, 4), far), go(view(z, y, 4), near)
    b_own = go(view(z, y, 5), up), go(view(z, y, 5), down)
    yield
    a_up.arrive()
    a_low = go(view(z, y_down, 0), up)
    b_up.arrive()
    b_low = go(view(z_down, y, 2), far)
    a_down.arrive()
    a_high = go(view(z, y_up, 1), down)
    b_down.arrive()
    b_high = go(view(z_up, y, 3), near)
    a_side = [(i, go(view(z, i, 4), far), go(view(z, i, 4), near)) for i in (y_down, y_up)]
    b_side = [(i, go(view(i, y, 5), up), go(view(i, y, 5), down)) for i in (z_down, z_up)]
    yield
    last = []
    a_own[0].arrive()
    last.append(go(view(z_down, y, 0), far))
    b_own[0].arrive()
    last.append(go(view(z, y_down, 2), up))
    a_own[1].arrive()
    last.append(go(view(z_up, y, 1), near))
    b_own[1].arrive()
    last.append(go(view(z, y_up, 3), down))
    a_low.arrive()
    a_high.arrive()
    a_side.append((y_far, go(view(z, y_far, 4), far), go(view(z, y_far, 4), near)))
    b_low.arrive()
    b_high.arrive()
    b_side.append((z_far, go(view(z_far, y, 5), up), go(view(z_far, y, 5), down)))
    for k in range(3):
        if k != 1:
            yield
        i, first, second = a_side[k]
        first.arrive()
        last.append(go(view(z_down, i, 0), far))
        second.arrive()
        last.append(go(view(z_up, i, 1), near))
        i, first, second = b_side[k]
        first.arrive()
        last.append(go(view(i, y_down, 2), up))
        second.arrive()
        last.append(go(view(i, y_up, 3), down))
    yield
    for copy in last:
        copy.arrive()


def gather_tokens(copies, ref, sent):
    c, x, across = lax.axis_index("c"), lax.axis_index("x"), other("c", 1)
    right, left = {"x": other("x", 1)}, {"x": other("x", -1)}

    def go(block, to):
        return copies.start(block, block, to)

    own = ref.at[c, x]
    sent.append([go(own, right), go(own, left), go(own, {"c": across})])
    yield
    sent[0][0].arrive()
    last = [go(ref.at[c, other("x", -1), pl.ds(0, 64)], right)]
    side = [go(ref.at[c, other("x", -1)], {"c": across})]
    sent[0][1].arrive()
    last.append(go(ref.at[c, other("x", 1), pl.ds(64, 64)], left))
    side.append(go(ref.at[c, other("x", 1)], {"c": across}))
    sent.append(last + side)
    yield
    for copy in last:
        copy.arrive()
    sent.append([go(ref.at[c, other("x", 2)], {"c": across})])
    yield
    for copies_of_stage in sent:
        for copy in copies_of_stage:
            copy.arrive()
            copy.leave()


def gather_vectors(copies, group, rows, ref):
    z, y, c, x = (lax.axis_index(a) for a in ALL)
    sent = [copies.start(group.at[c, x], group.at[c, x], to) for to in token_partners()]
    yield
    for copy in sent:
        copy.arrive()
    rows[pl.ds(0, 16), :] = jnp.zeros((16, PAIR), jnp.float32)
    for d in range(TPN):
        rows[pl.ds((176 * d) // PAIR, 3), :] += group[d // 4, d % 4, pl.ds(0, 3), :]
    ref[z, y] = rows[pl.ds(0, 16), :].astype(jnp.bfloat16)
    sent = [copies.start(ref.at[z, y], ref.at[z, y], to) for to in weight_partners()]
    yield
    for copy in sent:
        copy.arrive()


def expand_to_group(copies, send, ref, width):
    z, y, c, x = (lax.axis_index(a) for a in ALL)
    rows = pl.ds(pl.multiple_of((c * 4 + x) * 16, 16), 16)
    sent = []
    for to in token_partners():
        sent.append(copies.start(send.at[to["c"] * 4 + to["x"]], ref.at[z, y, rows], to))
    ref[z, y, rows] = send[c * 4 + x]
    yield
    for copy in sent:
        copy.arrive()


def by_rows(ref, rows):
    quarter = rows // 4

    def view(z, y, part):
        start, size = (part * quarter, quarter) if part < 4 else ((part - 4) * 2 * quarter, 2 * quarter)
        return ref.at[z, y, pl.ds(start, size)]

    return view


def by_columns(ref, columns):
    quarter = columns // 4

    def view(z, y, part):
        start, size = (part * quarter, quarter) if part < 4 else ((part - 4) * 2 * quarter, 2 * quarter)
        return ref.at[z, y, :, pl.ds(start, size)]

    return view


def step(*works):
    for work in works:
        next(work, None)


def row_of(ref, first, count):
    return jnp.concatenate([ref[pl.ds(first + i, 1), :] for i in range(count)], axis=1)


def ring_sum(copies, axis, block, land, low_part, high_part):
    ahead, behind = other(axis, 1), other(axis, -1)
    up, down = {axis: ahead}, {axis: behind}
    far = other(axis, 2)
    t_low = copies.start(block(far, low_part), land.at[0], up)
    t_high = copies.start(block(far, high_part), land.at[1], down)
    d_high = copies.start(block(ahead, high_part), land.at[3], up)
    d_low = copies.start(block(behind, low_part), land.at[2], down)
    yield
    t_low.arrive()
    land[0] = land[0] + block(ahead, low_part)[...]
    p_low = copies.start(land.at[0], land.at[4], up)
    t_high.arrive()
    land[1] = land[1] + block(behind, high_part)[...]
    p_high = copies.start(land.at[1], land.at[5], down)
    yield
    for copy in (d_low, d_high, p_low, p_high):
        copy.arrive()
    for copy in (t_low, t_high, d_low, d_high, p_low, p_high):
        copy.leave()


def three(own, land, high, at=...):
    f32 = jnp.float32
    first, second = land.at[4 + high], land.at[2 + high]
    return own[at].astype(f32) + first[at].astype(f32) + second[at].astype(f32)


def both(first, second):
    while True:
        done = [next(first, 0), next(second, 0)]
        if 0 in done:
            return
        yield


def scatter_weights(copies, view, wide, narrow, give):
    z, y = lax.axis_index("z"), lax.axis_index("y")
    every = slice(None)
    low = jnp.bfloat16
    yield from both(
        ring_sum(copies, "y", lambda i, p: view(every, i, p), wide.at[0], 0, 1),
        ring_sum(copies, "z", lambda i, p: view(i, every, p), wide.at[1], 2, 3),
    )
    for high in range(2):
        own = view(every, y, high)
        for i in range(4):
            own[i] = three(own, wide.at[0], high, i).astype(low)
        own = view(z, every, 2 + high)
        for i in range(4):
            own[i] = three(own, wide.at[1], high, i).astype(low)
    yield from both(
        ring_sum(copies, "z", lambda i, p: view(i, y, p), narrow.at[0], 0, 1),
        ring_sum(copies, "y", lambda i, p: view(z, i, p), narrow.at[1], 2, 3),
    )
    for high in range(2):
        give(high, three(view(z, y, high), narrow.at[0], high))
        give(2 + high, three(view(z, y, 2 + high), narrow.at[1], high))


def scatter_tokens(copies, ref, core_land, land, give, core_free, ring_free, first):
    c, x, across = lax.axis_index("c"), lax.axis_index("x"), other("c", 1)
    if not first:
        pl.semaphore_wait(core_free, 1)
    came = copies.start(ref.at[across], core_land, {"c": across})
    yield
    came.arrive()
    for i in range(4):
        ref[c, i] = ref[c, i] + core_land[i]
    if first:
        pl.semaphore_signal(core_free, inc=1, device_id={"c": across}, device_id_type=MESH)
    else:
        pl.semaphore_wait(ring_free, 2)
    yield from ring_sum(copies, "x", lambda i, p: ref.at[c, i, pl.ds(p * 64, 64)], land, 0, 1)
    for high in range(2):
        own = ref.at[c, x, pl.ds(high * 64, 64)]

        def chunk(r, _):
            rows = pl.ds(pl.multiple_of(r * 16, 16), 16)
            give(high, r, three(own, land, high, rows))
            return 0

        lax.fori_loop(0, 4, chunk, 0)
    if first:
        for way in (1, -1):
            to = {"x": other("x", way)}
            pl.semaphore_signal(ring_free, inc=1, device_id=to, device_id_type=MESH)


def landed(copy):
    yield
    copy.arrive()


def sum_vectors(copies, part, came, mine, zy, out):
    z, y, c, x = (lax.axis_index(a) for a in ALL)
    t = c * 4 + x
    sent = [
        copies.start(part.at[to["c"] * 4 + to["x"]], came.at[t], to) for to in token_partners()
    ]
    came[t] = part[t]
    yield
    for copy in sent:
        copy.arrive()
    total = jnp.sum(came[...], axis=0)
    for i in range(6):
        mine[pl.ds(i, 1), :] = total[i // 2 : i // 2 + 1, (i % 2) * PAIR : (i % 2 + 1) * PAIR]
    zy[z, y] = mine[...]
    sent = [copies.start(mine, zy.at[z, y], to) for to in weight_partners()]
    yield
    for copy in sent:
        copy.arrive()
    out[c, x] = jnp.sum(zy[...].reshape(16, 24, PAIR), axis=0)
    sent = [copies.start(out.at[c, x], out.at[c, x], to) for to in token_partners()]
    yield
    for copy in sent:
        copy.arrive()


def return_to_group(copies, ref, out):
    c, x = lax.axis_index("c"), lax.axis_index("x")
    t = c * 4 + x
    sent = []
    for to in token_partners():
        sent.append(copies.start(ref.at[to["c"] * 4 + to["x"]], out.at[t], to))
    out[t] = ref[t]
    yield
    for copy in sent:
        copy.arrive()


def turned(values, table, sign):
    turn, ahead, behind = table
    up = pltpu.roll(values, PAIR - ROT // 2, 1)
    down = pltpu.roll(values, ROT // 2, 1)
    if sign > 0:
        return values * turn + up * ahead + down * behind
    return values * turn - up * ahead - down * behind


def attend(meta, turn_ref, qkv, att, g, p):
    low, f32 = jnp.bfloat16, jnp.float32
    lane = lax.broadcasted_iota(jnp.int32, (BLOCK, PAIR), 1)
    first = lane < HEAD
    zero = jnp.zeros((BLOCK, PAIR), low)
    row_at = lax.broadcasted_iota(jnp.int32, (BLOCK, BLOCK), 0)
    col_at = lax.broadcasted_iota(jnp.int32, (BLOCK, BLOCK), 1)
    cols = [pl.ds(pl.multiple_of(i * 2 * PAIR + p * PAIR, PAIR), PAIR) for i in range(3)]
    d_k = [jnp.zeros((BLOCK, PAIR), f32) for _ in range(4)]
    d_v = [jnp.zeros((BLOCK, PAIR), f32) for _ in range(4)]
    for b in range(4):
        rows, width = pl.ds(b * BLOCK, BLOCK), (b + 1) * BLOCK
        keys = pl.ds(0, width)
        base = meta[:, 4 + b : 5 + b] * BLOCK
        diagonal = (col_at <= row_at) & (col_at.astype(f32) + base < meta[:, 8 + b : 9 + b])
        bias = [
            jnp.where(meta[:, e : e + 1] == meta[:, b : b + 1], 0.0, MASKED)
            + jnp.zeros((BLOCK, BLOCK), f32)
            for e in range(b)
        ]
        bias.append(jnp.where(diagonal, 0.0, MASKED).astype(f32))
        bias = bias[0] if b == 0 else jnp.concatenate(bias, axis=1)
        q, da = qkv[g, rows, cols[0]], att[g, rows, cols[0]]
        k, v = qkv[g, keys, cols[1]], qkv[g, keys, cols[2]]
        qs = [jnp.where(first, q, zero), jnp.where(first, zero, q)]
        das = [jnp.where(first, da, zero), jnp.where(first, zero, da)]
        atts, probs, dss = [], [], []
        for h in range(2):
            s = dot_t(qs[h], k) + bias
            w = jnp.exp(s - jnp.max(s, axis=1, keepdims=True))
            prob = w * (1.0 / jnp.sum(w, axis=1, keepdims=True))
            probs.append(prob.astype(low))
            atts.append(dot(probs[h], v))
            dp = dot_t(das[h], v)
            dss.append((prob * (dp - jnp.sum(prob * dp, axis=1, keepdims=True))).astype(low))
        att[g, rows, cols[0]] = jnp.where(first, atts[0], atts[1]).astype(low)
        dq = jnp.where(first, dot(dss[0], k), dot(dss[1], k)) * SCALE
        qkv[g, rows, cols[0]] = turned(dq, table_of(meta, turn_ref, b), -1).astype(low)
        dk = cross(jnp.concatenate(dss, axis=0), jnp.concatenate(qs, axis=0))
        dv = cross(jnp.concatenate(probs, axis=0), jnp.concatenate(das, axis=0))
        for e in range(b + 1):
            d_k[e] = d_k[e] + dk[e * BLOCK : (e + 1) * BLOCK]
            d_v[e] = d_v[e] + dv[e * BLOCK : (e + 1) * BLOCK]
    for b in range(4):
        rows = pl.ds(b * BLOCK, BLOCK)
        qkv[g, rows, cols[1]] = turned(d_k[b], table_of(meta, turn_ref, b), -1).astype(low)
        qkv[g, rows, cols[2]] = d_v[b].astype(low)


def table_of(meta, turn_ref, b):
    rank = meta[:, 4 + b : 5 + b]
    parts = [turn_ref[:, pl.ds(r * BLOCK, BLOCK), :] for r in range(3)]
    table = jnp.where((rank == 0.0)[None], parts[0], jnp.where((rank == 1.0)[None], parts[1], parts[2]))
    return table[0], table[1], table[2]


def layer_kernel(
    tokens_ref, cot_ref, seq_ref, length_ref, vec_ref, turn_ref, q_hbm, d_hbm, e_hbm, s_hbm,
    out_ref, ig_ref, ge_out, gq_out, gd_out, gs_out, vec_out,
    we, wq, wd, ws, normed, d_out, act, d_pre, qkv, att,
    ge, gq, gd, gs, stage, bias_e, vec_group, vec_all, vec_rows, we_send, wq_send, wd_own,
    wide_e, narrow_e, wide_d, narrow_d, wide_s, narrow_s,
    core_land, ring_land, res_e, res_q, res_d,
    vec_line, vec_sum, vec_part, vec_came, vec_mine, vec_zy,
    send, recv, local, core_free, ring_free, wide_free,
):
    low, f32 = jnp.bfloat16, jnp.float32
    z, y, c, x = (lax.axis_index(a) for a in ALL)
    t = c * 4 + x
    copies = Copies(send, recv)
    greet()

    loads = [
        pltpu.make_async_copy(q_hbm, stage.at[pl.ds(16, 16), pl.ds(0, 6144)], local.at[0]),
        pltpu.make_async_copy(d_hbm, stage.at[pl.ds(16, 16), pl.ds(6144, 2048)], local.at[1]),
        pltpu.make_async_copy(e_hbm, stage.at[pl.ds(0, 16)], local.at[2]),
    ]
    for k in range(4):
        rows = pl.ds(16 * k, 16)
        place = stage.at[pl.ds(32, 16), pl.ds(2048 * k, 2048)]
        loads.append(pltpu.make_async_copy(s_hbm.at[rows], place, local.at[3 + k]))
    for load in loads:
        load.start()

    lane = lax.broadcasted_iota(jnp.int32, (1, PAIR), 1)
    seqs = [seq_ref[0, b] for b in range(4)]
    own_meta = jnp.zeros((1, PAIR), f32)
    own_rank, own_limit = jnp.zeros((1, 1), f32), jnp.zeros((1, 1), f32)
    for b in range(4):
        rank = jnp.int32(0)
        for e in range(b):
            rank = rank + jnp.where(seqs[e] == seqs[b], 1, 0)
        limit = jnp.where(seqs[b] == 0, length_ref[0, 0], length_ref[0, 1])
        for at, value in ((b, seqs[b]), (4 + b, rank), (8 + b, limit)):
            own_meta = jnp.where(lane == at, value.astype(f32), own_meta)
        own_rank = jnp.where(x == b, rank.astype(f32), own_rank)
        own_limit = jnp.where(x == b, limit.astype(f32), own_limit)
    vec_line[...] = jnp.zeros_like(vec_line)
    vec_line[pl.ds(0, 1), pl.ds(0, 176)] = vec_ref[...].astype(low).astype(f32)
    line = pltpu.roll(vec_line[...], 16 * lax.rem(3 * t + 24 * (z * 4 + y), 8), 1)
    vec_own = vec_group.at[c, x]
    vec_own[...] = jnp.zeros((8, PAIR), f32)
    for k in range(3):
        vec_own[pl.ds(k, 1), :] = line[0:1, k * PAIR : (k + 1) * PAIR]
    vec_own[pl.ds(4, 1), :] = own_meta

    def d_out_rows(rows, first):
        row_at = lax.broadcasted_iota(jnp.int32, (16, 1), 0) + first
        live = (row_at.astype(f32) + own_rank * BLOCK < own_limit).astype(f32)
        return cot_ref[rows, :].astype(f32) * live

    def mask_chunk(r, _):
        rows = pl.ds(pl.multiple_of(r * 16, 16), 16)
        d_out[c, x, rows] = d_out_rows(rows, r * 16).astype(low)
        return 0

    normed[c, x] = tokens_ref[...]
    lax.fori_loop(0, 8, mask_chunk, 0)
    loads[0].wait()
    for k in range(8):
        for i in range(6):
            col = (i // 2) * 2048 + (1 - i % 2) * 1024 + k * PAIR
            piece = stage[pl.ds(16, 16), pl.ds(col, PAIR)]
            wq_send[k, :, pl.ds(i * PAIR, PAIR)] = piece.astype(low)
    loads[1].wait()
    wd_own[...] = stage[pl.ds(16, 16), pl.ds(6144, 2048)].astype(low)
    left16 = lax.broadcasted_iota(jnp.int32, (16, PAIR), 1) < HEAD
    loads[2].wait()
    for j in range(8):
        for k in range(4):
            first = stage[pl.ds(0, 16), pl.ds(j * 1024 + k * PAIR, PAIR)]
            second = stage[pl.ds(0, 16), pl.ds(j * 1024 + 512 + k * PAIR, PAIR)]
            even = jnp.where(left16, first, pltpu.roll(second, HEAD, 1))
            odd = jnp.where(left16, pltpu.roll(first, HEAD, 1), second)
            we_send[2 * k, :, pl.ds(j * PAIR, PAIR)] = even.astype(low)
            we_send[2 * k + 1, :, pl.ds(j * PAIR, PAIR)] = odd.astype(low)
    for k in range(4):
        loads[3 + k].wait()
        ws[z, y, pl.ds(16 * k, 16)] = stage[pl.ds(32, 16), pl.ds(2048 * k, 2048)].astype(low)
    enter()

    works, stages, tasks, finished = {}, {}, {}, set()
    token_sends = []

    def finish(*names):
        for name in names:
            for _ in works[name]:
                pass
            finished.add(name)

    def advance(name):
        if name not in works:
            works[name], stages[name] = begin(name), 0
        stages[name] += 1
        if next(works[name], 0) == 0:
            finished.add(name)

    def reach(name, stage):
        while stages[name] < stage:
            advance(name)

    def begin(name):
        if name == "vec":
            return gather_vectors(copies, vec_group, vec_rows, vec_all)
        if name == "to_q":
            return expand_to_group(copies, wq_send, wq, 768)
        if name == "to_e":
            return expand_to_group(copies, we_send, we, 1024)
        if name == "to_d":
            there = dense_partner()
            return landed(copies.start(wd_own, wd.at[there["z"], there["y"]], there))
        if name == "q":
            finish("to_q")
            return gather_weights(copies, by_rows(wq, 128))
        if name == "d":
            finish("to_d")
            return gather_weights(copies, by_columns(wd, 2048))
        if name == "e":
            finish("to_e")
            return gather_weights(copies, by_rows(we, 128))
        if name == "s":
            return gather_weights(copies, by_rows(ws, 64))
        if name == "cot":
            return gather_tokens(copies, d_out, [])
        if name == "tok":
            return gather_tokens(copies, normed, token_sends)
        if name == "sum_d":
            return scatter_weights(copies, by_columns(gd, 2048), wide_d, narrow_d, give_d)
        if name == "sum_q":
            return sum_q()
        if name in ("sum_e0", "sum_e1"):
            half = int(name[-1])
            cols = pl.ds(half * 512, 512)
            return scatter_weights(
                copies,
                by_rows(ge.at[:, :, :, cols], 128),
                wide_e.at[:, :, :, :, cols],
                narrow_e.at[:, :, :, cols],
                give_e(half),
            )
        if name in ("sum_s0", "sum_s1"):
            finish("sum_q")
            if "wide" not in finished:
                pl.semaphore_wait(wide_free, 4)
                finished.add("wide")
            half = int(name[-1])
            cols = pl.ds(half * 1024, 1024)
            return scatter_weights(
                copies,
                by_rows(gs.at[:, :, :, cols], 64),
                wide_s.at[:, :, :, :, cols],
                narrow_s.at[:, :, :, cols],
                give_s(half),
            )
        if name in ("n0", "n1", "o0", "o1"):
            half = int(name[-1])
            if name[0] == "o":
                finish("n" + name[1])
            cols = pl.ds(half * 1024, 1024)
            return scatter_tokens(
                copies,
                (normed if name[0] == "n" else d_out).at[:, :, :, cols],
                core_land.at[:, :, cols],
                ring_land.at[:, :, cols],
                (give_n if name[0] == "n" else give_o)(half),
                core_free.at[half],
                ring_free.at[half],
                name[0] == "n",
            )
        if name == "back_q":
            finish("sum_q")
            return return_to_group(copies, res_q, gq_out)
        if name == "back_e":
            finish("sum_e0", "sum_e1")
            return return_to_group(copies, res_e, ge_out)
        if name == "back_d":
            finish("sum_d")
            return landed(copies.start(res_d, gd_out, dense_partner()))
        return sum_vectors(copies, vec_part, vec_came, vec_mine, vec_zy, vec_out)

    def vec_task():
        finish("vec")
        for i in range(16):
            block = vec_all[i // 4, i % 4].astype(f32)
            vec_rows[pl.ds(11 * i, 11), :] = block[0:11]

    def norm_blocks(blocks):
        def chunk(r, _):
            rows = pl.ds(pl.multiple_of(r * 16, 16), 16)
            for core, chip in blocks:
                values = normed[core, chip, rows].astype(f32)
                center = values - jnp.mean(values, axis=1, keepdims=True)
                inverse = lax.rsqrt(jnp.mean(center * center, axis=1, keepdims=True) + NORM_EPS)
                own = center * inverse * row_of(vec_rows, 0, 16) + row_of(vec_rows, 16, 16)
                normed[core, chip, rows] = own.astype(low)
            return 0

        lax.fori_loop(0, 8, chunk, 0)

    def norm_own():
        reach("tok", 2)
        for copy in token_sends[0]:
            copy.leave()
        token_sends[0][2].arrive()
        norm_blocks([(c, x), (1 - c, x)])

    def norm_sides():
        reach("tok", 3)
        for copy in token_sends[1]:
            copy.leave()
        for copy in token_sends[1][2:]:
            copy.arrive()
        for way in (-1, 1):
            norm_blocks([(c, other("x", way)), (1 - c, other("x", way))])

    def norm_far():
        finish("tok")
        token_sends[2][0].leave()
        norm_blocks([(c, other("x", 2)), (1 - c, other("x", 2))])

    def qkv_tile(g, _):
        meta = vec_group[g, x, pl.ds(4, 1), :]
        projected = dot(normed[g].reshape(512, MODEL), wq[...].reshape(MODEL, 768))
        for p in range(6):
            bias = vec_rows[pl.ds(32 + (p // 2) * 16 + (1 - p % 2) * 8 + t, 1), :]
            for b in range(4):
                rows = pl.ds(b * BLOCK, BLOCK)
                part = projected[b * BLOCK : (b + 1) * BLOCK, p * PAIR : (p + 1) * PAIR] + bias
                if p < 4:
                    part = turned(part, table_of(meta, turn_ref, b), 1)
                part = part.astype(low)
                if p < 2:
                    part = part * jnp.asarray(SCALE, low)
                qkv[g, rows, pl.ds(p * PAIR, PAIR)] = part
        att[g] = dot_t(d_out[g].reshape(512, MODEL), wd[...].reshape(256, MODEL)).astype(low)
        return 0

    def qkv_task(g):
        def task():
            finish("tok", "cot", "q", "d")
            lax.fori_loop(g, g + 1, qkv_tile, 0)

        return task

    def attend_tile(i, _):
        g, p = i // 2, lax.rem(i, 2)
        attend(vec_group[g, x, pl.ds(4, 1), :], turn_ref, qkv, att, g, p)
        return 0

    def dense_tile(n, _):
        cols = pl.ds(pl.multiple_of(n * 1024, 1024), 1024)
        term = cross(att[...].reshape(1024, 256), d_out[:, :, :, cols].reshape(1024, 1024))
        gd[:, :, :, cols] = term.astype(low).reshape(4, 4, 16, 1024)
        return 0

    def give_d(part, total):
        res_d[:, pl.ds(part * 512, 512)] = total.astype(low)

    def qkv_grad_tile(i, _):
        mine = normed[:, :, :, pl.ds(pl.multiple_of(i * 512, 512), 512)].reshape(1024, 512)
        term = cross(mine, qkv[...].reshape(1024, 768)).astype(low).reshape(4, BLOCK, 768)
        gq[i, :, :, pl.ds(0, 768)] = term[:, :64]
        gq[i, :, :, pl.ds(768, 768)] = term[:, 64:]
        return 0

    def give_q(part, total):
        res_q[part] = total[:, :768].astype(low)
        res_q[4 + part] = total[:, 768:].astype(low)

    def sum_q():
        short = pl.ds(0, 1536)
        yield from scatter_weights(
            copies,
            by_rows(gq, 64),
            wide_s.at[:, :, :, :, short],
            narrow_s.at[:, :, :, short],
            give_q,
        )
        for axis in ("y", "z"):
            for way in (1, -1):
                to = {axis: other(axis, way)}
                pl.semaphore_signal(wide_free, inc=1, device_id=to, device_id_type=MESH)

    def up_tile(i, _):
        g, n = i // 2, lax.rem(i, 2)
        cols = pl.ds(pl.multiple_of(n * 512, 512), 512)
        pre_term = dot(normed[g].reshape(512, MODEL), we[:, :, :, cols].reshape(MODEL, 512))
        for k in range(8):
            stage[:, pl.ds(k * 512, 512)] = pre_term[k * 64 : k * 64 + 64]
        act_term = dot_t(d_out[g].reshape(512, MODEL), ws[pl.ds(2 * n, 2)].reshape(512, MODEL))
        for k in range(8):
            stage[:, pl.ds(4096 + k * 512, 512)] = act_term[k * 64 : k * 64 + 64]

        def chunk(r, _):
            rows = pl.ds(pl.multiple_of(r * 16, 16), 16)
            at = pl.ds(pl.multiple_of(lax.rem(r, 4) * 16, 16), 16)
            across = r // 4
            pre = stage[at, pl.ds(pl.multiple_of(across * 512, 512), 512)]
            pre = pre + bias_e[pl.ds(0, 1), cols]
            square = pre * pre
            inner = jnp.tanh(GELU_A * (pre + GELU_B * (square * pre)))
            cover = 0.5 + 0.5 * inner
            act[g, rows, cols] = (pre * cover).astype(low)
            slope = cover + 0.5 * pre * (1.0 - inner * inner) * (
                GELU_A + (3.0 * GELU_A * GELU_B) * square
            )
            d_act = stage[at, pl.ds(pl.multiple_of(4096 + across * 512, 512), 512)]
            d_pre[g, rows, cols] = (d_act * slope).astype(low)
            return 0

        lax.fori_loop(0, 32, chunk, 0)
        return 0

    def up_bias():
        odd = lax.rem(t, 2) == 1
        half = t // 2
        left = lane < HEAD
        bias_e[...] = jnp.zeros_like(bias_e)
        for j in range(8):
            r0 = vec_rows[pl.ds(96 + 8 * j + half, 1), :]
            r1 = vec_rows[pl.ds(100 + 8 * j + half, 1), :]
            even_row = jnp.where(left, r0, pltpu.roll(r1, HEAD, 1))
            odd_row = jnp.where(left, pltpu.roll(r0, HEAD, 1), r1)
            bias_e[pl.ds(0, 1), pl.ds(j * PAIR, PAIR)] = jnp.where(odd, odd_row, even_row)

    def up_task(i):
        def task():
            finish("e", "s")
            if i == 0:
                up_bias()
            lax.fori_loop(i, i + 1, up_tile, 0)

        return task

    def expand_tile(half):
        cols = pl.ds(half * 512, 512)

        def body(i, _):
            mine = normed[:, :, :, pl.ds(pl.multiple_of(i * 512, 512), 512)].reshape(1024, 512)
            term = cross(mine, d_pre[:, :, cols].reshape(1024, 512))
            ge[i, :, :, cols] = term.astype(low).reshape(4, BLOCK, 512)
            return 0

        return body

    def give_e(half):
        def give(part, total):
            cols = pl.ds(half * 512, 512)
            res_e[pl.ds(2 * part, 2), :, cols] = total.astype(low).reshape(2, 16, 512)

        return give

    def shrink_tile(half):
        cols = pl.ds(half * 1024, 1024)

        def body(j, _):
            mine = act[:, :, pl.ds(pl.multiple_of(j * 512, 512), 512)].reshape(1024, 512)
            term = cross(mine, d_out[:, :, :, cols].reshape(1024, 1024))
            gs[pl.ds(2 * j, 2), :, :, cols] = term.astype(low).reshape(2, 4, 64, 1024)
            return 0

        return body

    def give_s(half):
        def give(part, total):
            gs_out[pl.ds(part * 16, 16), pl.ds(half * 1024, 1024)] = total

        return give

    def down_tile(g):
        def body(i, _):
            cols = pl.ds(pl.multiple_of(i * 512, 512), 512)
            term = dot_t(qkv[g], wq[i].reshape(512, 768)) + dot_t(d_pre[g], we[i].reshape(512, 1024))
            normed[g, :, :, cols] = term.astype(low).reshape(4, BLOCK, 512)
            return 0

        return body

    def give_n(half):
        def give(high, r, total):
            at = pl.ds(pl.multiple_of(r * 16, 16), 16)
            stage[at, pl.ds(high * 2048 + half * 1024, 1024)] = total

        return give

    def out_tile(g):
        def body(i, _):
            cols = pl.ds(pl.multiple_of(i * 512, 512), 512)
            term = dot(att[g], wd[:, :, :, cols].reshape(256, 512)) + dot(
                act[g], ws[:, :, :, cols].reshape(1024, 512)
            )
            d_out[g, :, :, cols] = term.astype(low).reshape(4, BLOCK, 512)
            return 0

        return body

    def give_o(half):
        def give(high, r, total):
            rows = pl.ds(pl.multiple_of(high * 64 + r * 16, 16), 16)
            cols = pl.ds(half * 1024, 1024)
            add_bias = row_of(vec_rows, 80 + half * 8, 8) + row_of(vec_rows, 160 + half * 8, 8)
            out_ref[rows, cols] = (tokens_ref[rows, cols].astype(f32) + (total + add_bias)).astype(low)

        return give

    def norm_back():
        finish("n0", "n1")
        gain = row_of(vec_rows, 0, 16)
        vec_sum[...] = jnp.zeros_like(vec_sum)

        def chunk(r, _):
            rows = pl.ds(pl.multiple_of(r * 16, 16), 16)
            at = pl.ds(pl.multiple_of(lax.rem(r, 4) * 16, 16), 16)
            total = stage[at, pl.ds(pl.multiple_of((r // 4) * 2048, 2048), 2048)]
            mine = tokens_ref[rows, :].astype(f32)
            middle = mine - jnp.mean(mine, axis=1, keepdims=True)
            spread = lax.rsqrt(jnp.mean(middle * middle, axis=1, keepdims=True) + NORM_EPS)
            xhat = middle * spread
            e = total * gain
            mean_e = jnp.mean(e, axis=1, keepdims=True)
            mean_x = jnp.mean(e * xhat, axis=1, keepdims=True)
            dy = d_out_rows(rows, r * 16)
            ig_ref[rows, :] = (dy + spread * (e - mean_e - xhat * mean_x)).astype(low)
            for i, value in enumerate((total * xhat, total, dy)):
                vec_sum[i] += value[0:8] + value[8:16]
            return 0

        lax.fori_loop(0, 8, chunk, 0)
        vec_part[...] = jnp.zeros_like(vec_part)
        for i in range(3):
            total = jnp.sum(vec_sum[i], axis=0, keepdims=True)
            for k in range(8):
                vec_part[k, pl.ds(i, 1), :] = total[:, k * 256 : k * 256 + 256]

    def column_sums():
        ones = jnp.ones((8, 1024), low)
        vec_mine[...] = jnp.zeros_like(vec_mine)
        qkv_sum = dot(ones, qkv[...].reshape(1024, 768))
        for i in range(6):
            vec_mine[pl.ds(6 + i, 1), :] = qkv_sum[0:1, i * PAIR : (i + 1) * PAIR]
        pre_sum = dot(ones, d_pre[...].reshape(1024, 1024))
        for i in range(8):
            vec_mine[pl.ds(12 + i, 1), :] = pre_sum[0:1, i * PAIR : (i + 1) * PAIR]

    def loop(first, last, tile):
        return lambda: lax.fori_loop(first, last, tile, 0)

    tasks = {
        "vec_rows": vec_task, "norm_own": norm_own, "norm_sides": norm_sides, "norm_far": norm_far,
        "qkv0": qkv_task(0), "qkv1": qkv_task(1), "grad_d": loop(0, 2, dense_tile),
        "grad_q0": loop(0, 2, qkv_grad_tile), "grad_q1": loop(2, 4, qkv_grad_tile),
        "grad_e0": loop(0, 4, expand_tile(0)), "grad_e1": loop(0, 4, expand_tile(1)),
        "grad_s0": loop(0, 2, shrink_tile(0)), "grad_s1": loop(0, 2, shrink_tile(1)),
        "norm_back": norm_back, "col_sums": column_sums,
    }
    for i in range(4):
        tasks["att" + str(i)] = loop(i, i + 1, attend_tile)
        tasks["up" + str(i)] = up_task(i)
    for half in range(2):
        for name, tile in (("down", down_tile), ("out", out_tile)):
            for at, g in (("a", 1 - c), ("b", c)):
                tasks[name + at + str(half)] = loop(2 * half, 2 * half + 2, tile(g))

    for name in SCHEDULE:
        if name in tasks:
            tasks[name]()
        else:
            advance(name)
    finish(*works)
    copies.finish()


def layer(tokens, cotangent, block_seq, seq_lengths, vectors, weights):
    low, f32 = jnp.bfloat16, jnp.float32
    vmem = pl.BlockSpec(memory_space=pltpu.VMEM)
    smem = pl.BlockSpec(memory_space=pltpu.SMEM)
    anywhere = pl.BlockSpec(memory_space=pl.ANY)
    turn = jnp.asarray(np.stack(rotary_constants())[:, : 3 * BLOCK])
    outs = [
        ((BLOCK, MODEL), low), ((BLOCK, MODEL), low), ((8, 16, 1024), low), ((8, 16, 768), low),
        ((16, MODEL), low), ((64, MODEL), f32), ((2, 4, 24, PAIR), f32),
    ]
    held = [
        ((4, 4, 128, 1024), low), ((4, 4, 128, 768), low), ((4, 4, 16, 2048), low),
        ((4, 4, 64, 2048), low), ((2, 4, 128, 2048), low), ((2, 4, 128, 2048), low),
        ((2, 512, 1024), low), ((2, 512, 1024), low), ((2, 512, 768), low), ((2, 512, 256), low),
        ((4, 4, 128, 1024), low), ((4, 4, 64, 1536), low), ((4, 4, 16, 2048), low),
        ((4, 4, 64, 2048), low), ((64, 8192), f32), ((8, 1024), f32),
        ((2, 4, 8, 128), f32), ((4, 4, 16, 128), low), ((184, 128), f32),
        ((8, 16, 1024), low), ((8, 16, 768), low), ((16, 2048), low),
        ((2, 6, 4, 32, 1024), low), ((2, 6, 32, 1024), low),
        ((2, 6, 4, 16, 512), low), ((2, 6, 16, 512), low),
        ((2, 6, 4, 16, 2048), low), ((2, 6, 16, 2048), low),
        ((4, 128, 2048), low), ((6, 64, 2048), low),
        ((8, 16, 1024), low), ((8, 16, 768), low), ((16, 2048), low), ((8, 384), f32),
        ((3, 8, MODEL), f32), ((8, 8, 256), f32), ((8, 8, 256), f32), ((24, 128), f32),
        ((4, 4, 24, 128), f32),
    ]
    return pl.pallas_call(
        layer_kernel,
        in_specs=[vmem, vmem, smem, smem, vmem, vmem] + [anywhere] * 4,
        out_specs=[vmem] * 7,
        out_shape=[jax.ShapeDtypeStruct(s, k) for s, k in outs],
        scratch_shapes=[pltpu.VMEM(s, k) for s, k in held]
        + [
            pltpu.SemaphoreType.DMA((COPIES,)),
            pltpu.SemaphoreType.DMA((COPIES,)),
            pltpu.SemaphoreType.DMA((7,)),
            pltpu.SemaphoreType.REGULAR((2,)),
            pltpu.SemaphoreType.REGULAR((2,)),
            pltpu.SemaphoreType.REGULAR,
        ],
        compiler_params=pltpu.CompilerParams(
            collective_id=0, has_side_effects=True, vmem_limit_bytes=64 * 2**20
        ),
        name="layer",
    )(tokens, cotangent, block_seq, seq_lengths, vectors[None, :], turn, *weights)


def update_kernel(out_in, ig_in, ge, gq, gd, gs, vec, *refs):
    f32 = jnp.float32
    masters, moments, seconds = refs[0:5], refs[5:10], refs[10:15]
    out_ref, ig_ref = refs[15:17]
    results = [refs[17 + 3 * i : 20 + 3 * i] for i in range(5)]
    flat = refs[32]
    out_ref[...] = out_in[...]
    ig_ref[...] = ig_in[...]

    def update(i, at, gradient):
        grad_ref, state_ref, new_ref = results[i]
        grad_ref[at] = gradient
        state, new = adam_step(
            masters[i][at], moments[i][at], seconds[i][at], gradient, RATES[i], DECAYS[i]
        )
        state_ref[at] = state
        new_ref[at] = new

    every = slice(None)
    for s in range(3):
        for hi in range(2):
            for t in range(TPN):
                col = s * MODEL + hi * 1024 + t * PAIR
                piece = gq[t, :, pl.ds((2 * s + 1 - hi) * PAIR, PAIR)].astype(f32)
                update(0, (every, pl.ds(col, PAIR)), piece)
    for k in range(16):
        cols = (every, pl.ds(k * PAIR, PAIR))
        update(1, cols, gd[cols].astype(f32))
        for r in range(4):
            at = (pl.ds(16 * r, 16), pl.ds(k * PAIR, PAIR))
            update(3, at, gs[at])
    left = lax.broadcasted_iota(jnp.int32, (16, PAIR), 1) < HEAD
    for j in range(16):
        for k in range(4):
            first = ge[2 * k, :, pl.ds((j // 2) * PAIR, PAIR)].astype(f32)
            second = ge[2 * k + 1, :, pl.ds((j // 2) * PAIR, PAIR)].astype(f32)
            if j % 2 == 0:
                second = pltpu.roll(second, HEAD, 1)
            else:
                first = pltpu.roll(first, HEAD, 1)
            update(2, (every, pl.ds(j * 512 + k * PAIR, PAIR)), jnp.where(left, first, second))

    flat[...] = jnp.zeros_like(flat)
    left = lax.broadcasted_iota(jnp.int32, (1, PAIR), 1) < HEAD

    def line(t, row):
        return vec[t // 4, t % 4, pl.ds(row, 1), :]

    for t in range(TPN):
        for i in range(2):
            for row, base in ((0, 0), (1, 16), (2, 80), (2, 160)):
                flat[pl.ds(base + 2 * t + i, 1), :] = line(t, 2 * row + i)
        for s in range(3):
            for hi in range(2):
                at = 32 + s * 16 + hi * 8 + t
                flat[pl.ds(at, 1), :] = line(t, 6 + 2 * s + 1 - hi)
    for j in range(16):
        for k in range(4):
            first = line(2 * k, 12 + j // 2)
            second = line(2 * k + 1, 12 + j // 2)
            if j % 2 == 0:
                second = pltpu.roll(second, HEAD, 1)
            else:
                first = pltpu.roll(first, HEAD, 1)
            flat[pl.ds(96 + 4 * j + k, 1), :] = jnp.where(left, first, second)
    z, y, c, x = (lax.axis_index(a) for a in ALL)
    number = ((z * 4 + y) * 2 + c) * 4 + x
    first = (176 * number) // 128
    own = jnp.concatenate([flat[pl.ds(first + i, 1), :] for i in range(3)], axis=1)
    own = jnp.broadcast_to(own, (8, 3 * PAIR))
    own = pltpu.roll(own, lax.rem(3 * PAIR - 16 * lax.rem(3 * number, 8), 3 * PAIR), 1)
    update(4, (every, every), own[0:1, 0:176])


def update_all(parts, masters, moments, seconds):
    f32 = jnp.float32
    vmem = pl.BlockSpec(memory_space=pltpu.VMEM)
    shapes = [jax.ShapeDtypeStruct(p.shape, p.dtype) for p in parts[:2]]
    for w in masters:
        shapes += [jax.ShapeDtypeStruct(w.shape, f32)] * 3
    return pl.pallas_call(
        update_kernel,
        in_specs=[vmem] * 22,
        out_specs=[vmem] * 17,
        out_shape=shapes,
        scratch_shapes=[pltpu.VMEM((184, PAIR), f32)],
        compiler_params=pltpu.CompilerParams(vmem_limit_bytes=62 * 2**20),
        name="update",
    )(*parts, *masters, *moments, *seconds)


def adam_step(weight, moment, second, gradient, step_rate, step_decay):
    moment_new = BETA_ONE * moment + (1 - BETA_ONE) * gradient
    second_new = BETA_TWO * second + (1 - BETA_TWO) * gradient * gradient
    moment_hat = moment_new / (1 - BETA_ONE**STEP)
    second_hat = second_new / (1 - BETA_TWO**STEP)
    updated = weight - step_rate * (
        moment_hat / (jnp.sqrt(second_hat) + ADAM_EPS) + step_decay * weight
    )
    return (second_new, updated)


def shards(
    tokens, cotangent, block_seq, seq_lengths,
    qkv_weight, qkv_moment, qkv_second,
    dense_weight, dense_moment, dense_second,
    expand_weight, expand_moment, expand_second,
    shrink_weight, shrink_moment, shrink_second,
    vectors, vec_moment, vec_second,
):
    parts = layer(
        tokens,
        cotangent,
        block_seq,
        seq_lengths,
        vectors,
        (qkv_weight, dense_weight, expand_weight, shrink_weight),
    )
    masters = (qkv_weight, dense_weight, expand_weight, shrink_weight, vectors[None, :])
    moments = (qkv_moment, dense_moment, expand_moment, shrink_moment, vec_moment[None, :])
    seconds = (qkv_second, dense_second, expand_second, shrink_second, vec_second[None, :])
    results = update_all(parts, masters, moments, seconds)
    return (*results[:14], *(r[0] for r in results[14:]))


def solution(mesh):
    finer = Mesh(mesh.devices.reshape(*SIZES), ALL)
    whole, group = P(ALL, None), P(DP, None)
    return jax.shard_map(
        shards,
        mesh=finer,
        in_specs=(whole, whole, group, group, *[whole] * 12, *[P(ALL)] * 3),
        out_specs=(*[whole] * 14, *[P(ALL)] * 3),
        check_vma=False,
    )
```

```python
import functools

import jax
import jax.numpy as jnp
import numpy as np
from jax import lax
from jax.experimental import pallas as pl
from jax.experimental.pallas import tpu as pltpu
from jax.sharding import Mesh
from jax.sharding import PartitionSpec as P

HEAD = 64
ROT = 32
BLOCK = 128
STEP = 10
GROUP = 512
MODEL = 2048
FF = 8192
PAIR = 2 * HEAD
ALL = ("z", "y", "c", "x")
DP = ("z", "y", "c")
ZY = ("z", "y")
TP = ("c", "x")
SIZES = (4, 4, 2, 4)
TPN = 8
COPIES = 480
SCHEDULE = (
    "to_q", "vec", "s", "to_d", "tok", "d", "q", "to_e", "cot", "vec_rows", "q", "q", "tok",
    "q", "q", "e", "cot", "norm_own", "s", "norm_sides", "cot", "norm_far", "s", "qkv0", "e",
    "att0", "qkv1", "s", "att1", "e", "att2", "e", "att3", "s", "grad_q0", "e", "grad_q1",
    "grad_d", "sum_q", "up0", "up1", "sum_d", "up2", "sum_q", "up3", "grad_e0", "sum_q",
    "sum_e0", "grad_e1", "downa1", "n1", "downb1", "sum_q", "sum_e1", "grad_s0", "n1",
    "grad_s1", "sum_e0", "back_q", "downa0", "n0", "sum_s0", "downb0", "n0", "sum_s1", "outa0",
    "sum_e1", "o0", "sum_d", "outa1", "o1", "n1", "outb1", "n0", "outb0", "o0", "sum_s1",
    "sum_d", "sum_e1", "sum_e0", "o1", "norm_back", "col_sums", "sum_s0", "vec_back", "sum_d",
    "sum_e1", "back_d", "sum_e0", "o0", "sum_s1", "vec_back", "o1", "back_e", "sum_s0",
    "sum_s0", "sum_s1", "vec_back",
)
SCALE = HEAD ** (-0.5)

NORM_EPS = 1e-05
MASKED = -1e30
BETA_ONE = 0.9
BETA_TWO = 0.999
ADAM_EPS = 1e-08
RATES = (0.02, 0.1, 0.02, 0.01, 0.4)
DECAYS = (0.1, 0.1, 0.1, 0.1, 0.0)
GELU_A = float(np.sqrt(2.0 / np.pi))
GELU_B = 0.044715


def dot(a, b):
    return jnp.dot(a, b, preferred_element_type=jnp.float32)


def dot_t(a, b):
    return lax.dot_general(a, b, (((1,), (1,)), ((), ())), preferred_element_type=jnp.float32)


def cross(a, b):
    return lax.dot_general(a, b, (((0,), (0,)), ((), ())), preferred_element_type=jnp.float32)


def rotary_constants():
    half = np.arange(ROT // 2, dtype=np.float32)
    inverse = (10000.0 ** (-2.0 * half.astype(np.float64) / ROT)).astype(np.float32)
    angle = (np.arange(GROUP, dtype=np.float32)[:, None] * inverse[None, :]).astype(np.float64)
    cosine, sine = np.cos(angle).astype(np.float32), np.sin(angle).astype(np.float32)
    one = np.ones((GROUP, HEAD - ROT), np.float32)
    zero = np.zeros((GROUP, ROT // 2), np.float32)
    rest = np.zeros((GROUP, HEAD - ROT), np.float32)
    turn = np.concatenate([cosine, cosine, one], axis=1)
    ahead = np.concatenate([-sine, zero, rest], axis=1)
    behind = np.concatenate([zero, sine, rest], axis=1)
    return tuple(np.concatenate([a, a], axis=1) for a in (turn, ahead, behind))


MESH = pl.DeviceIdType.MESH


def other(axis, step):
    size = SIZES[ALL.index(axis)]
    return lax.rem(lax.axis_index(axis) + step + size, size)


class Copy:
    def __init__(self, copy):
        self.copy, self.here, self.gone = copy, False, False

    def arrive(self):
        if not self.here:
            self.copy.wait_recv()
        self.here = True

    def leave(self):
        if not self.gone:
            self.copy.wait_send()
        self.gone = True


class Copies:
    def __init__(self, send, recv):
        self.send, self.recv, self.all = send, recv, []

    def start(self, src, dst, to):
        at = len(self.all)
        copy = pltpu.make_async_remote_copy(
            src_ref=src,
            dst_ref=dst,
            send_sem=self.send.at[at],
            recv_sem=self.recv.at[at],
            device_id=to,
            device_id_type=MESH,
        )
        copy.start()
        self.all.append(Copy(copy))
        return self.all[-1]

    def finish(self):
        for copy in self.all:
            copy.leave()


def greet():
    barrier = pltpu.get_barrier_semaphore()
    for partner in token_partners() + weight_partners() + [dense_partner()]:
        pl.semaphore_signal(barrier, inc=1, device_id=partner, device_id_type=MESH)


def enter():
    pl.semaphore_wait(pltpu.get_barrier_semaphore(), 23)


def token_partners():
    return [{"c": other("c", i), "x": other("x", j)} for i in range(2) for j in range(4) if i + j]


def weight_partners():
    return [{"z": other("z", i), "y": other("y", j)} for i in range(4) for j in range(4) if i + j]


def dense_partner():
    z, y, c, x = (lax.axis_index(a) for a in ALL)
    return {"z": (1 - z // 2) * 2 + c, "y": x, "c": lax.rem(z, 2), "x": y}


def gather_weights(copies, view):
    z, y = lax.axis_index("z"), lax.axis_index("y")
    z_up, z_down, y_up, y_down = other("z", 1), other("z", -1), other("y", 1), other("y", -1)
    z_far, y_far = other("z", 2), other("y", 2)
    up, down, far, near = {"y": y_up}, {"y": y_down}, {"z": z_up}, {"z": z_down}

    def go(block, to):
        return copies.start(block, block, to)

    a_up, a_down = go(view(z, y, 4), up), go(view(z, y, 4), down)
    b_up, b_down = go(view(z, y, 5), far), go(view(z, y, 5), near)
    a_own = go(view(z, y, 4), far), go(view(z, y, 4), near)
    b_own = go(view(z, y, 5), up), go(view(z, y, 5), down)
    yield
    a_up.arrive()
    a_low = go(view(z, y_down, 0), up)
    b_up.arrive()
    b_low = go(view(z_down, y, 2), far)
    a_down.arrive()
    a_high = go(view(z, y_up, 1), down)
    b_down.arrive()
    b_high = go(view(z_up, y, 3), near)
    a_side = [(i, go(view(z, i, 4), far), go(view(z, i, 4), near)) for i in (y_down, y_up)]
    b_side = [(i, go(view(i, y, 5), up), go(view(i, y, 5), down)) for i in (z_down, z_up)]
    yield
    last = []
    a_own[0].arrive()
    last.append(go(view(z_down, y, 0), far))
    b_own[0].arrive()
    last.append(go(view(z, y_down, 2), up))
    a_own[1].arrive()
    last.append(go(view(z_up, y, 1), near))
    b_own[1].arrive()
    last.append(go(view(z, y_up, 3), down))
    a_low.arrive()
    a_high.arrive()
    a_side.append((y_far, go(view(z, y_far, 4), far), go(view(z, y_far, 4), near)))
    b_low.arrive()
    b_high.arrive()
    b_side.append((z_far, go(view(z_far, y, 5), up), go(view(z_far, y, 5), down)))
    for k in range(3):
        if k != 1:
            yield
        i, first, second = a_side[k]
        first.arrive()
        last.append(go(view(z_down, i, 0), far))
        second.arrive()
        last.append(go(view(z_up, i, 1), near))
        i, first, second = b_side[k]
        first.arrive()
        last.append(go(view(i, y_down, 2), up))
        second.arrive()
        last.append(go(view(i, y_up, 3), down))
    yield
    for copy in last:
        copy.arrive()


def gather_tokens(copies, ref, sent):
    c, x, across = lax.axis_index("c"), lax.axis_index("x"), other("c", 1)
    right, left = {"x": other("x", 1)}, {"x": other("x", -1)}

    def go(block, to):
        return copies.start(block, block, to)

    own = ref.at[c, x]
    sent.append([go(own, right), go(own, left), go(own, {"c": across})])
    yield
    sent[0][0].arrive()
    last = [go(ref.at[c, other("x", -1), pl.ds(0, 64)], right)]
    side = [go(ref.at[c, other("x", -1)], {"c": across})]
    sent[0][1].arrive()
    last.append(go(ref.at[c, other("x", 1), pl.ds(64, 64)], left))
    side.append(go(ref.at[c, other("x", 1)], {"c": across}))
    sent.append(last + side)
    yield
    for copy in last:
        copy.arrive()
    sent.append([go(ref.at[c, other("x", 2)], {"c": across})])
    yield
    for copies_of_stage in sent:
        for copy in copies_of_stage:
            copy.arrive()
            copy.leave()


def gather_vectors(copies, group, rows, place):
    c, x = lax.axis_index("c"), lax.axis_index("x")
    sent = [copies.start(group.at[c, x], group.at[c, x], to) for to in token_partners()]
    yield
    for copy in sent:
        copy.arrive()
    rows[pl.ds(0, 16), :] = jnp.zeros((16, PAIR), jnp.float32)
    for d in range(TPN):
        rows[pl.ds((176 * d) // PAIR, 3), :] += group[d // 4, d % 4, pl.ds(0, 3), :]
    place[:, pl.ds(0, PAIR)] = rows[pl.ds(0, 16), :].astype(jnp.bfloat16)
    place[:, pl.ds(PAIR, 3 * PAIR)] = jnp.zeros((16, 3 * PAIR), jnp.bfloat16)


def expand_to_group(copies, send, ref, width):
    z, y, c, x = (lax.axis_index(a) for a in ALL)
    rows = pl.ds(pl.multiple_of((c * 4 + x) * 16, 16), 16)
    sent = []
    for to in token_partners():
        sent.append(copies.start(send.at[to["c"] * 4 + to["x"]], ref.at[z, y, rows], to))
    ref[z, y, rows] = send[c * 4 + x]
    yield
    for copy in sent:
        copy.arrive()


def by_rows(ref, rows):
    quarter = rows // 4

    def view(z, y, part):
        start, size = (part * quarter, quarter) if part < 4 else ((part - 4) * 2 * quarter, 2 * quarter)
        return ref.at[z, y, pl.ds(start, size)]

    return view


def by_columns(ref, columns):
    quarter = columns // 4

    def view(z, y, part):
        start, size = (part * quarter, quarter) if part < 4 else ((part - 4) * 2 * quarter, 2 * quarter)
        return ref.at[z, y, :, pl.ds(start, size)]

    return view


def step(*works):
    for work in works:
        next(work, None)


def row_of(ref, first, count):
    return jnp.concatenate([ref[pl.ds(first + i, 1), :] for i in range(count)], axis=1)


def ring_sum(copies, axis, block, land, low_part, high_part):
    ahead, behind = other(axis, 1), other(axis, -1)
    up, down = {axis: ahead}, {axis: behind}
    far = other(axis, 2)
    t_low = copies.start(block(far, low_part), land.at[0], up)
    t_high = copies.start(block(far, high_part), land.at[1], down)
    d_high = copies.start(block(ahead, high_part), land.at[3], up)
    d_low = copies.start(block(behind, low_part), land.at[2], down)
    yield
    t_low.arrive()
    land[0] = land[0] + block(ahead, low_part)[...]
    p_low = copies.start(land.at[0], land.at[4], up)
    t_high.arrive()
    land[1] = land[1] + block(behind, high_part)[...]
    p_high = copies.start(land.at[1], land.at[5], down)
    yield
    for copy in (d_low, d_high, p_low, p_high):
        copy.arrive()
    for copy in (t_low, t_high, d_low, d_high, p_low, p_high):
        copy.leave()


def three(own, land, high, at=...):
    f32 = jnp.float32
    first, second = land.at[4 + high], land.at[2 + high]
    return own[at].astype(f32) + first[at].astype(f32) + second[at].astype(f32)


def both(first, second):
    while True:
        done = [next(first, 0), next(second, 0)]
        if 0 in done:
            return
        yield


def scatter_weights(copies, view, wide, narrow, give):
    z, y = lax.axis_index("z"), lax.axis_index("y")
    every = slice(None)
    low = jnp.bfloat16
    yield from both(
        ring_sum(copies, "y", lambda i, p: view(every, i, p), wide.at[0], 0, 1),
        ring_sum(copies, "z", lambda i, p: view(i, every, p), wide.at[1], 2, 3),
    )
    for high in range(2):
        own = view(every, y, high)
        for i in range(4):
            own[i] = three(own, wide.at[0], high, i).astype(low)
        own = view(z, every, 2 + high)
        for i in range(4):
            own[i] = three(own, wide.at[1], high, i).astype(low)
    yield from both(
        ring_sum(copies, "z", lambda i, p: view(i, y, p), narrow.at[0], 0, 1),
        ring_sum(copies, "y", lambda i, p: view(z, i, p), narrow.at[1], 2, 3),
    )
    for high in range(2):
        give(high, three(view(z, y, high), narrow.at[0], high))
        give(2 + high, three(view(z, y, 2 + high), narrow.at[1], high))


def scatter_tokens(copies, ref, core_land, land, give, core_free, ring_free, first):
    c, x, across = lax.axis_index("c"), lax.axis_index("x"), other("c", 1)
    if not first:
        pl.semaphore_wait(core_free, 1)
    came = copies.start(ref.at[across], core_land, {"c": across})
    yield
    came.arrive()
    for i in range(4):
        ref[c, i] = ref[c, i] + core_land[i]
    if first:
        pl.semaphore_signal(core_free, inc=1, device_id={"c": across}, device_id_type=MESH)
    else:
        pl.semaphore_wait(ring_free, 2)
    yield from ring_sum(copies, "x", lambda i, p: ref.at[c, i, pl.ds(p * 64, 64)], land, 0, 1)
    for high in range(2):
        own = ref.at[c, x, pl.ds(high * 64, 64)]

        def chunk(r, _):
            rows = pl.ds(pl.multiple_of(r * 16, 16), 16)
            give(high, r, three(own, land, high, rows))
            return 0

        lax.fori_loop(0, 4, chunk, 0)
    if first:
        for way in (1, -1):
            to = {"x": other("x", way)}
            pl.semaphore_signal(ring_free, inc=1, device_id=to, device_id_type=MESH)


def landed(copy):
    yield
    copy.arrive()


def sum_vectors(copies, part, came, mine, zy, out):
    z, y, c, x = (lax.axis_index(a) for a in ALL)
    t = c * 4 + x
    sent = [
        copies.start(part.at[to["c"] * 4 + to["x"]], came.at[t], to) for to in token_partners()
    ]
    came[t] = part[t]
    yield
    for copy in sent:
        copy.arrive()
    total = jnp.sum(came[...], axis=0)
    for i in range(6):
        mine[pl.ds(i, 1), :] = total[i // 2 : i // 2 + 1, (i % 2) * PAIR : (i % 2 + 1) * PAIR]
    zy[z, y] = mine[...]
    sent = [copies.start(mine, zy.at[z, y], to) for to in weight_partners()]
    yield
    for copy in sent:
        copy.arrive()
    out[c, x] = jnp.sum(zy[...].reshape(16, 24, PAIR), axis=0)
    sent = [copies.start(out.at[c, x], out.at[c, x], to) for to in token_partners()]
    yield
    for copy in sent:
        copy.arrive()


def return_to_group(copies, ref, out):
    c, x = lax.axis_index("c"), lax.axis_index("x")
    t = c * 4 + x
    sent = []
    for to in token_partners():
        sent.append(copies.start(ref.at[to["c"] * 4 + to["x"]], out.at[t], to))
    out[t] = ref[t]
    yield
    for copy in sent:
        copy.arrive()


def turned(values, table, sign):
    turn, ahead, behind = table
    up = pltpu.roll(values, PAIR - ROT // 2, 1)
    down = pltpu.roll(values, ROT // 2, 1)
    if sign > 0:
        return values * turn + up * ahead + down * behind
    return values * turn - up * ahead - down * behind


def attend(meta, turn_ref, qkv, att, g, p):
    low, f32 = jnp.bfloat16, jnp.float32
    lane = lax.broadcasted_iota(jnp.int32, (BLOCK, PAIR), 1)
    first = lane < HEAD
    zero = jnp.zeros((BLOCK, PAIR), low)
    row_at = lax.broadcasted_iota(jnp.int32, (BLOCK, BLOCK), 0)
    col_at = lax.broadcasted_iota(jnp.int32, (BLOCK, BLOCK), 1)
    cols = [pl.ds(pl.multiple_of(i * 2 * PAIR + p * PAIR, PAIR), PAIR) for i in range(3)]
    d_k = [jnp.zeros((BLOCK, PAIR), f32) for _ in range(4)]
    d_v = [jnp.zeros((BLOCK, PAIR), f32) for _ in range(4)]
    for b in range(4):
        rows, width = pl.ds(b * BLOCK, BLOCK), (b + 1) * BLOCK
        keys = pl.ds(0, width)
        base = meta[:, 4 + b : 5 + b] * BLOCK
        diagonal = (col_at <= row_at) & (col_at.astype(f32) + base < meta[:, 8 + b : 9 + b])
        bias = [
            jnp.where(meta[:, e : e + 1] == meta[:, b : b + 1], 0.0, MASKED)
            + jnp.zeros((BLOCK, BLOCK), f32)
            for e in range(b)
        ]
        bias.append(jnp.where(diagonal, 0.0, MASKED).astype(f32))
        bias = bias[0] if b == 0 else jnp.concatenate(bias, axis=1)
        q, da = qkv[g, rows, cols[0]], att[g, rows, cols[0]]
        k, v = qkv[g, keys, cols[1]], qkv[g, keys, cols[2]]
        qs = [jnp.where(first, q, zero), jnp.where(first, zero, q)]
        das = [jnp.where(first, da, zero), jnp.where(first, zero, da)]
        atts, probs, dss = [], [], []
        for h in range(2):
            s = dot_t(qs[h], k) + bias
            w = jnp.exp(s - jnp.max(s, axis=1, keepdims=True))
            prob = w * (1.0 / jnp.sum(w, axis=1, keepdims=True))
            probs.append(prob.astype(low))
            atts.append(dot(probs[h], v))
            dp = dot_t(das[h], v)
            dss.append((prob * (dp - jnp.sum(prob * dp, axis=1, keepdims=True))).astype(low))
        att[g, rows, cols[0]] = jnp.where(first, atts[0], atts[1]).astype(low)
        dq = jnp.where(first, dot(dss[0], k), dot(dss[1], k)) * SCALE
        qkv[g, rows, cols[0]] = turned(dq, table_of(meta, turn_ref, b), -1).astype(low)
        dk = cross(jnp.concatenate(dss, axis=0), jnp.concatenate(qs, axis=0))
        dv = cross(jnp.concatenate(probs, axis=0), jnp.concatenate(das, axis=0))
        for e in range(b + 1):
            d_k[e] = d_k[e] + dk[e * BLOCK : (e + 1) * BLOCK]
            d_v[e] = d_v[e] + dv[e * BLOCK : (e + 1) * BLOCK]
    for b in range(4):
        rows = pl.ds(b * BLOCK, BLOCK)
        qkv[g, rows, cols[1]] = turned(d_k[b], table_of(meta, turn_ref, b), -1).astype(low)
        qkv[g, rows, cols[2]] = d_v[b].astype(low)


def table_of(meta, turn_ref, b):
    rank = meta[:, 4 + b : 5 + b]
    parts = [turn_ref[:, pl.ds(r * BLOCK, BLOCK), :] for r in range(3)]
    table = jnp.where((rank == 0.0)[None], parts[0], jnp.where((rank == 1.0)[None], parts[1], parts[2]))
    return table[0], table[1], table[2]


def layer_kernel(
    tokens_ref, cot_ref, seq_ref, length_ref, vec_ref, turn_ref, q_hbm, d_hbm, e_hbm, s_hbm,
    out_ref, ig_ref, ge_out, gq_out, gd_out, gs_out, vec_out,
    we, wq, wd, ws, normed, d_out, act, d_pre, qkv, att,
    ge, gq, gd, gs, stage, bias_e, vec_group, vec_rows, we_send, wq_send, wd_own,
    wide_e, narrow_e, wide_d, narrow_d, wide_s, narrow_s,
    core_land, ring_land, res_e, res_q, res_d,
    vec_line, vec_sum, vec_part, vec_came, vec_mine, vec_zy,
    send, recv, local, core_free, ring_free, wide_free,
):
    low, f32 = jnp.bfloat16, jnp.float32
    z, y, c, x = (lax.axis_index(a) for a in ALL)
    t = c * 4 + x
    copies = Copies(send, recv)
    greet()

    loads = [
        pltpu.make_async_copy(q_hbm, stage.at[pl.ds(16, 16), pl.ds(0, 6144)], local.at[0]),
        pltpu.make_async_copy(d_hbm, stage.at[pl.ds(16, 16), pl.ds(6144, 2048)], local.at[1]),
        pltpu.make_async_copy(e_hbm, stage.at[pl.ds(0, 16)], local.at[2]),
    ]
    for k in range(4):
        rows = pl.ds(16 * k, 16)
        place = stage.at[pl.ds(32, 16), pl.ds(2048 * k, 2048)]
        loads.append(pltpu.make_async_copy(s_hbm.at[rows], place, local.at[3 + k]))
    for load in loads:
        load.start()

    lane = lax.broadcasted_iota(jnp.int32, (1, PAIR), 1)
    seqs = [seq_ref[0, b] for b in range(4)]
    own_meta = jnp.zeros((1, PAIR), f32)
    own_rank, own_limit = jnp.zeros((1, 1), f32), jnp.zeros((1, 1), f32)
    for b in range(4):
        rank = jnp.int32(0)
        for e in range(b):
            rank = rank + jnp.where(seqs[e] == seqs[b], 1, 0)
        limit = jnp.where(seqs[b] == 0, length_ref[0, 0], length_ref[0, 1])
        for at, value in ((b, seqs[b]), (4 + b, rank), (8 + b, limit)):
            own_meta = jnp.where(lane == at, value.astype(f32), own_meta)
        own_rank = jnp.where(x == b, rank.astype(f32), own_rank)
        own_limit = jnp.where(x == b, limit.astype(f32), own_limit)
    vec_line[...] = jnp.zeros_like(vec_line)
    vec_line[pl.ds(0, 1), pl.ds(0, 176)] = vec_ref[...].astype(low).astype(f32)
    line = pltpu.roll(vec_line[...], 16 * lax.rem(3 * t + 24 * (z * 4 + y), 8), 1)
    vec_own = vec_group.at[c, x]
    vec_own[...] = jnp.zeros((8, PAIR), f32)
    for k in range(3):
        vec_own[pl.ds(k, 1), :] = line[0:1, k * PAIR : (k + 1) * PAIR]
    vec_own[pl.ds(4, 1), :] = own_meta

    def d_out_rows(rows, first):
        row_at = lax.broadcasted_iota(jnp.int32, (16, 1), 0) + first
        live = (row_at.astype(f32) + own_rank * BLOCK < own_limit).astype(f32)
        return cot_ref[rows, :].astype(f32) * live

    def mask_chunk(r, _):
        rows = pl.ds(pl.multiple_of(r * 16, 16), 16)
        d_out[c, x, rows] = d_out_rows(rows, r * 16).astype(low)
        return 0

    normed[c, x] = tokens_ref[...]
    lax.fori_loop(0, 8, mask_chunk, 0)
    loads[0].wait()
    for k in range(8):
        for i in range(6):
            col = (i // 2) * 2048 + (1 - i % 2) * 1024 + k * PAIR
            piece = stage[pl.ds(16, 16), pl.ds(col, PAIR)]
            wq_send[k, :, pl.ds(i * PAIR, PAIR)] = piece.astype(low)
    loads[1].wait()
    wd_own[...] = stage[pl.ds(16, 16), pl.ds(6144, 2048)].astype(low)
    left16 = lax.broadcasted_iota(jnp.int32, (16, PAIR), 1) < HEAD
    loads[2].wait()
    for j in range(8):
        for k in range(4):
            first = stage[pl.ds(0, 16), pl.ds(j * 1024 + k * PAIR, PAIR)]
            second = stage[pl.ds(0, 16), pl.ds(j * 1024 + 512 + k * PAIR, PAIR)]
            even = jnp.where(left16, first, pltpu.roll(second, HEAD, 1))
            odd = jnp.where(left16, pltpu.roll(first, HEAD, 1), second)
            we_send[2 * k, :, pl.ds(j * PAIR, PAIR)] = even.astype(low)
            we_send[2 * k + 1, :, pl.ds(j * PAIR, PAIR)] = odd.astype(low)
    for k in range(4):
        loads[3 + k].wait()
        ws[z, y, pl.ds(16 * k, 16)] = stage[pl.ds(32, 16), pl.ds(2048 * k, 2048)].astype(low)
    enter()

    works, stages, tasks, finished = {}, {}, {}, set()
    token_sends = []

    def finish(*names):
        for name in names:
            for _ in works[name]:
                pass
            finished.add(name)

    def advance(name):
        if name not in works:
            works[name], stages[name] = begin(name), 0
        stages[name] += 1
        if next(works[name], 0) == 0:
            finished.add(name)

    def reach(name, stage):
        while stages[name] < stage:
            advance(name)

    def begin(name):
        if name == "vec":
            return gather_vectors(copies, vec_group, vec_rows, wd.at[z, y, :, pl.ds(MODEL, 512)])
        if name == "to_q":
            return expand_to_group(copies, wq_send, wq, 768)
        if name == "to_e":
            return expand_to_group(copies, we_send, we, 1024)
        if name == "to_d":
            there = dense_partner()
            place = wd.at[there["z"], there["y"], :, pl.ds(0, MODEL)]
            return landed(copies.start(wd_own, place, there))
        if name == "q":
            finish("to_q")
            return gather_weights(copies, by_rows(wq, 128))
        if name == "d":
            finish("to_d", "vec")
            return gather_weights(copies, by_columns(wd, 2560))
        if name == "e":
            finish("to_e")
            return gather_weights(copies, by_rows(we, 128))
        if name == "s":
            return gather_weights(copies, by_rows(ws, 64))
        if name == "cot":
            return gather_tokens(copies, d_out, [])
        if name == "tok":
            return gather_tokens(copies, normed, token_sends)
        if name == "sum_d":
            return scatter_weights(copies, by_columns(gd, 2048), wide_d, narrow_d, give_d)
        if name == "sum_q":
            return sum_q()
        if name in ("sum_e0", "sum_e1"):
            half = int(name[-1])
            cols = pl.ds(half * 512, 512)
            return scatter_weights(
                copies,
                by_rows(ge.at[:, :, :, cols], 128),
                wide_e.at[:, :, :, :, cols],
                narrow_e.at[:, :, :, cols],
                give_e(half),
            )
        if name in ("sum_s0", "sum_s1"):
            finish("sum_q")
            if "wide" not in finished:
                pl.semaphore_wait(wide_free, 4)
                finished.add("wide")
            half = int(name[-1])
            cols = pl.ds(half * 1024, 1024)
            return scatter_weights(
                copies,
                by_rows(gs.at[:, :, :, cols], 64),
                wide_s.at[:, :, :, :, cols],
                narrow_s.at[:, :, :, cols],
                give_s(half),
            )
        if name in ("n0", "n1", "o0", "o1"):
            half = int(name[-1])
            if name[0] == "o":
                finish("n" + name[1])
            cols = pl.ds(half * 1024, 1024)
            return scatter_tokens(
                copies,
                (normed if name[0] == "n" else d_out).at[:, :, :, cols],
                core_land.at[:, :, cols],
                ring_land.at[:, :, cols],
                (give_n if name[0] == "n" else give_o)(half),
                core_free.at[half],
                ring_free.at[half],
                name[0] == "n",
            )
        if name == "back_q":
            finish("sum_q")
            return return_to_group(copies, res_q, gq_out)
        if name == "back_e":
            finish("sum_e0", "sum_e1")
            return return_to_group(copies, res_e, ge_out)
        if name == "back_d":
            finish("sum_d")
            return landed(copies.start(res_d, gd_out, dense_partner()))
        return sum_vectors(copies, vec_part, vec_came, vec_mine, vec_zy, vec_out)

    def vec_task():
        finish("d")
        for i in range(16):
            block = wd[i // 4, i % 4, :, pl.ds(MODEL, PAIR)].astype(f32)
            vec_rows[pl.ds(11 * i, 11), :] = block[0:11]

    def norm_blocks(blocks):
        def chunk(r, _):
            rows = pl.ds(pl.multiple_of(r * 16, 16), 16)
            for core, chip in blocks:
                values = normed[core, chip, rows].astype(f32)
                center = values - jnp.mean(values, axis=1, keepdims=True)
                inverse = lax.rsqrt(jnp.mean(center * center, axis=1, keepdims=True) + NORM_EPS)
                own = center * inverse * row_of(vec_rows, 0, 16) + row_of(vec_rows, 16, 16)
                normed[core, chip, rows] = own.astype(low)
            return 0

        lax.fori_loop(0, 8, chunk, 0)

    def norm_own():
        reach("tok", 2)
        for copy in token_sends[0]:
            copy.leave()
        token_sends[0][2].arrive()
        norm_blocks([(c, x), (1 - c, x)])

    def norm_sides():
        reach("tok", 3)
        for copy in token_sends[1]:
            copy.leave()
        for copy in token_sends[1][2:]:
            copy.arrive()
        for way in (-1, 1):
            norm_blocks([(c, other("x", way)), (1 - c, other("x", way))])

    def norm_far():
        finish("tok")
        token_sends[2][0].leave()
        norm_blocks([(c, other("x", 2)), (1 - c, other("x", 2))])

    def qkv_tile(g, _):
        meta = vec_group[g, x, pl.ds(4, 1), :]
        projected = dot(normed[g].reshape(512, MODEL), wq[...].reshape(MODEL, 768))
        for p in range(6):
            bias = vec_rows[pl.ds(32 + (p // 2) * 16 + (1 - p % 2) * 8 + t, 1), :]
            for b in range(4):
                rows = pl.ds(b * BLOCK, BLOCK)
                part = projected[b * BLOCK : (b + 1) * BLOCK, p * PAIR : (p + 1) * PAIR] + bias
                if p < 4:
                    part = turned(part, table_of(meta, turn_ref, b), 1)
                part = part.astype(low)
                if p < 2:
                    part = part * jnp.asarray(SCALE, low)
                qkv[g, rows, pl.ds(p * PAIR, PAIR)] = part
        att[g] = dot_t(d_out[g].reshape(512, MODEL), wd[:, :, :, pl.ds(0, MODEL)].reshape(256, MODEL)).astype(low)
        return 0

    def qkv_task(g):
        def task():
            finish("tok", "cot", "q", "d")
            lax.fori_loop(g, g + 1, qkv_tile, 0)

        return task

    def attend_tile(i, _):
        g, p = i // 2, lax.rem(i, 2)
        attend(vec_group[g, x, pl.ds(4, 1), :], turn_ref, qkv, att, g, p)
        return 0

    def dense_tile(n, _):
        cols = pl.ds(pl.multiple_of(n * 1024, 1024), 1024)
        term = cross(att[...].reshape(1024, 256), d_out[:, :, :, cols].reshape(1024, 1024))
        gd[:, :, :, cols] = term.astype(low).reshape(4, 4, 16, 1024)
        return 0

    def give_d(part, total):
        res_d[:, pl.ds(part * 512, 512)] = total.astype(low)

    def qkv_grad_tile(i, _):
        mine = normed[:, :, :, pl.ds(pl.multiple_of(i * 512, 512), 512)].reshape(1024, 512)
        term = cross(mine, qkv[...].reshape(1024, 768)).astype(low).reshape(4, BLOCK, 768)
        gq[i, :, :, pl.ds(0, 768)] = term[:, :64]
        gq[i, :, :, pl.ds(768, 768)] = term[:, 64:]
        return 0

    def give_q(part, total):
        res_q[part] = total[:, :768].astype(low)
        res_q[4 + part] = total[:, 768:].astype(low)

    def sum_q():
        short = pl.ds(0, 1536)
        yield from scatter_weights(
            copies,
            by_rows(gq, 64),
            wide_s.at[:, :, :, :, short],
            narrow_s.at[:, :, :, short],
            give_q,
        )
        for axis in ("y", "z"):
            for way in (1, -1):
                to = {axis: other(axis, way)}
                pl.semaphore_signal(wide_free, inc=1, device_id=to, device_id_type=MESH)

    def up_tile(i, _):
        g, n = i // 2, lax.rem(i, 2)
        cols = pl.ds(pl.multiple_of(n * 512, 512), 512)
        pre_term = dot(normed[g].reshape(512, MODEL), we[:, :, :, cols].reshape(MODEL, 512))
        for k in range(8):
            stage[:, pl.ds(k * 512, 512)] = pre_term[k * 64 : k * 64 + 64]
        act_term = dot_t(d_out[g].reshape(512, MODEL), ws[pl.ds(2 * n, 2)].reshape(512, MODEL))
        for k in range(8):
            stage[:, pl.ds(4096 + k * 512, 512)] = act_term[k * 64 : k * 64 + 64]

        def chunk(r, _):
            rows = pl.ds(pl.multiple_of(r * 16, 16), 16)
            at = pl.ds(pl.multiple_of(lax.rem(r, 4) * 16, 16), 16)
            across = r // 4
            pre = stage[at, pl.ds(pl.multiple_of(across * 512, 512), 512)]
            pre = pre + bias_e[pl.ds(0, 1), cols]
            square = pre * pre
            inner = jnp.tanh(GELU_A * (pre + GELU_B * (square * pre)))
            cover = 0.5 + 0.5 * inner
            act[g, rows, cols] = (pre * cover).astype(low)
            slope = cover + 0.5 * pre * (1.0 - inner * inner) * (
                GELU_A + (3.0 * GELU_A * GELU_B) * square
            )
            d_act = stage[at, pl.ds(pl.multiple_of(4096 + across * 512, 512), 512)]
            d_pre[g, rows, cols] = (d_act * slope).astype(low)
            return 0

        lax.fori_loop(0, 32, chunk, 0, unroll=2)
        return 0

    def up_bias():
        odd = lax.rem(t, 2) == 1
        half = t // 2
        left = lane < HEAD
        bias_e[...] = jnp.zeros_like(bias_e)
        for j in range(8):
            r0 = vec_rows[pl.ds(96 + 8 * j + half, 1), :]
            r1 = vec_rows[pl.ds(100 + 8 * j + half, 1), :]
            even_row = jnp.where(left, r0, pltpu.roll(r1, HEAD, 1))
            odd_row = jnp.where(left, pltpu.roll(r0, HEAD, 1), r1)
            bias_e[pl.ds(0, 1), pl.ds(j * PAIR, PAIR)] = jnp.where(odd, odd_row, even_row)

    def up_task(i):
        def task():
            finish("e", "s")
            if i == 0:
                up_bias()
            lax.fori_loop(i, i + 1, up_tile, 0)

        return task

    def expand_tile(half):
        cols = pl.ds(half * 512, 512)

        def body(i, _):
            mine = normed[:, :, :, pl.ds(pl.multiple_of(i * 512, 512), 512)].reshape(1024, 512)
            term = cross(mine, d_pre[:, :, cols].reshape(1024, 512))
            ge[i, :, :, cols] = term.astype(low).reshape(4, BLOCK, 512)
            return 0

        return body

    def give_e(half):
        def give(part, total):
            cols = pl.ds(half * 512, 512)
            res_e[pl.ds(2 * part, 2), :, cols] = total.astype(low).reshape(2, 16, 512)

        return give

    def shrink_tile(half):
        cols = pl.ds(half * 1024, 1024)

        def body(j, _):
            mine = act[:, :, pl.ds(pl.multiple_of(j * 512, 512), 512)].reshape(1024, 512)
            term = cross(mine, d_out[:, :, :, cols].reshape(1024, 1024))
            gs[pl.ds(2 * j, 2), :, :, cols] = term.astype(low).reshape(2, 4, 64, 1024)
            return 0

        return body

    def give_s(half):
        def give(part, total):
            gs_out[pl.ds(part * 16, 16), pl.ds(half * 1024, 1024)] = total

        return give

    def down_tile(g):
        def body(i, _):
            cols = pl.ds(pl.multiple_of(i * 512, 512), 512)
            term = dot_t(qkv[g], wq[i].reshape(512, 768)) + dot_t(d_pre[g], we[i].reshape(512, 1024))
            normed[g, :, :, cols] = term.astype(low).reshape(4, BLOCK, 512)
            return 0

        return body

    def give_n(half):
        def give(high, r, total):
            at = pl.ds(pl.multiple_of(r * 16, 16), 16)
            stage[at, pl.ds(high * 2048 + half * 1024, 1024)] = total

        return give

    def out_tile(g):
        def body(i, _):
            cols = pl.ds(pl.multiple_of(i * 512, 512), 512)
            term = dot(att[g], wd[:, :, :, cols].reshape(256, 512)) + dot(
                act[g], ws[:, :, :, cols].reshape(1024, 512)
            )
            d_out[g, :, :, cols] = term.astype(low).reshape(4, BLOCK, 512)
            return 0

        return body

    def give_o(half):
        def give(high, r, total):
            rows = pl.ds(pl.multiple_of(high * 64 + r * 16, 16), 16)
            cols = pl.ds(half * 1024, 1024)
            add_bias = row_of(vec_rows, 80 + half * 8, 8) + row_of(vec_rows, 160 + half * 8, 8)
            out_ref[rows, cols] = (tokens_ref[rows, cols].astype(f32) + (total + add_bias)).astype(low)

        return give

    def norm_back():
        finish("n0", "n1")
        gain = row_of(vec_rows, 0, 16)
        vec_sum[...] = jnp.zeros_like(vec_sum)

        def chunk(r, _):
            rows = pl.ds(pl.multiple_of(r * 16, 16), 16)
            at = pl.ds(pl.multiple_of(lax.rem(r, 4) * 16, 16), 16)
            total = stage[at, pl.ds(pl.multiple_of((r // 4) * 2048, 2048), 2048)]
            mine = tokens_ref[rows, :].astype(f32)
            middle = mine - jnp.mean(mine, axis=1, keepdims=True)
            spread = lax.rsqrt(jnp.mean(middle * middle, axis=1, keepdims=True) + NORM_EPS)
            xhat = middle * spread
            e = total * gain
            mean_e = jnp.mean(e, axis=1, keepdims=True)
            mean_x = jnp.mean(e * xhat, axis=1, keepdims=True)
            dy = d_out_rows(rows, r * 16)
            ig_ref[rows, :] = (dy + spread * (e - mean_e - xhat * mean_x)).astype(low)
            for i, value in enumerate((total * xhat, total, dy)):
                vec_sum[i] += value[0:8] + value[8:16]
            return 0

        lax.fori_loop(0, 8, chunk, 0)
        vec_part[...] = jnp.zeros_like(vec_part)
        for i in range(3):
            total = jnp.sum(vec_sum[i], axis=0, keepdims=True)
            for k in range(8):
                vec_part[k, pl.ds(i, 1), :] = total[:, k * 256 : k * 256 + 256]

    def column_sums():
        ones = jnp.ones((8, 1024), low)
        vec_mine[...] = jnp.zeros_like(vec_mine)
        qkv_sum = dot(ones, qkv[...].reshape(1024, 768))
        for i in range(6):
            vec_mine[pl.ds(6 + i, 1), :] = qkv_sum[0:1, i * PAIR : (i + 1) * PAIR]
        pre_sum = dot(ones, d_pre[...].reshape(1024, 1024))
        for i in range(8):
            vec_mine[pl.ds(12 + i, 1), :] = pre_sum[0:1, i * PAIR : (i + 1) * PAIR]

    def loop(first, last, tile):
        return lambda: lax.fori_loop(first, last, tile, 0)

    tasks = {
        "vec_rows": vec_task, "norm_own": norm_own, "norm_sides": norm_sides, "norm_far": norm_far,
        "qkv0": qkv_task(0), "qkv1": qkv_task(1), "grad_d": loop(0, 2, dense_tile),
        "grad_q0": loop(0, 2, qkv_grad_tile), "grad_q1": loop(2, 4, qkv_grad_tile),
        "grad_e0": loop(0, 4, expand_tile(0)), "grad_e1": loop(0, 4, expand_tile(1)),
        "grad_s0": loop(0, 2, shrink_tile(0)), "grad_s1": loop(0, 2, shrink_tile(1)),
        "norm_back": norm_back, "col_sums": column_sums,
    }
    for i in range(4):
        tasks["att" + str(i)] = loop(i, i + 1, attend_tile)
        tasks["up" + str(i)] = up_task(i)
    for half in range(2):
        for name, tile in (("down", down_tile), ("out", out_tile)):
            for at, g in (("a", 1 - c), ("b", c)):
                tasks[name + at + str(half)] = loop(2 * half, 2 * half + 2, tile(g))

    for name in SCHEDULE:
        if name in tasks:
            tasks[name]()
        else:
            advance(name)
    finish(*works)
    copies.finish()


def layer(tokens, cotangent, block_seq, seq_lengths, vectors, weights):
    low, f32 = jnp.bfloat16, jnp.float32
    vmem = pl.BlockSpec(memory_space=pltpu.VMEM)
    smem = pl.BlockSpec(memory_space=pltpu.SMEM)
    anywhere = pl.BlockSpec(memory_space=pl.ANY)
    turn = jnp.asarray(np.stack(rotary_constants())[:, : 3 * BLOCK])
    outs = [
        ((BLOCK, MODEL), low), ((BLOCK, MODEL), low), ((8, 16, 1024), low), ((8, 16, 768), low),
        ((16, MODEL), low), ((64, MODEL), f32), ((2, 4, 24, PAIR), f32),
    ]
    held = [
        ((4, 4, 128, 1024), low), ((4, 4, 128, 768), low), ((4, 4, 16, 2560), low),
        ((4, 4, 64, 2048), low), ((2, 4, 128, 2048), low), ((2, 4, 128, 2048), low),
        ((2, 512, 1024), low), ((2, 512, 1024), low), ((2, 512, 768), low), ((2, 512, 256), low),
        ((4, 4, 128, 1024), low), ((4, 4, 64, 1536), low), ((4, 4, 16, 2048), low),
        ((4, 4, 64, 2048), low), ((64, 8192), f32), ((8, 1024), f32),
        ((2, 4, 8, 128), f32), ((184, 128), f32),
        ((8, 16, 1024), low), ((8, 16, 768), low), ((16, 2048), low),
        ((2, 6, 4, 32, 1024), low), ((2, 6, 32, 1024), low),
        ((2, 6, 4, 16, 512), low), ((2, 6, 16, 512), low),
        ((2, 6, 4, 16, 2048), low), ((2, 6, 16, 2048), low),
        ((4, 128, 2048), low), ((6, 64, 2048), low),
        ((8, 16, 1024), low), ((8, 16, 768), low), ((16, 2048), low), ((8, 384), f32),
        ((3, 8, MODEL), f32), ((8, 8, 256), f32), ((8, 8, 256), f32), ((24, 128), f32),
        ((4, 4, 24, 128), f32),
    ]
    return pl.pallas_call(
        layer_kernel,
        in_specs=[vmem, vmem, smem, smem, vmem, vmem] + [anywhere] * 4,
        out_specs=[vmem] * 7,
        out_shape=[jax.ShapeDtypeStruct(s, k) for s, k in outs],
        scratch_shapes=[pltpu.VMEM(s, k) for s, k in held]
        + [
            pltpu.SemaphoreType.DMA((COPIES,)),
            pltpu.SemaphoreType.DMA((COPIES,)),
            pltpu.SemaphoreType.DMA((7,)),
            pltpu.SemaphoreType.REGULAR((2,)),
            pltpu.SemaphoreType.REGULAR((2,)),
            pltpu.SemaphoreType.REGULAR,
        ],
        compiler_params=pltpu.CompilerParams(
            collective_id=0, has_side_effects=True, vmem_limit_bytes=64 * 2**20
        ),
        name="layer",
    )(tokens, cotangent, block_seq, seq_lengths, vectors[None, :], turn, *weights)


def update_kernel(out_in, ig_in, ge, gq, gd, gs, vec, *refs):
    f32 = jnp.float32
    masters, moments, seconds = refs[0:5], refs[5:10], refs[10:15]
    out_ref, ig_ref = refs[15:17]
    results = [refs[17 + 3 * i : 20 + 3 * i] for i in range(5)]
    flat = refs[32]
    out_ref[...] = out_in[...]
    ig_ref[...] = ig_in[...]

    def update(i, at, gradient):
        grad_ref, state_ref, new_ref = results[i]
        grad_ref[at] = gradient
        state, new = adam_step(
            masters[i][at], moments[i][at], seconds[i][at], gradient, RATES[i], DECAYS[i]
        )
        state_ref[at] = state
        new_ref[at] = new

    every = slice(None)
    for s in range(3):
        for hi in range(2):
            for t in range(TPN):
                col = s * MODEL + hi * 1024 + t * PAIR
                piece = gq[t, :, pl.ds((2 * s + 1 - hi) * PAIR, PAIR)].astype(f32)
                update(0, (every, pl.ds(col, PAIR)), piece)
    for k in range(16):
        cols = (every, pl.ds(k * PAIR, PAIR))
        update(1, cols, gd[cols].astype(f32))
        for r in range(4):
            at = (pl.ds(16 * r, 16), pl.ds(k * PAIR, PAIR))
            update(3, at, gs[at])
    left = lax.broadcasted_iota(jnp.int32, (16, PAIR), 1) < HEAD
    for j in range(16):
        for k in range(4):
            first = ge[2 * k, :, pl.ds((j // 2) * PAIR, PAIR)].astype(f32)
            second = ge[2 * k + 1, :, pl.ds((j // 2) * PAIR, PAIR)].astype(f32)
            if j % 2 == 0:
                second = pltpu.roll(second, HEAD, 1)
            else:
                first = pltpu.roll(first, HEAD, 1)
            update(2, (every, pl.ds(j * 512 + k * PAIR, PAIR)), jnp.where(left, first, second))

    flat[...] = jnp.zeros_like(flat)
    left = lax.broadcasted_iota(jnp.int32, (1, PAIR), 1) < HEAD

    def line(t, row):
        return vec[t // 4, t % 4, pl.ds(row, 1), :]

    for t in range(TPN):
        for i in range(2):
            for row, base in ((0, 0), (1, 16), (2, 80), (2, 160)):
                flat[pl.ds(base + 2 * t + i, 1), :] = line(t, 2 * row + i)
        for s in range(3):
            for hi in range(2):
                at = 32 + s * 16 + hi * 8 + t
                flat[pl.ds(at, 1), :] = line(t, 6 + 2 * s + 1 - hi)
    for j in range(16):
        for k in range(4):
            first = line(2 * k, 12 + j // 2)
            second = line(2 * k + 1, 12 + j // 2)
            if j % 2 == 0:
                second = pltpu.roll(second, HEAD, 1)
            else:
                first = pltpu.roll(first, HEAD, 1)
            flat[pl.ds(96 + 4 * j + k, 1), :] = jnp.where(left, first, second)
    z, y, c, x = (lax.axis_index(a) for a in ALL)
    number = ((z * 4 + y) * 2 + c) * 4 + x
    first = (176 * number) // 128
    own = jnp.concatenate([flat[pl.ds(first + i, 1), :] for i in range(3)], axis=1)
    own = jnp.broadcast_to(own, (8, 3 * PAIR))
    own = pltpu.roll(own, lax.rem(3 * PAIR - 16 * lax.rem(3 * number, 8), 3 * PAIR), 1)
    update(4, (every, every), own[0:1, 0:176])


def update_all(parts, masters, moments, seconds):
    f32 = jnp.float32
    vmem = pl.BlockSpec(memory_space=pltpu.VMEM)
    shapes = [jax.ShapeDtypeStruct(p.shape, p.dtype) for p in parts[:2]]
    for w in masters:
        shapes += [jax.ShapeDtypeStruct(w.shape, f32)] * 3
    return pl.pallas_call(
        update_kernel,
        in_specs=[vmem] * 22,
        out_specs=[vmem] * 17,
        out_shape=shapes,
        scratch_shapes=[pltpu.VMEM((184, PAIR), f32)],
        compiler_params=pltpu.CompilerParams(vmem_limit_bytes=62 * 2**20),
        name="update",
    )(*parts, *masters, *moments, *seconds)


def adam_step(weight, moment, second, gradient, step_rate, step_decay):
    moment_new = BETA_ONE * moment + (1 - BETA_ONE) * gradient
    second_new = BETA_TWO * second + (1 - BETA_TWO) * gradient * gradient
    moment_hat = moment_new / (1 - BETA_ONE**STEP)
    second_hat = second_new / (1 - BETA_TWO**STEP)
    updated = weight - step_rate * (
        moment_hat / (jnp.sqrt(second_hat) + ADAM_EPS) + step_decay * weight
    )
    return (second_new, updated)


def shards(
    tokens, cotangent, block_seq, seq_lengths,
    qkv_weight, qkv_moment, qkv_second,
    dense_weight, dense_moment, dense_second,
    expand_weight, expand_moment, expand_second,
    shrink_weight, shrink_moment, shrink_second,
    vectors, vec_moment, vec_second,
):
    parts = layer(
        tokens,
        cotangent,
        block_seq,
        seq_lengths,
        vectors,
        (qkv_weight, dense_weight, expand_weight, shrink_weight),
    )
    masters = (qkv_weight, dense_weight, expand_weight, shrink_weight, vectors[None, :])
    moments = (qkv_moment, dense_moment, expand_moment, shrink_moment, vec_moment[None, :])
    seconds = (qkv_second, dense_second, expand_second, shrink_second, vec_second[None, :])
    results = update_all(parts, masters, moments, seconds)
    return (*results[:14], *(r[0] for r in results[14:]))


def solution(mesh):
    finer = Mesh(mesh.devices.reshape(*SIZES), ALL)
    whole, group = P(ALL, None), P(DP, None)
    return jax.shard_map(
        shards,
        mesh=finer,
        in_specs=(whole, whole, group, group, *[whole] * 12, *[P(ALL)] * 3),
        out_specs=(*[whole] * 14, *[P(ALL)] * 3),
        check_vma=False,
    )
```

```python
import functools

import jax
import jax.numpy as jnp
import numpy as np
from jax import lax
from jax.experimental import pallas as pl
from jax.experimental.pallas import tpu as pltpu
from jax.sharding import Mesh
from jax.sharding import PartitionSpec as P

HEAD = 64
ROT = 32
BLOCK = 128
STEP = 10
GROUP = 512
MODEL = 2048
FF = 8192
PAIR = 2 * HEAD
ALL = ("z", "y", "c", "x")
DP = ("z", "y", "c")
ZY = ("z", "y")
TP = ("c", "x")
SIZES = (4, 4, 2, 4)
TPN = 8
COPIES = 480
SCHEDULE = (
    "to_q", "s", "tok", "q", "s", "vec", "to_d", "cot", "q", "d", "tok", "to_e", "q",
    "vec_rows", "q", "q", "cot", "norm_own", "e", "norm_sides", "norm_far", "qkv0", "cot", "s",
    "s", "qkv1", "d_att", "e", "att0", "att1", "e", "att2", "s", "att3", "grad_d", "e", "e",
    "grad_q0", "grad_q1", "sum_q", "up0", "up1", "up2", "sum_q", "up3", "grad_e0", "grad_e1",
    "sum_d", "sum_e1", "downa1", "n1", "grad_s0", "sum_e0", "sum_q", "downa0", "downb1", "n1",
    "n0", "grad_s1", "sum_q", "sum_e1", "downb0", "sum_e0", "n0", "sum_s1", "sum_d", "n1",
    "outa0", "sum_e1", "outa1", "sum_e0", "sum_s0", "n0", "col_sums", "o1", "back_q", "outb1",
    "norm_back", "sum_e1", "vec_back", "o1", "o0", "sum_d", "outb0", "sum_e0", "sum_s0",
    "sum_d", "o0", "sum_s1", "o1", "back_d", "sum_s0", "vec_back", "sum_s1", "back_e", "sum_s0",
    "sum_s1", "o0", "vec_back", "sum_s1",
)
SCALE = HEAD ** (-0.5)

NORM_EPS = 1e-05
MASKED = -1e30
BETA_ONE = 0.9
BETA_TWO = 0.999
ADAM_EPS = 1e-08
RATES = (0.02, 0.1, 0.02, 0.01, 0.4)
DECAYS = (0.1, 0.1, 0.1, 0.1, 0.0)
GELU_A = float(np.sqrt(2.0 / np.pi))
GELU_B = 0.044715


def dot(a, b):
    return jnp.dot(a, b, preferred_element_type=jnp.float32)


def dot_t(a, b):
    return lax.dot_general(a, b, (((1,), (1,)), ((), ())), preferred_element_type=jnp.float32)


def cross(a, b):
    return lax.dot_general(a, b, (((0,), (0,)), ((), ())), preferred_element_type=jnp.float32)


def rotary_constants():
    half = np.arange(ROT // 2, dtype=np.float32)
    inverse = (10000.0 ** (-2.0 * half.astype(np.float64) / ROT)).astype(np.float32)
    angle = (np.arange(GROUP, dtype=np.float32)[:, None] * inverse[None, :]).astype(np.float64)
    cosine, sine = np.cos(angle).astype(np.float32), np.sin(angle).astype(np.float32)
    one = np.ones((GROUP, HEAD - ROT), np.float32)
    zero = np.zeros((GROUP, ROT // 2), np.float32)
    rest = np.zeros((GROUP, HEAD - ROT), np.float32)
    turn = np.concatenate([cosine, cosine, one], axis=1)
    ahead = np.concatenate([-sine, zero, rest], axis=1)
    behind = np.concatenate([zero, sine, rest], axis=1)
    return tuple(np.concatenate([a, a], axis=1) for a in (turn, ahead, behind))


MESH = pl.DeviceIdType.MESH


def other(axis, step):
    size = SIZES[ALL.index(axis)]
    return lax.rem(lax.axis_index(axis) + step + size, size)


class Copy:
    def __init__(self, copy):
        self.copy, self.here, self.gone = copy, False, False

    def arrive(self):
        if not self.here:
            self.copy.wait_recv()
        self.here = True

    def leave(self):
        if not self.gone:
            self.copy.wait_send()
        self.gone = True


class Copies:
    def __init__(self, send, recv):
        self.send, self.recv, self.all = send, recv, []

    def start(self, src, dst, to):
        at = len(self.all)
        copy = pltpu.make_async_remote_copy(
            src_ref=src,
            dst_ref=dst,
            send_sem=self.send.at[at],
            recv_sem=self.recv.at[at],
            device_id=to,
            device_id_type=MESH,
        )
        copy.start()
        self.all.append(Copy(copy))
        return self.all[-1]

    def finish(self):
        for copy in self.all:
            copy.leave()


def greet():
    barrier = pltpu.get_barrier_semaphore()
    for partner in token_partners() + weight_partners() + [dense_partner()]:
        pl.semaphore_signal(barrier, inc=1, device_id=partner, device_id_type=MESH)


def enter():
    pl.semaphore_wait(pltpu.get_barrier_semaphore(), 23)


def token_partners():
    return [{"c": other("c", i), "x": other("x", j)} for i in range(2) for j in range(4) if i + j]


def weight_partners():
    return [{"z": other("z", i), "y": other("y", j)} for i in range(4) for j in range(4) if i + j]


def dense_partner():
    z, y, c, x = (lax.axis_index(a) for a in ALL)
    return {"z": (1 - z // 2) * 2 + c, "y": x, "c": lax.rem(z, 2), "x": y}


def gather_weights(copies, view):
    z, y = lax.axis_index("z"), lax.axis_index("y")
    z_up, z_down, y_up, y_down = other("z", 1), other("z", -1), other("y", 1), other("y", -1)
    z_far, y_far = other("z", 2), other("y", 2)
    up, down, far, near = {"y": y_up}, {"y": y_down}, {"z": z_up}, {"z": z_down}

    def go(block, to):
        return copies.start(block, block, to)

    a_up, a_down = go(view(z, y, 4), up), go(view(z, y, 4), down)
    b_up, b_down = go(view(z, y, 5), far), go(view(z, y, 5), near)
    a_own = go(view(z, y, 4), far), go(view(z, y, 4), near)
    b_own = go(view(z, y, 5), up), go(view(z, y, 5), down)
    yield
    a_up.arrive()
    a_low = go(view(z, y_down, 0), up)
    b_up.arrive()
    b_low = go(view(z_down, y, 2), far)
    a_down.arrive()
    a_high = go(view(z, y_up, 1), down)
    b_down.arrive()
    b_high = go(view(z_up, y, 3), near)
    a_side = [(i, go(view(z, i, 4), far), go(view(z, i, 4), near)) for i in (y_down, y_up)]
    b_side = [(i, go(view(i, y, 5), up), go(view(i, y, 5), down)) for i in (z_down, z_up)]
    yield
    last = []
    a_own[0].arrive()
    last.append(go(view(z_down, y, 0), far))
    b_own[0].arrive()
    last.append(go(view(z, y_down, 2), up))
    a_own[1].arrive()
    last.append(go(view(z_up, y, 1), near))
    b_own[1].arrive()
    last.append(go(view(z, y_up, 3), down))
    a_low.arrive()
    a_high.arrive()
    a_side.append((y_far, go(view(z, y_far, 4), far), go(view(z, y_far, 4), near)))
    b_low.arrive()
    b_high.arrive()
    b_side.append((z_far, go(view(z_far, y, 5), up), go(view(z_far, y, 5), down)))
    for k in range(3):
        if k != 1:
            yield
        i, first, second = a_side[k]
        first.arrive()
        last.append(go(view(z_down, i, 0), far))
        second.arrive()
        last.append(go(view(z_up, i, 1), near))
        i, first, second = b_side[k]
        first.arrive()
        last.append(go(view(i, y_down, 2), up))
        second.arrive()
        last.append(go(view(i, y_up, 3), down))
    yield
    for copy in last:
        copy.arrive()


def gather_tokens(copies, ref, sent):
    c, x, across = lax.axis_index("c"), lax.axis_index("x"), other("c", 1)
    right, left = {"x": other("x", 1)}, {"x": other("x", -1)}

    def go(block, to):
        return copies.start(block, block, to)

    own = ref.at[c, x]
    sent.append([go(own, right), go(own, left), go(own, {"c": across})])
    yield
    sent[0][0].arrive()
    last = [go(ref.at[c, other("x", -1), pl.ds(0, 64)], right)]
    side = [go(ref.at[c, other("x", -1)], {"c": across})]
    sent[0][1].arrive()
    last.append(go(ref.at[c, other("x", 1), pl.ds(64, 64)], left))
    side.append(go(ref.at[c, other("x", 1)], {"c": across}))
    sent.append(last + side)
    yield
    for copy in last:
        copy.arrive()
    sent.append([go(ref.at[c, other("x", 2)], {"c": across})])
    yield
    for copies_of_stage in sent:
        for copy in copies_of_stage:
            copy.arrive()
            copy.leave()


def gather_vectors(copies, group, rows, place):
    c, x = lax.axis_index("c"), lax.axis_index("x")
    sent = [copies.start(group.at[c, x], group.at[c, x], to) for to in token_partners()]
    yield
    for copy in sent:
        copy.arrive()
    rows[pl.ds(0, 16), :] = jnp.zeros((16, PAIR), jnp.float32)
    for d in range(TPN):
        rows[pl.ds((176 * d) // PAIR, 3), :] += group[d // 4, d % 4, pl.ds(0, 3), :]
    place[:, pl.ds(0, PAIR)] = rows[pl.ds(0, 16), :].astype(jnp.bfloat16)
    place[:, pl.ds(PAIR, 3 * PAIR)] = jnp.zeros((16, 3 * PAIR), jnp.bfloat16)


def expand_to_group(copies, send, ref, width):
    z, y, c, x = (lax.axis_index(a) for a in ALL)
    rows = pl.ds(pl.multiple_of((c * 4 + x) * 16, 16), 16)
    sent = []
    for to in token_partners():
        sent.append(copies.start(send.at[to["c"] * 4 + to["x"]], ref.at[z, y, rows], to))
    ref[z, y, rows] = send[c * 4 + x]
    yield
    for copy in sent:
        copy.arrive()


def by_rows(ref, rows):
    quarter = rows // 4

    def view(z, y, part):
        start, size = (part * quarter, quarter) if part < 4 else ((part - 4) * 2 * quarter, 2 * quarter)
        return ref.at[z, y, pl.ds(start, size)]

    return view


def by_columns(ref, columns):
    quarter = columns // 4

    def view(z, y, part):
        start, size = (part * quarter, quarter) if part < 4 else ((part - 4) * 2 * quarter, 2 * quarter)
        return ref.at[z, y, :, pl.ds(start, size)]

    return view


def step(*works):
    for work in works:
        next(work, None)


def row_of(ref, first, count):
    return jnp.concatenate([ref[pl.ds(first + i, 1), :] for i in range(count)], axis=1)


def ring_sum(copies, axis, block, land, low_part, high_part):
    ahead, behind = other(axis, 1), other(axis, -1)
    up, down = {axis: ahead}, {axis: behind}
    far = other(axis, 2)
    t_low = copies.start(block(far, low_part), land.at[0], up)
    t_high = copies.start(block(far, high_part), land.at[1], down)
    d_high = copies.start(block(ahead, high_part), land.at[3], up)
    d_low = copies.start(block(behind, low_part), land.at[2], down)
    yield
    t_low.arrive()
    land[0] = land[0] + block(ahead, low_part)[...]
    p_low = copies.start(land.at[0], land.at[4], up)
    t_high.arrive()
    land[1] = land[1] + block(behind, high_part)[...]
    p_high = copies.start(land.at[1], land.at[5], down)
    yield
    for copy in (d_low, d_high, p_low, p_high):
        copy.arrive()
    for copy in (t_low, t_high, d_low, d_high, p_low, p_high):
        copy.leave()


def three(own, land, high, at=...):
    f32 = jnp.float32
    first, second = land.at[4 + high], land.at[2 + high]
    return own[at].astype(f32) + first[at].astype(f32) + second[at].astype(f32)


def both(first, second):
    while True:
        done = [next(first, 0), next(second, 0)]
        if 0 in done:
            return
        yield


def scatter_weights(copies, view, wide, narrow, give):
    z, y = lax.axis_index("z"), lax.axis_index("y")
    every = slice(None)
    low = jnp.bfloat16
    yield from both(
        ring_sum(copies, "y", lambda i, p: view(every, i, p), wide.at[0], 0, 1),
        ring_sum(copies, "z", lambda i, p: view(i, every, p), wide.at[1], 2, 3),
    )
    for high in range(2):
        own = view(every, y, high)
        for i in range(4):
            own[i] = three(own, wide.at[0], high, i).astype(low)
        own = view(z, every, 2 + high)
        for i in range(4):
            own[i] = three(own, wide.at[1], high, i).astype(low)
    yield from both(
        ring_sum(copies, "z", lambda i, p: view(i, y, p), narrow.at[0], 0, 1),
        ring_sum(copies, "y", lambda i, p: view(z, i, p), narrow.at[1], 2, 3),
    )
    for high in range(2):
        give(high, three(view(z, y, high), narrow.at[0], high))
        give(2 + high, three(view(z, y, 2 + high), narrow.at[1], high))


def scatter_tokens(copies, ref, core_land, land, give, core_free, ring_free, first):
    c, x, across = lax.axis_index("c"), lax.axis_index("x"), other("c", 1)
    if not first:
        pl.semaphore_wait(core_free, 1)
    came = copies.start(ref.at[across], core_land, {"c": across})
    yield
    came.arrive()
    for i in range(4):
        ref[c, i] = ref[c, i] + core_land[i]
    if first:
        pl.semaphore_signal(core_free, inc=1, device_id={"c": across}, device_id_type=MESH)
    else:
        pl.semaphore_wait(ring_free, 2)
    yield from ring_sum(copies, "x", lambda i, p: ref.at[c, i, pl.ds(p * 64, 64)], land, 0, 1)
    for high in range(2):
        own = ref.at[c, x, pl.ds(high * 64, 64)]

        def chunk(r, _):
            rows = pl.ds(pl.multiple_of(r * 16, 16), 16)
            give(high, r, three(own, land, high, rows))
            return 0

        lax.fori_loop(0, 4, chunk, 0)
    if first:
        for way in (1, -1):
            to = {"x": other("x", way)}
            pl.semaphore_signal(ring_free, inc=1, device_id=to, device_id_type=MESH)


def landed(copy):
    yield
    copy.arrive()


def sum_vectors(copies, part, came, mine, zy, out):
    z, y, c, x = (lax.axis_index(a) for a in ALL)
    t = c * 4 + x
    sent = [
        copies.start(part.at[to["c"] * 4 + to["x"]], came.at[t], to) for to in token_partners()
    ]
    came[t] = part[t]
    yield
    for copy in sent:
        copy.arrive()
    total = jnp.sum(came[...], axis=0)
    for i in range(6):
        mine[pl.ds(i, 1), :] = total[i // 2 : i // 2 + 1, (i % 2) * PAIR : (i % 2 + 1) * PAIR]
    zy[z, y] = mine[...]
    sent = [copies.start(mine, zy.at[z, y], to) for to in weight_partners()]
    yield
    for copy in sent:
        copy.arrive()
    out[c, x] = jnp.sum(zy[...].reshape(16, 24, PAIR), axis=0)
    sent = [copies.start(out.at[c, x], out.at[c, x], to) for to in token_partners()]
    yield
    for copy in sent:
        copy.arrive()


def return_to_group(copies, ref, out):
    c, x = lax.axis_index("c"), lax.axis_index("x")
    t = c * 4 + x
    sent = []
    for to in token_partners():
        sent.append(copies.start(ref.at[to["c"] * 4 + to["x"]], out.at[t], to))
    out[t] = ref[t]
    yield
    for copy in sent:
        copy.arrive()


def turned(values, table, sign):
    turn, ahead, behind = table
    up = pltpu.roll(values, PAIR - ROT // 2, 1)
    down = pltpu.roll(values, ROT // 2, 1)
    if sign > 0:
        return values * turn + up * ahead + down * behind
    return values * turn - up * ahead - down * behind


def attend(meta, turn_ref, qkv, att, g, p):
    low, f32 = jnp.bfloat16, jnp.float32
    lane = lax.broadcasted_iota(jnp.int32, (BLOCK, PAIR), 1)
    first = lane < HEAD
    zero = jnp.zeros((BLOCK, PAIR), low)
    row_at = lax.broadcasted_iota(jnp.int32, (BLOCK, BLOCK), 0)
    col_at = lax.broadcasted_iota(jnp.int32, (BLOCK, BLOCK), 1)
    cols = [pl.ds(pl.multiple_of(i * 2 * PAIR + p * PAIR, PAIR), PAIR) for i in range(3)]
    d_k = [jnp.zeros((BLOCK, PAIR), f32) for _ in range(4)]
    d_v = [jnp.zeros((BLOCK, PAIR), f32) for _ in range(4)]
    held = [qkv[g, :, cols[i]] for i in range(3)] + [att[g, :, cols[0]]]
    done = []
    for b in range(4):
        rows, width = slice(b * BLOCK, (b + 1) * BLOCK), (b + 1) * BLOCK
        base = meta[:, 4 + b : 5 + b] * BLOCK
        diagonal = (col_at <= row_at) & (col_at.astype(f32) + base < meta[:, 8 + b : 9 + b])
        bias = [
            jnp.where(meta[:, e : e + 1] == meta[:, b : b + 1], 0.0, MASKED)
            + jnp.zeros((BLOCK, BLOCK), f32)
            for e in range(b)
        ]
        bias.append(jnp.where(diagonal, 0.0, MASKED).astype(f32))
        bias = bias[0] if b == 0 else jnp.concatenate(bias, axis=1)
        q, da, k, v = held[0][rows], held[3][rows], held[1][:width], held[2][:width]
        qs = jnp.concatenate([jnp.where(first, q, zero), jnp.where(first, zero, q)], axis=0)
        das = jnp.concatenate([jnp.where(first, da, zero), jnp.where(first, zero, da)], axis=0)
        scores = dot_t(qs, k) + jnp.concatenate([bias, bias], axis=0)
        w = jnp.exp(scores - jnp.max(scores, axis=1, keepdims=True))
        prob = w * (1.0 / jnp.sum(w, axis=1, keepdims=True))
        prob_low = prob.astype(low)
        summed = dot(prob_low, v)
        dp = dot_t(das, v)
        ds = (prob * (dp - jnp.sum(prob * dp, axis=1, keepdims=True))).astype(low)
        dq = dot(ds, k)
        dq = jnp.where(first, dq[:BLOCK], dq[BLOCK:]) * SCALE
        dq = turned(dq, table_of(meta, turn_ref, b), -1).astype(low)
        done.append((jnp.where(first, summed[:BLOCK], summed[BLOCK:]).astype(low), dq))
        dk = cross(ds, qs)
        dv = cross(prob_low, das)
        for e in range(b + 1):
            d_k[e] = d_k[e] + dk[e * BLOCK : (e + 1) * BLOCK]
            d_v[e] = d_v[e] + dv[e * BLOCK : (e + 1) * BLOCK]
    for b in range(4):
        rows = pl.ds(b * BLOCK, BLOCK)
        att[g, rows, cols[0]], qkv[g, rows, cols[0]] = done[b]
        qkv[g, rows, cols[1]] = turned(d_k[b], table_of(meta, turn_ref, b), -1).astype(low)
        qkv[g, rows, cols[2]] = d_v[b].astype(low)


def table_of(meta, turn_ref, b):
    rank = meta[:, 4 + b : 5 + b]
    parts = [turn_ref[:, pl.ds(r * BLOCK, BLOCK), :] for r in range(3)]
    table = jnp.where((rank == 0.0)[None], parts[0], jnp.where((rank == 1.0)[None], parts[1], parts[2]))
    return table[0], table[1], table[2]


def layer_kernel(
    tokens_ref, cot_ref, seq_ref, length_ref, vec_ref, turn_ref, q_hbm, d_hbm, e_hbm, s_hbm,
    out_ref, ig_ref, ge_out, gq_out, gd_out, gs_out, vec_out,
    we, wq, wd, ws, normed, d_out, act, d_pre, qkv, att,
    ge, gq, gd, gs, stage, bias_e, vec_group, vec_rows, we_send, wq_send, wd_own,
    wide_e, narrow_e, wide_d, narrow_d, wide_s, narrow_s,
    core_land, ring_land, res_e, res_q, res_d,
    vec_line, vec_sum, vec_part, vec_came, vec_mine, vec_zy,
    send, recv, local, core_free, ring_free, wide_free,
):
    low, f32 = jnp.bfloat16, jnp.float32
    z, y, c, x = (lax.axis_index(a) for a in ALL)
    t = c * 4 + x
    copies = Copies(send, recv)
    greet()

    loads = [
        pltpu.make_async_copy(q_hbm, stage.at[pl.ds(16, 16), pl.ds(0, 6144)], local.at[0]),
        pltpu.make_async_copy(d_hbm, stage.at[pl.ds(16, 16), pl.ds(6144, 2048)], local.at[1]),
        pltpu.make_async_copy(e_hbm, stage.at[pl.ds(0, 16)], local.at[2]),
    ]
    for k in range(4):
        rows = pl.ds(16 * k, 16)
        place = stage.at[pl.ds(32, 16), pl.ds(2048 * k, 2048)]
        loads.append(pltpu.make_async_copy(s_hbm.at[rows], place, local.at[3 + k]))
    for load in loads:
        load.start()

    lane = lax.broadcasted_iota(jnp.int32, (1, PAIR), 1)
    seqs = [seq_ref[0, b] for b in range(4)]
    own_meta = jnp.zeros((1, PAIR), f32)
    own_rank, own_limit = jnp.zeros((1, 1), f32), jnp.zeros((1, 1), f32)
    for b in range(4):
        rank = jnp.int32(0)
        for e in range(b):
            rank = rank + jnp.where(seqs[e] == seqs[b], 1, 0)
        limit = jnp.where(seqs[b] == 0, length_ref[0, 0], length_ref[0, 1])
        for at, value in ((b, seqs[b]), (4 + b, rank), (8 + b, limit)):
            own_meta = jnp.where(lane == at, value.astype(f32), own_meta)
        own_rank = jnp.where(x == b, rank.astype(f32), own_rank)
        own_limit = jnp.where(x == b, limit.astype(f32), own_limit)
    vec_line[...] = jnp.zeros_like(vec_line)
    vec_line[pl.ds(0, 1), pl.ds(0, 176)] = vec_ref[...].astype(low).astype(f32)
    line = pltpu.roll(vec_line[...], 16 * lax.rem(3 * t + 24 * (z * 4 + y), 8), 1)
    vec_own = vec_group.at[c, x]
    vec_own[...] = jnp.zeros((8, PAIR), f32)
    for k in range(3):
        vec_own[pl.ds(k, 1), :] = line[0:1, k * PAIR : (k + 1) * PAIR]
    vec_own[pl.ds(4, 1), :] = own_meta

    def d_out_rows(rows, first):
        row_at = lax.broadcasted_iota(jnp.int32, (16, 1), 0) + first
        live = (row_at.astype(f32) + own_rank * BLOCK < own_limit).astype(f32)
        return cot_ref[rows, :].astype(f32) * live

    def mask_chunk(r, _):
        rows = pl.ds(pl.multiple_of(r * 16, 16), 16)
        d_out[c, x, rows] = d_out_rows(rows, r * 16).astype(low)
        return 0


    def scaled(rows):
        values = tokens_ref[rows, :].astype(f32)
        middle = values - jnp.mean(values, axis=1, keepdims=True)
        spread = lax.rsqrt(jnp.mean(middle * middle, axis=1, keepdims=True) + NORM_EPS)
        return middle * spread, spread

    def scale_chunk(r, _):
        rows = pl.ds(pl.multiple_of(r * 16, 16), 16)
        normed[c, x, rows] = scaled(rows)[0].astype(low)
        return 0

    lax.fori_loop(0, 8, scale_chunk, 0)
    loads[0].wait()
    for k in range(8):
        for i in range(6):
            col = (i // 2) * 2048 + (1 - i % 2) * 1024 + k * PAIR
            piece = stage[pl.ds(16, 16), pl.ds(col, PAIR)]
            wq_send[k, :, pl.ds(i * PAIR, PAIR)] = piece.astype(low)
    enter()

    def cast_dense():
        loads[1].wait()
        wd_own[...] = stage[pl.ds(16, 16), pl.ds(6144, 2048)].astype(low)

    def cast_expand():
        left16 = lax.broadcasted_iota(jnp.int32, (16, PAIR), 1) < HEAD
        loads[2].wait()
        for j in range(8):
            for k in range(4):
                first = stage[pl.ds(0, 16), pl.ds(j * 1024 + k * PAIR, PAIR)]
                second = stage[pl.ds(0, 16), pl.ds(j * 1024 + 512 + k * PAIR, PAIR)]
                even = jnp.where(left16, first, pltpu.roll(second, HEAD, 1))
                odd = jnp.where(left16, pltpu.roll(first, HEAD, 1), second)
                we_send[2 * k, :, pl.ds(j * PAIR, PAIR)] = even.astype(low)
                we_send[2 * k + 1, :, pl.ds(j * PAIR, PAIR)] = odd.astype(low)

    def cast_shrink():
        for k in range(4):
            loads[3 + k].wait()
            ws[z, y, pl.ds(16 * k, 16)] = stage[pl.ds(32, 16), pl.ds(2048 * k, 2048)].astype(low)

    works, stages, tasks, finished = {}, {}, {}, set()
    token_sends = []

    def finish(*names):
        for name in names:
            for _ in works[name]:
                pass
            finished.add(name)

    def advance(name):
        if name not in works:
            works[name], stages[name] = begin(name), 0
        stages[name] += 1
        if next(works[name], 0) == 0:
            finished.add(name)

    def reach(name, stage):
        while stages[name] < stage:
            advance(name)

    def begin(name):
        if name == "vec":
            return gather_vectors(copies, vec_group, vec_rows, wd.at[z, y, :, pl.ds(MODEL, 512)])
        if name == "to_q":
            return expand_to_group(copies, wq_send, wq, 768)
        if name == "to_e":
            cast_expand()
            return expand_to_group(copies, we_send, we, 1024)
        if name == "to_d":
            cast_dense()
            there = dense_partner()
            place = wd.at[there["z"], there["y"], :, pl.ds(0, MODEL)]
            return landed(copies.start(wd_own, place, there))
        if name == "q":
            finish("to_q")
            return gather_weights(copies, by_rows(wq, 128))
        if name == "d":
            finish("to_d", "vec")
            return gather_weights(copies, by_columns(wd, 2560))
        if name == "e":
            finish("to_e")
            return gather_weights(copies, by_rows(we, 128))
        if name == "s":
            cast_shrink()
            return gather_weights(copies, by_rows(ws, 64))
        if name == "cot":
            lax.fori_loop(0, 8, mask_chunk, 0)
            return gather_tokens(copies, d_out, [])
        if name == "tok":
            return gather_tokens(copies, normed, token_sends)
        if name == "sum_d":
            return scatter_weights(copies, by_columns(gd, 2048), wide_d, narrow_d, give_d)
        if name == "sum_q":
            return sum_q()
        if name in ("sum_e0", "sum_e1"):
            half = int(name[-1])
            cols = pl.ds(half * 512, 512)
            return scatter_weights(
                copies,
                by_rows(ge.at[:, :, :, cols], 128),
                wide_e.at[:, :, :, :, cols],
                narrow_e.at[:, :, :, cols],
                give_e(half),
            )
        if name in ("sum_s0", "sum_s1"):
            finish("sum_q")
            if "wide" not in finished:
                pl.semaphore_wait(wide_free, 4)
                finished.add("wide")
            half = int(name[-1])
            cols = pl.ds(half * 1024, 1024)
            return scatter_weights(
                copies,
                by_rows(gs.at[:, :, :, cols], 64),
                wide_s.at[:, :, :, :, cols],
                narrow_s.at[:, :, :, cols],
                give_s(half),
            )
        if name in ("n0", "n1", "o0", "o1"):
            half = int(name[-1])
            if name[0] == "o":
                finish("n" + name[1])
            cols = pl.ds(half * 1024, 1024)
            return scatter_tokens(
                copies,
                (normed if name[0] == "n" else d_out).at[:, :, :, cols],
                core_land.at[:, :, cols],
                ring_land.at[:, :, cols],
                (give_n if name[0] == "n" else give_o)(half),
                core_free.at[half],
                ring_free.at[half],
                name[0] == "n",
            )
        if name == "back_q":
            finish("sum_q")
            return return_to_group(copies, res_q, gq_out)
        if name == "back_e":
            finish("sum_e0", "sum_e1")
            return return_to_group(copies, res_e, ge_out)
        if name == "back_d":
            finish("sum_d")
            return landed(copies.start(res_d, gd_out, dense_partner()))
        return sum_vectors(copies, vec_part, vec_came, vec_mine, vec_zy, vec_out)

    def vec_task():
        finish("d")
        for i in range(16):
            block = wd[i // 4, i % 4, :, pl.ds(MODEL, PAIR)].astype(f32)
            vec_rows[pl.ds(11 * i, 11), :] = block[0:11]

    def norm_blocks(blocks):
        def chunk(r, _):
            rows = pl.ds(pl.multiple_of(r * 16, 16), 16)
            for core, chip in blocks:
                xhat = normed[core, chip, rows].astype(f32)
                whole = xhat * row_of(vec_rows, 0, 16) + row_of(vec_rows, 16, 16)
                normed[core, chip, rows] = whole.astype(low)
            return 0

        lax.fori_loop(0, 8, chunk, 0)

    def norm_own():
        reach("tok", 2)
        for copy in token_sends[0]:
            copy.leave()
        token_sends[0][2].arrive()
        norm_blocks([(c, x), (1 - c, x)])

    def norm_sides():
        reach("tok", 3)
        for copy in token_sends[1]:
            copy.leave()
        for copy in token_sends[1][2:]:
            copy.arrive()
        for way in (-1, 1):
            norm_blocks([(c, other("x", way)), (1 - c, other("x", way))])

    def norm_far():
        finish("tok")
        token_sends[2][0].leave()
        norm_blocks([(c, other("x", 2)), (1 - c, other("x", 2))])

    def qkv_tile(g, _):
        meta = vec_group[g, x, pl.ds(4, 1), :]
        projected = dot(normed[g].reshape(512, MODEL), wq[...].reshape(MODEL, 768))
        for p in range(6):
            bias = vec_rows[pl.ds(32 + (p // 2) * 16 + (1 - p % 2) * 8 + t, 1), :]
            for b in range(4):
                rows = pl.ds(b * BLOCK, BLOCK)
                part = projected[b * BLOCK : (b + 1) * BLOCK, p * PAIR : (p + 1) * PAIR] + bias
                if p < 4:
                    part = turned(part, table_of(meta, turn_ref, b), 1)
                part = part.astype(low)
                if p < 2:
                    part = part * jnp.asarray(SCALE, low)
                qkv[g, rows, pl.ds(p * PAIR, PAIR)] = part
        return 0

    def d_att_tile(g, _):
        dense = wd[:, :, :, pl.ds(0, MODEL)].reshape(256, MODEL)
        att[g] = dot_t(d_out[g].reshape(512, MODEL), dense).astype(low)
        return 0

    def d_att_task():
        finish("cot", "d")
        lax.fori_loop(0, 2, d_att_tile, 0)

    def qkv_task(g):
        def task():
            finish("tok", "q")
            lax.fori_loop(g, g + 1, qkv_tile, 0)

        return task

    def attend_tile(i, _):
        g, p = i // 2, lax.rem(i, 2)
        attend(vec_group[g, x, pl.ds(4, 1), :], turn_ref, qkv, att, g, p)
        return 0

    def dense_tile(n, _):
        cols = pl.ds(pl.multiple_of(n * 1024, 1024), 1024)
        term = cross(att[...].reshape(1024, 256), d_out[:, :, :, cols].reshape(1024, 1024))
        gd[:, :, :, cols] = term.astype(low).reshape(4, 4, 16, 1024)
        return 0

    def give_d(part, total):
        res_d[:, pl.ds(part * 512, 512)] = total.astype(low)

    def qkv_grad_tile(i, _):
        mine = normed[:, :, :, pl.ds(pl.multiple_of(i * 512, 512), 512)].reshape(1024, 512)
        term = cross(mine, qkv[...].reshape(1024, 768)).astype(low).reshape(4, BLOCK, 768)
        gq[i, :, :, pl.ds(0, 768)] = term[:, :64]
        gq[i, :, :, pl.ds(768, 768)] = term[:, 64:]
        return 0

    def give_q(part, total):
        res_q[part] = total[:, :768].astype(low)
        res_q[4 + part] = total[:, 768:].astype(low)

    def sum_q():
        short = pl.ds(0, 1536)
        yield from scatter_weights(
            copies,
            by_rows(gq, 64),
            wide_s.at[:, :, :, :, short],
            narrow_s.at[:, :, :, short],
            give_q,
        )
        for axis in ("y", "z"):
            for way in (1, -1):
                to = {axis: other(axis, way)}
                pl.semaphore_signal(wide_free, inc=1, device_id=to, device_id_type=MESH)

    def up_tile(i, _):
        g, n = i // 2, lax.rem(i, 2)
        cols = pl.ds(pl.multiple_of(n * 512, 512), 512)
        pre_term = dot(normed[g].reshape(512, MODEL), we[:, :, :, cols].reshape(MODEL, 512))
        for k in range(8):
            stage[:, pl.ds(k * 512, 512)] = pre_term[k * 64 : k * 64 + 64]
        act_term = dot_t(d_out[g].reshape(512, MODEL), ws[pl.ds(2 * n, 2)].reshape(512, MODEL))
        for k in range(8):
            stage[:, pl.ds(4096 + k * 512, 512)] = act_term[k * 64 : k * 64 + 64]

        def chunk(r, _):
            rows = pl.ds(pl.multiple_of(r * 16, 16), 16)
            at = pl.ds(pl.multiple_of(lax.rem(r, 4) * 16, 16), 16)
            across = r // 4
            pre = stage[at, pl.ds(pl.multiple_of(across * 512, 512), 512)]
            pre = pre + bias_e[pl.ds(0, 1), cols]
            square = pre * pre
            inner = jnp.tanh(GELU_A * (pre + GELU_B * (square * pre)))
            cover = 0.5 + 0.5 * inner
            act[g, rows, cols] = (pre * cover).astype(low)
            slope = cover + 0.5 * pre * (1.0 - inner * inner) * (
                GELU_A + (3.0 * GELU_A * GELU_B) * square
            )
            d_act = stage[at, pl.ds(pl.multiple_of(4096 + across * 512, 512), 512)]
            d_pre[g, rows, cols] = (d_act * slope).astype(low)
            return 0

        lax.fori_loop(0, 32, chunk, 0, unroll=4)
        return 0

    def up_bias():
        odd = lax.rem(t, 2) == 1
        half = t // 2
        left = lane < HEAD
        bias_e[...] = jnp.zeros_like(bias_e)
        for j in range(8):
            r0 = vec_rows[pl.ds(96 + 8 * j + half, 1), :]
            r1 = vec_rows[pl.ds(100 + 8 * j + half, 1), :]
            even_row = jnp.where(left, r0, pltpu.roll(r1, HEAD, 1))
            odd_row = jnp.where(left, pltpu.roll(r0, HEAD, 1), r1)
            bias_e[pl.ds(0, 1), pl.ds(j * PAIR, PAIR)] = jnp.where(odd, odd_row, even_row)

    def up_task(i):
        def task():
            finish("e", "s")
            if i == 0:
                up_bias()
            lax.fori_loop(i, i + 1, up_tile, 0)

        return task

    def expand_tile(half):
        cols = pl.ds(half * 512, 512)

        def body(i, _):
            mine = normed[:, :, :, pl.ds(pl.multiple_of(i * 512, 512), 512)].reshape(1024, 512)
            term = cross(mine, d_pre[:, :, cols].reshape(1024, 512))
            ge[i, :, :, cols] = term.astype(low).reshape(4, BLOCK, 512)
            return 0

        return body

    def give_e(half):
        def give(part, total):
            cols = pl.ds(half * 512, 512)
            res_e[pl.ds(2 * part, 2), :, cols] = total.astype(low).reshape(2, 16, 512)

        return give

    def shrink_tile(half):
        cols = pl.ds(half * 1024, 1024)

        def body(j, _):
            mine = act[:, :, pl.ds(pl.multiple_of(j * 512, 512), 512)].reshape(1024, 512)
            term = cross(mine, d_out[:, :, :, cols].reshape(1024, 1024))
            gs[pl.ds(2 * j, 2), :, :, cols] = term.astype(low).reshape(2, 4, 64, 1024)
            return 0

        return body

    def give_s(half):
        def give(part, total):
            gs_out[pl.ds(part * 16, 16), pl.ds(half * 1024, 1024)] = total

        return give

    def down_tile(g):
        def body(i, _):
            cols = pl.ds(pl.multiple_of(i * 512, 512), 512)
            term = dot_t(qkv[g], wq[i].reshape(512, 768)) + dot_t(d_pre[g], we[i].reshape(512, 1024))
            normed[g, :, :, cols] = term.astype(low).reshape(4, BLOCK, 512)
            return 0

        return body

    def give_n(half):
        def give(high, r, total):
            at = pl.ds(pl.multiple_of(r * 16, 16), 16)
            stage[at, pl.ds(high * 2048 + half * 1024, 1024)] = total

        return give

    def out_tile(g):
        def body(i, _):
            cols = pl.ds(pl.multiple_of(i * 512, 512), 512)
            term = dot(att[g], wd[:, :, :, cols].reshape(256, 512)) + dot(
                act[g], ws[:, :, :, cols].reshape(1024, 512)
            )
            d_out[g, :, :, cols] = term.astype(low).reshape(4, BLOCK, 512)
            return 0

        return body

    def give_o(half):
        def give(high, r, total):
            rows = pl.ds(pl.multiple_of(high * 64 + r * 16, 16), 16)
            cols = pl.ds(half * 1024, 1024)
            add_bias = row_of(vec_rows, 80 + half * 8, 8) + row_of(vec_rows, 160 + half * 8, 8)
            out_ref[rows, cols] = (tokens_ref[rows, cols].astype(f32) + (total + add_bias)).astype(low)

        return give

    def norm_back():
        finish("n0", "n1")
        gain = row_of(vec_rows, 0, 16)
        vec_sum[...] = jnp.zeros_like(vec_sum)

        def chunk(r, _):
            rows = pl.ds(pl.multiple_of(r * 16, 16), 16)
            at = pl.ds(pl.multiple_of(lax.rem(r, 4) * 16, 16), 16)
            total = stage[at, pl.ds(pl.multiple_of((r // 4) * 2048, 2048), 2048)]
            xhat, spread = scaled(rows)
            e = total * gain
            mean_e = jnp.mean(e, axis=1, keepdims=True)
            mean_x = jnp.mean(e * xhat, axis=1, keepdims=True)
            dy = d_out_rows(rows, r * 16)
            ig_ref[rows, :] = (dy + spread * (e - mean_e - xhat * mean_x)).astype(low)
            for i, value in enumerate((total * xhat, total, dy)):
                vec_sum[i] += value[0:8] + value[8:16]
            return 0

        lax.fori_loop(0, 8, chunk, 0)
        vec_part[...] = jnp.zeros_like(vec_part)
        for i in range(3):
            total = jnp.sum(vec_sum[i], axis=0, keepdims=True)
            for k in range(8):
                vec_part[k, pl.ds(i, 1), :] = total[:, k * 256 : k * 256 + 256]

    def column_sums():
        ones = jnp.ones((8, 1024), low)
        vec_mine[...] = jnp.zeros_like(vec_mine)
        qkv_sum = dot(ones, qkv[...].reshape(1024, 768))
        for i in range(6):
            vec_mine[pl.ds(6 + i, 1), :] = qkv_sum[0:1, i * PAIR : (i + 1) * PAIR]
        pre_sum = dot(ones, d_pre[...].reshape(1024, 1024))
        for i in range(8):
            vec_mine[pl.ds(12 + i, 1), :] = pre_sum[0:1, i * PAIR : (i + 1) * PAIR]

    def loop(first, last, tile):
        return lambda: lax.fori_loop(first, last, tile, 0)

    tasks = {
        "vec_rows": vec_task, "norm_own": norm_own, "norm_sides": norm_sides, "norm_far": norm_far,
        "d_att": d_att_task, "qkv0": qkv_task(0), "qkv1": qkv_task(1), "grad_d": loop(0, 2, dense_tile),
        "grad_q0": loop(0, 2, qkv_grad_tile), "grad_q1": loop(2, 4, qkv_grad_tile),
        "grad_e0": loop(0, 4, expand_tile(0)), "grad_e1": loop(0, 4, expand_tile(1)),
        "grad_s0": loop(0, 2, shrink_tile(0)), "grad_s1": loop(0, 2, shrink_tile(1)),
        "norm_back": norm_back, "col_sums": column_sums,
    }
    for i in range(4):
        tasks["att" + str(i)] = loop(i, i + 1, attend_tile)
        tasks["up" + str(i)] = up_task(i)
    for half in range(2):
        for name, tile in (("down", down_tile), ("out", out_tile)):
            for at, g in (("a", 1 - c), ("b", c)):
                tasks[name + at + str(half)] = loop(2 * half, 2 * half + 2, tile(g))

    for name in SCHEDULE:
        if name in tasks:
            tasks[name]()
        else:
            advance(name)
    finish(*works)
    copies.finish()


def layer(tokens, cotangent, block_seq, seq_lengths, vectors, weights):
    low, f32 = jnp.bfloat16, jnp.float32
    vmem = pl.BlockSpec(memory_space=pltpu.VMEM)
    smem = pl.BlockSpec(memory_space=pltpu.SMEM)
    anywhere = pl.BlockSpec(memory_space=pl.ANY)
    turn = jnp.asarray(np.stack(rotary_constants())[:, : 3 * BLOCK])
    outs = [
        ((BLOCK, MODEL), low), ((BLOCK, MODEL), low), ((8, 16, 1024), low), ((8, 16, 768), low),
        ((16, MODEL), low), ((64, MODEL), f32), ((2, 4, 24, PAIR), f32),
    ]
    held = [
        ((4, 4, 128, 1024), low), ((4, 4, 128, 768), low), ((4, 4, 16, 2560), low),
        ((4, 4, 64, 2048), low), ((2, 4, 128, 2048), low), ((2, 4, 128, 2048), low),
        ((2, 512, 1024), low), ((2, 512, 1024), low), ((2, 512, 768), low), ((2, 512, 256), low),
        ((4, 4, 128, 1024), low), ((4, 4, 64, 1536), low), ((4, 4, 16, 2048), low),
        ((4, 4, 64, 2048), low), ((64, 8192), f32), ((8, 1024), f32),
        ((2, 4, 8, 128), f32), ((184, 128), f32),
        ((8, 16, 1024), low), ((8, 16, 768), low), ((16, 2048), low),
        ((2, 6, 4, 32, 1024), low), ((2, 6, 32, 1024), low),
        ((2, 6, 4, 16, 512), low), ((2, 6, 16, 512), low),
        ((2, 6, 4, 16, 2048), low), ((2, 6, 16, 2048), low),
        ((4, 128, 2048), low), ((6, 64, 2048), low),
        ((8, 16, 1024), low), ((8, 16, 768), low), ((16, 2048), low), ((8, 384), f32),
        ((3, 8, MODEL), f32), ((8, 8, 256), f32), ((8, 8, 256), f32), ((24, 128), f32),
        ((4, 4, 24, 128), f32),
    ]
    return pl.pallas_call(
        layer_kernel,
        in_specs=[vmem, vmem, smem, smem, vmem, vmem] + [anywhere] * 4,
        out_specs=[vmem] * 7,
        out_shape=[jax.ShapeDtypeStruct(s, k) for s, k in outs],
        scratch_shapes=[pltpu.VMEM(s, k) for s, k in held]
        + [
            pltpu.SemaphoreType.DMA((COPIES,)),
            pltpu.SemaphoreType.DMA((COPIES,)),
            pltpu.SemaphoreType.DMA((7,)),
            pltpu.SemaphoreType.REGULAR((2,)),
            pltpu.SemaphoreType.REGULAR((2,)),
            pltpu.SemaphoreType.REGULAR,
        ],
        compiler_params=pltpu.CompilerParams(
            collective_id=0, has_side_effects=True, vmem_limit_bytes=64 * 2**20
        ),
        name="layer",
    )(tokens, cotangent, block_seq, seq_lengths, vectors[None, :], turn, *weights)


def update_kernel(out_in, ig_in, ge, gq, gd, gs, vec, *refs):
    f32 = jnp.float32
    masters, moments, seconds = refs[0:5], refs[5:10], refs[10:15]
    out_ref, ig_ref = refs[15:17]
    results = [refs[17 + 3 * i : 20 + 3 * i] for i in range(5)]
    flat = refs[32]
    out_ref[...] = out_in[...]
    ig_ref[...] = ig_in[...]

    def update(i, at, gradient):
        grad_ref, state_ref, new_ref = results[i]
        grad_ref[at] = gradient
        state, new = adam_step(
            masters[i][at], moments[i][at], seconds[i][at], gradient, RATES[i], DECAYS[i]
        )
        state_ref[at] = state
        new_ref[at] = new

    every = slice(None)
    for s in range(3):
        for hi in range(2):
            for t in range(TPN):
                col = s * MODEL + hi * 1024 + t * PAIR
                piece = gq[t, :, pl.ds((2 * s + 1 - hi) * PAIR, PAIR)].astype(f32)
                update(0, (every, pl.ds(col, PAIR)), piece)
    for k in range(16):
        cols = (every, pl.ds(k * PAIR, PAIR))
        update(1, cols, gd[cols].astype(f32))
        for r in range(4):
            at = (pl.ds(16 * r, 16), pl.ds(k * PAIR, PAIR))
            update(3, at, gs[at])
    left = lax.broadcasted_iota(jnp.int32, (16, PAIR), 1) < HEAD
    for j in range(16):
        for k in range(4):
            first = ge[2 * k, :, pl.ds((j // 2) * PAIR, PAIR)].astype(f32)
            second = ge[2 * k + 1, :, pl.ds((j // 2) * PAIR, PAIR)].astype(f32)
            if j % 2 == 0:
                second = pltpu.roll(second, HEAD, 1)
            else:
                first = pltpu.roll(first, HEAD, 1)
            update(2, (every, pl.ds(j * 512 + k * PAIR, PAIR)), jnp.where(left, first, second))

    flat[...] = jnp.zeros_like(flat)
    left = lax.broadcasted_iota(jnp.int32, (1, PAIR), 1) < HEAD

    def line(t, row):
        return vec[t // 4, t % 4, pl.ds(row, 1), :]

    for t in range(TPN):
        for i in range(2):
            for row, base in ((0, 0), (1, 16), (2, 80), (2, 160)):
                flat[pl.ds(base + 2 * t + i, 1), :] = line(t, 2 * row + i)
        for s in range(3):
            for hi in range(2):
                at = 32 + s * 16 + hi * 8 + t
                flat[pl.ds(at, 1), :] = line(t, 6 + 2 * s + 1 - hi)
    for j in range(16):
        for k in range(4):
            first = line(2 * k, 12 + j // 2)
            second = line(2 * k + 1, 12 + j // 2)
            if j % 2 == 0:
                second = pltpu.roll(second, HEAD, 1)
            else:
                first = pltpu.roll(first, HEAD, 1)
            flat[pl.ds(96 + 4 * j + k, 1), :] = jnp.where(left, first, second)
    z, y, c, x = (lax.axis_index(a) for a in ALL)
    number = ((z * 4 + y) * 2 + c) * 4 + x
    first = (176 * number) // 128
    own = jnp.concatenate([flat[pl.ds(first + i, 1), :] for i in range(3)], axis=1)
    own = jnp.broadcast_to(own, (8, 3 * PAIR))
    own = pltpu.roll(own, lax.rem(3 * PAIR - 16 * lax.rem(3 * number, 8), 3 * PAIR), 1)
    update(4, (every, every), own[0:1, 0:176])


def update_all(parts, masters, moments, seconds):
    f32 = jnp.float32
    vmem = pl.BlockSpec(memory_space=pltpu.VMEM)
    shapes = [jax.ShapeDtypeStruct(p.shape, p.dtype) for p in parts[:2]]
    for w in masters:
        shapes += [jax.ShapeDtypeStruct(w.shape, f32)] * 3
    return pl.pallas_call(
        update_kernel,
        in_specs=[vmem] * 22,
        out_specs=[vmem] * 17,
        out_shape=shapes,
        scratch_shapes=[pltpu.VMEM((184, PAIR), f32)],
        compiler_params=pltpu.CompilerParams(vmem_limit_bytes=62 * 2**20),
        name="update",
    )(*parts, *masters, *moments, *seconds)


def adam_step(weight, moment, second, gradient, step_rate, step_decay):
    moment_new = BETA_ONE * moment + (1 - BETA_ONE) * gradient
    second_new = BETA_TWO * second + (1 - BETA_TWO) * gradient * gradient
    moment_hat = moment_new / (1 - BETA_ONE**STEP)
    second_hat = second_new / (1 - BETA_TWO**STEP)
    updated = weight - step_rate * (
        moment_hat / (jnp.sqrt(second_hat) + ADAM_EPS) + step_decay * weight
    )
    return (second_new, updated)


def shards(
    tokens, cotangent, block_seq, seq_lengths,
    qkv_weight, qkv_moment, qkv_second,
    dense_weight, dense_moment, dense_second,
    expand_weight, expand_moment, expand_second,
    shrink_weight, shrink_moment, shrink_second,
    vectors, vec_moment, vec_second,
):
    parts = layer(
        tokens,
        cotangent,
        block_seq,
        seq_lengths,
        vectors,
        (qkv_weight, dense_weight, expand_weight, shrink_weight),
    )
    masters = (qkv_weight, dense_weight, expand_weight, shrink_weight, vectors[None, :])
    moments = (qkv_moment, dense_moment, expand_moment, shrink_moment, vec_moment[None, :])
    seconds = (qkv_second, dense_second, expand_second, shrink_second, vec_second[None, :])
    results = update_all(parts, masters, moments, seconds)
    return (*results[:14], *(r[0] for r in results[14:]))


def solution(mesh):
    finer = Mesh(mesh.devices.reshape(*SIZES), ALL)
    whole, group = P(ALL, None), P(DP, None)
    return jax.shard_map(
        shards,
        mesh=finer,
        in_specs=(whole, whole, group, group, *[whole] * 12, *[P(ALL)] * 3),
        out_specs=(*[whole] * 14, *[P(ALL)] * 3),
        check_vma=False,
    )
```

```python
import functools

import jax
import jax.numpy as jnp
import numpy as np
from jax import lax
from jax.experimental import pallas as pl
from jax.experimental.pallas import tpu as pltpu
from jax.sharding import Mesh
from jax.sharding import PartitionSpec as P

HEAD = 64
ROT = 32
BLOCK = 128
STEP = 10
GROUP = 512
MODEL = 2048
FF = 8192
PAIR = 2 * HEAD
ALL = ("z", "y", "c", "x")
DP = ("z", "y", "c")
ZY = ("z", "y")
TP = ("c", "x")
SIZES = (4, 4, 2, 4)
TPN = 8
COPIES = 480
SCHEDULE = (
    "s", "vec", "to_d", "to_q", "d", "tok", "to_e", "q", "s", "cot", "vec_rows", "q", "tok",
    "q", "e", "q", "norm_own", "cot", "norm_sides", "q", "norm_far", "e", "d_att", "qkv0", "e",
    "qkv1", "s", "att0", "att1", "s", "e", "att2", "att3", "e", "s", "grad_q0", "grad_q1",
    "sum_q", "grad_d", "up0", "up1", "up2", "sum_q", "up3", "grad_e0", "sum_e0", "sum_q",
    "grad_e1", "downa1", "n1", "downb1", "sum_d", "sum_q", "sum_e1", "downa0", "n1", "downb0",
    "n0", "grad_s0", "back_q", "sum_e0", "sum_d", "n0", "sum_e1", "grad_s1", "outa0", "n1",
    "sum_d", "sum_s1", "sum_s0", "outa1", "col_sums", "sum_e1", "sum_d", "n0", "o1", "outb1",
    "norm_back", "vec_back", "back_d", "o1", "o0", "sum_e0", "outb0", "sum_s1", "o0", "sum_e1",
    "sum_s0", "back_e", "vec_back", "sum_s1", "sum_s0", "o0", "o1", "sum_s1", "sum_s0",
    "vec_back", "sum_s1",
)
SCALE = HEAD ** (-0.5)

NORM_EPS = 1e-05
MASKED = -1e30
BETA_ONE = 0.9
BETA_TWO = 0.999
ADAM_EPS = 1e-08
RATES = (0.02, 0.1, 0.02, 0.01, 0.4)
DECAYS = (0.1, 0.1, 0.1, 0.1, 0.0)
GELU_A = float(np.sqrt(2.0 / np.pi))
GELU_B = 0.044715


def dot(a, b):
    return jnp.dot(a, b, preferred_element_type=jnp.float32)


def dot_t(a, b):
    return lax.dot_general(a, b, (((1,), (1,)), ((), ())), preferred_element_type=jnp.float32)


def cross(a, b):
    return lax.dot_general(a, b, (((0,), (0,)), ((), ())), preferred_element_type=jnp.float32)


def rotary_constants():
    half = np.arange(ROT // 2, dtype=np.float32)
    inverse = (10000.0 ** (-2.0 * half.astype(np.float64) / ROT)).astype(np.float32)
    angle = (np.arange(GROUP, dtype=np.float32)[:, None] * inverse[None, :]).astype(np.float64)
    cosine, sine = np.cos(angle).astype(np.float32), np.sin(angle).astype(np.float32)
    one = np.ones((GROUP, HEAD - ROT), np.float32)
    zero = np.zeros((GROUP, ROT // 2), np.float32)
    rest = np.zeros((GROUP, HEAD - ROT), np.float32)
    turn = np.concatenate([cosine, cosine, one], axis=1)
    ahead = np.concatenate([-sine, zero, rest], axis=1)
    behind = np.concatenate([zero, sine, rest], axis=1)
    return tuple(np.concatenate([a, a], axis=1) for a in (turn, ahead, behind))


MESH = pl.DeviceIdType.MESH


def other(axis, step):
    size = SIZES[ALL.index(axis)]
    return lax.rem(lax.axis_index(axis) + step + size, size)


class Copy:
    def __init__(self, copy):
        self.copy, self.here, self.gone = copy, False, False

    def arrive(self):
        if not self.here:
            self.copy.wait_recv()
        self.here = True

    def leave(self):
        if not self.gone:
            self.copy.wait_send()
        self.gone = True


class Copies:
    def __init__(self, send, recv):
        self.send, self.recv, self.all = send, recv, []

    def start(self, src, dst, to):
        at = len(self.all)
        copy = pltpu.make_async_remote_copy(
            src_ref=src,
            dst_ref=dst,
            send_sem=self.send.at[at],
            recv_sem=self.recv.at[at],
            device_id=to,
            device_id_type=MESH,
        )
        copy.start()
        self.all.append(Copy(copy))
        return self.all[-1]

    def finish(self):
        for copy in self.all:
            copy.leave()


def greet():
    barrier = pltpu.get_barrier_semaphore()
    for partner in token_partners() + weight_partners() + [dense_partner()]:
        pl.semaphore_signal(barrier, inc=1, device_id=partner, device_id_type=MESH)


def enter():
    pl.semaphore_wait(pltpu.get_barrier_semaphore(), 23)


def token_partners():
    return [{"c": other("c", i), "x": other("x", j)} for i in range(2) for j in range(4) if i + j]


def weight_partners():
    return [{"z": other("z", i), "y": other("y", j)} for i in range(4) for j in range(4) if i + j]


def dense_partner():
    z, y, c, x = (lax.axis_index(a) for a in ALL)
    return {"z": (1 - z // 2) * 2 + c, "y": x, "c": lax.rem(z, 2), "x": y}


def gather_weights(copies, view):
    z, y = lax.axis_index("z"), lax.axis_index("y")
    z_up, z_down, y_up, y_down = other("z", 1), other("z", -1), other("y", 1), other("y", -1)
    z_far, y_far = other("z", 2), other("y", 2)
    up, down, far, near = {"y": y_up}, {"y": y_down}, {"z": z_up}, {"z": z_down}

    def go(block, to):
        return copies.start(block, block, to)

    a_up, a_down = go(view(z, y, 4), up), go(view(z, y, 4), down)
    b_up, b_down = go(view(z, y, 5), far), go(view(z, y, 5), near)
    a_own = go(view(z, y, 4), far), go(view(z, y, 4), near)
    b_own = go(view(z, y, 5), up), go(view(z, y, 5), down)
    yield
    a_up.arrive()
    a_low = go(view(z, y_down, 0), up)
    b_up.arrive()
    b_low = go(view(z_down, y, 2), far)
    a_down.arrive()
    a_high = go(view(z, y_up, 1), down)
    b_down.arrive()
    b_high = go(view(z_up, y, 3), near)
    a_side = [(i, go(view(z, i, 4), far), go(view(z, i, 4), near)) for i in (y_down, y_up)]
    b_side = [(i, go(view(i, y, 5), up), go(view(i, y, 5), down)) for i in (z_down, z_up)]
    yield
    last = []
    a_own[0].arrive()
    last.append(go(view(z_down, y, 0), far))
    b_own[0].arrive()
    last.append(go(view(z, y_down, 2), up))
    a_own[1].arrive()
    last.append(go(view(z_up, y, 1), near))
    b_own[1].arrive()
    last.append(go(view(z, y_up, 3), down))
    a_low.arrive()
    a_high.arrive()
    a_side.append((y_far, go(view(z, y_far, 4), far), go(view(z, y_far, 4), near)))
    b_low.arrive()
    b_high.arrive()
    b_side.append((z_far, go(view(z_far, y, 5), up), go(view(z_far, y, 5), down)))
    for k in range(3):
        if k != 1:
            yield
        i, first, second = a_side[k]
        first.arrive()
        last.append(go(view(z_down, i, 0), far))
        second.arrive()
        last.append(go(view(z_up, i, 1), near))
        i, first, second = b_side[k]
        first.arrive()
        last.append(go(view(i, y_down, 2), up))
        second.arrive()
        last.append(go(view(i, y_up, 3), down))
    yield
    for copy in last:
        copy.arrive()


def gather_tokens(copies, ref, sent):
    c, x, across = lax.axis_index("c"), lax.axis_index("x"), other("c", 1)
    right, left = {"x": other("x", 1)}, {"x": other("x", -1)}

    def go(block, to):
        return copies.start(block, block, to)

    own = ref.at[c, x]
    sent.append([go(own, right), go(own, left), go(own, {"c": across})])
    yield
    sent[0][0].arrive()
    last = [go(ref.at[c, other("x", -1), pl.ds(0, 64)], right)]
    side = [go(ref.at[c, other("x", -1)], {"c": across})]
    sent[0][1].arrive()
    last.append(go(ref.at[c, other("x", 1), pl.ds(64, 64)], left))
    side.append(go(ref.at[c, other("x", 1)], {"c": across}))
    sent.append(last + side)
    yield
    for copy in last:
        copy.arrive()
    sent.append([go(ref.at[c, other("x", 2)], {"c": across})])
    yield
    for copies_of_stage in sent:
        for copy in copies_of_stage:
            copy.arrive()
            copy.leave()


def gather_vectors(copies, group, rows, place):
    c, x = lax.axis_index("c"), lax.axis_index("x")
    sent = [copies.start(group.at[c, x], group.at[c, x], to) for to in token_partners()]
    yield
    for copy in sent:
        copy.arrive()
    rows[pl.ds(0, 16), :] = jnp.zeros((16, PAIR), jnp.float32)
    for d in range(TPN):
        rows[pl.ds((176 * d) // PAIR, 3), :] += group[d // 4, d % 4, pl.ds(0, 3), :]
    place[:, pl.ds(0, PAIR)] = rows[pl.ds(0, 16), :].astype(jnp.bfloat16)
    place[:, pl.ds(PAIR, 3 * PAIR)] = jnp.zeros((16, 3 * PAIR), jnp.bfloat16)


def expand_to_group(copies, send, ref, width):
    z, y, c, x = (lax.axis_index(a) for a in ALL)
    rows = pl.ds(pl.multiple_of((c * 4 + x) * 16, 16), 16)
    sent = []
    for to in token_partners():
        sent.append(copies.start(send.at[to["c"] * 4 + to["x"]], ref.at[z, y, rows], to))
    ref[z, y, rows] = send[c * 4 + x]
    yield
    for copy in sent:
        copy.arrive()


def by_rows(ref, rows):
    quarter = rows // 4

    def view(z, y, part):
        start, size = (part * quarter, quarter) if part < 4 else ((part - 4) * 2 * quarter, 2 * quarter)
        return ref.at[z, y, pl.ds(start, size)]

    return view


def by_columns(ref, columns):
    quarter = columns // 4

    def view(z, y, part):
        start, size = (part * quarter, quarter) if part < 4 else ((part - 4) * 2 * quarter, 2 * quarter)
        return ref.at[z, y, :, pl.ds(start, size)]

    return view


def step(*works):
    for work in works:
        next(work, None)


def row_of(ref, first, count):
    return jnp.concatenate([ref[pl.ds(first + i, 1), :] for i in range(count)], axis=1)


def ring_sum(copies, axis, block, land, low_part, high_part):
    ahead, behind = other(axis, 1), other(axis, -1)
    up, down = {axis: ahead}, {axis: behind}
    far = other(axis, 2)
    t_low = copies.start(block(far, low_part), land.at[0], up)
    t_high = copies.start(block(far, high_part), land.at[1], down)
    d_high = copies.start(block(ahead, high_part), land.at[3], up)
    d_low = copies.start(block(behind, low_part), land.at[2], down)
    yield
    t_low.arrive()
    land[0] = land[0] + block(ahead, low_part)[...]
    p_low = copies.start(land.at[0], land.at[4], up)
    t_high.arrive()
    land[1] = land[1] + block(behind, high_part)[...]
    p_high = copies.start(land.at[1], land.at[5], down)
    yield
    for copy in (d_low, d_high, p_low, p_high):
        copy.arrive()
    for copy in (t_low, t_high, d_low, d_high, p_low, p_high):
        copy.leave()


def three(own, land, high, at=...):
    f32 = jnp.float32
    first, second = land.at[4 + high], land.at[2 + high]
    return own[at].astype(f32) + first[at].astype(f32) + second[at].astype(f32)


def both(first, second):
    while True:
        done = [next(first, 0), next(second, 0)]
        if 0 in done:
            return
        yield


def scatter_weights(copies, view, wide, narrow, give):
    z, y = lax.axis_index("z"), lax.axis_index("y")
    every = slice(None)
    low = jnp.bfloat16
    yield from both(
        ring_sum(copies, "y", lambda i, p: view(every, i, p), wide.at[0], 0, 1),
        ring_sum(copies, "z", lambda i, p: view(i, every, p), wide.at[1], 2, 3),
    )
    for high in range(2):
        own = view(every, y, high)
        for i in range(4):
            own[i] = three(own, wide.at[0], high, i).astype(low)
        own = view(z, every, 2 + high)
        for i in range(4):
            own[i] = three(own, wide.at[1], high, i).astype(low)
    yield from both(
        ring_sum(copies, "z", lambda i, p: view(i, y, p), narrow.at[0], 0, 1),
        ring_sum(copies, "y", lambda i, p: view(z, i, p), narrow.at[1], 2, 3),
    )
    for high in range(2):
        give(high, three(view(z, y, high), narrow.at[0], high))
        give(2 + high, three(view(z, y, 2 + high), narrow.at[1], high))


def scatter_tokens(copies, ref, core_land, land, give, core_free, ring_free, first):
    c, x, across = lax.axis_index("c"), lax.axis_index("x"), other("c", 1)
    if not first:
        pl.semaphore_wait(core_free, 1)
    came = copies.start(ref.at[across], core_land, {"c": across})
    yield
    came.arrive()
    for i in range(4):
        ref[c, i] = ref[c, i] + core_land[i]
    if first:
        pl.semaphore_signal(core_free, inc=1, device_id={"c": across}, device_id_type=MESH)
    else:
        pl.semaphore_wait(ring_free, 2)
    yield from ring_sum(copies, "x", lambda i, p: ref.at[c, i, pl.ds(p * 64, 64)], land, 0, 1)
    for high in range(2):
        own = ref.at[c, x, pl.ds(high * 64, 64)]

        def chunk(r, _):
            rows = pl.ds(pl.multiple_of(r * 16, 16), 16)
            give(high, r, three(own, land, high, rows))
            return 0

        lax.fori_loop(0, 4, chunk, 0)
    if first:
        for way in (1, -1):
            to = {"x": other("x", way)}
            pl.semaphore_signal(ring_free, inc=1, device_id=to, device_id_type=MESH)


def landed(copy):
    yield
    copy.arrive()


def sum_vectors(copies, part, came, mine, zy, out):
    z, y, c, x = (lax.axis_index(a) for a in ALL)
    t = c * 4 + x
    sent = [
        copies.start(part.at[to["c"] * 4 + to["x"]], came.at[t], to) for to in token_partners()
    ]
    came[t] = part[t]
    yield
    for copy in sent:
        copy.arrive()
    total = jnp.sum(came[...], axis=0)
    for i in range(6):
        mine[pl.ds(i, 1), :] = total[i // 2 : i // 2 + 1, (i % 2) * PAIR : (i % 2 + 1) * PAIR]
    zy[z, y] = mine[...]
    sent = [copies.start(mine, zy.at[z, y], to) for to in weight_partners()]
    yield
    for copy in sent:
        copy.arrive()
    out[c, x] = jnp.sum(zy[...].reshape(16, 24, PAIR), axis=0)
    sent = [copies.start(out.at[c, x], out.at[c, x], to) for to in token_partners()]
    yield
    for copy in sent:
        copy.arrive()


def return_to_group(copies, ref, out):
    c, x = lax.axis_index("c"), lax.axis_index("x")
    t = c * 4 + x
    sent = []
    for to in token_partners():
        sent.append(copies.start(ref.at[to["c"] * 4 + to["x"]], out.at[t], to))
    out[t] = ref[t]
    yield
    for copy in sent:
        copy.arrive()


def turned(values, table, sign):
    turn, ahead, behind = table
    up = pltpu.roll(values, PAIR - ROT // 2, 1)
    down = pltpu.roll(values, ROT // 2, 1)
    if sign > 0:
        return values * turn + up * ahead + down * behind
    return values * turn - up * ahead - down * behind


def attend(meta, turn_ref, qkv, att, g, p):
    low, f32 = jnp.bfloat16, jnp.float32
    lane = lax.broadcasted_iota(jnp.int32, (BLOCK, PAIR), 1)
    first = lane < HEAD
    zero = jnp.zeros((BLOCK, PAIR), low)
    row_at = lax.broadcasted_iota(jnp.int32, (BLOCK, BLOCK), 0)
    col_at = lax.broadcasted_iota(jnp.int32, (BLOCK, BLOCK), 1)
    cols = [pl.ds(pl.multiple_of(i * 2 * PAIR + p * PAIR, PAIR), PAIR) for i in range(3)]
    d_k = [jnp.zeros((BLOCK, PAIR), f32) for _ in range(4)]
    d_v = [jnp.zeros((BLOCK, PAIR), f32) for _ in range(4)]
    held = [qkv[g, :, cols[i]] for i in range(3)] + [att[g, :, cols[0]]]
    done = []
    for b in range(4):
        rows, width = slice(b * BLOCK, (b + 1) * BLOCK), (b + 1) * BLOCK
        base = meta[:, 4 + b : 5 + b] * BLOCK
        diagonal = (col_at <= row_at) & (col_at.astype(f32) + base < meta[:, 8 + b : 9 + b])
        bias = [
            jnp.where(meta[:, e : e + 1] == meta[:, b : b + 1], 0.0, MASKED)
            + jnp.zeros((BLOCK, BLOCK), f32)
            for e in range(b)
        ]
        bias.append(jnp.where(diagonal, 0.0, MASKED).astype(f32))
        bias = bias[0] if b == 0 else jnp.concatenate(bias, axis=1)
        q, da, k, v = held[0][rows], held[3][rows], held[1][:width], held[2][:width]
        qs = jnp.concatenate([jnp.where(first, q, zero), jnp.where(first, zero, q)], axis=0)
        das = jnp.concatenate([jnp.where(first, da, zero), jnp.where(first, zero, da)], axis=0)
        scores = dot_t(qs, k) + jnp.concatenate([bias, bias], axis=0)
        w = jnp.exp(scores - jnp.max(scores, axis=1, keepdims=True))
        prob = w * (1.0 / jnp.sum(w, axis=1, keepdims=True))
        prob_low = prob.astype(low)
        summed = dot(prob_low, v)
        dp = dot_t(das, v)
        ds = (prob * (dp - jnp.sum(prob * dp, axis=1, keepdims=True))).astype(low)
        dq = dot(ds, k)
        dq = jnp.where(first, dq[:BLOCK], dq[BLOCK:]) * SCALE
        dq = turned(dq, table_of(meta, turn_ref, b), -1).astype(low)
        done.append((jnp.where(first, summed[:BLOCK], summed[BLOCK:]).astype(low), dq))
        dk = cross(ds, qs)
        dv = cross(prob_low, das)
        for e in range(b + 1):
            d_k[e] = d_k[e] + dk[e * BLOCK : (e + 1) * BLOCK]
            d_v[e] = d_v[e] + dv[e * BLOCK : (e + 1) * BLOCK]
    for b in range(4):
        rows = pl.ds(b * BLOCK, BLOCK)
        att[g, rows, cols[0]], qkv[g, rows, cols[0]] = done[b]
        qkv[g, rows, cols[1]] = turned(d_k[b], table_of(meta, turn_ref, b), -1).astype(low)
        qkv[g, rows, cols[2]] = d_v[b].astype(low)


def table_of(meta, turn_ref, b):
    rank = meta[:, 4 + b : 5 + b]
    parts = [turn_ref[:, pl.ds(r * BLOCK, BLOCK), :] for r in range(3)]
    table = jnp.where((rank == 0.0)[None], parts[0], jnp.where((rank == 1.0)[None], parts[1], parts[2]))
    return table[0], table[1], table[2]


def layer_kernel(
    tokens_ref, cot_ref, seq_ref, length_ref, vec_ref, turn_ref, q_hbm, d_hbm, e_hbm, s_hbm,
    out_ref, ig_ref, ge_out, gq_out, gd_out, gs_out, vec_out,
    we, wq, wd, ws, normed, d_out, act, d_pre, qkv, att,
    ge, gq, gd, gs, stage, bias_e, vec_group, vec_rows, we_send, wq_send, wd_own,
    wide_e, narrow_e, wide_d, narrow_d, wide_s, narrow_s,
    core_land, ring_land, res_e, res_q, res_d,
    vec_line, vec_sum, vec_part, vec_came, vec_mine, vec_zy,
    send, recv, local, core_free, ring_free, wide_free,
):
    low, f32 = jnp.bfloat16, jnp.float32
    z, y, c, x = (lax.axis_index(a) for a in ALL)
    t = c * 4 + x
    copies = Copies(send, recv)
    greet()

    loads = [
        pltpu.make_async_copy(q_hbm, stage.at[pl.ds(16, 16), pl.ds(0, 6144)], local.at[0]),
        pltpu.make_async_copy(d_hbm, stage.at[pl.ds(16, 16), pl.ds(6144, 2048)], local.at[1]),
        pltpu.make_async_copy(e_hbm, stage.at[pl.ds(0, 16)], local.at[2]),
    ]
    for k in range(4):
        rows = pl.ds(16 * k, 16)
        place = stage.at[pl.ds(32, 16), pl.ds(2048 * k, 2048)]
        loads.append(pltpu.make_async_copy(s_hbm.at[rows], place, local.at[3 + k]))
    for load in loads:
        load.start()

    lane = lax.broadcasted_iota(jnp.int32, (1, PAIR), 1)
    seqs = [seq_ref[0, b] for b in range(4)]
    own_meta = jnp.zeros((1, PAIR), f32)
    own_rank, own_limit = jnp.zeros((1, 1), f32), jnp.zeros((1, 1), f32)
    for b in range(4):
        rank = jnp.int32(0)
        for e in range(b):
            rank = rank + jnp.where(seqs[e] == seqs[b], 1, 0)
        limit = jnp.where(seqs[b] == 0, length_ref[0, 0], length_ref[0, 1])
        for at, value in ((b, seqs[b]), (4 + b, rank), (8 + b, limit)):
            own_meta = jnp.where(lane == at, value.astype(f32), own_meta)
        own_rank = jnp.where(x == b, rank.astype(f32), own_rank)
        own_limit = jnp.where(x == b, limit.astype(f32), own_limit)
    vec_line[...] = jnp.zeros_like(vec_line)
    vec_line[pl.ds(0, 1), pl.ds(0, 176)] = vec_ref[...].astype(low).astype(f32)
    line = pltpu.roll(vec_line[...], 16 * lax.rem(3 * t + 24 * (z * 4 + y), 8), 1)
    vec_own = vec_group.at[c, x]
    vec_own[...] = jnp.zeros((8, PAIR), f32)
    for k in range(3):
        vec_own[pl.ds(k, 1), :] = line[0:1, k * PAIR : (k + 1) * PAIR]
    vec_own[pl.ds(4, 1), :] = own_meta

    def d_out_rows(rows, first):
        row_at = lax.broadcasted_iota(jnp.int32, (16, 1), 0) + first
        live = (row_at.astype(f32) + own_rank * BLOCK < own_limit).astype(f32)
        return cot_ref[rows, :].astype(f32) * live

    def mask_chunk(r, _):
        rows = pl.ds(pl.multiple_of(r * 16, 16), 16)
        d_out[c, x, rows] = d_out_rows(rows, r * 16).astype(low)
        return 0


    def scaled(rows):
        values = tokens_ref[rows, :].astype(f32)
        middle = values - jnp.mean(values, axis=1, keepdims=True)
        spread = lax.rsqrt(jnp.mean(middle * middle, axis=1, keepdims=True) + NORM_EPS)
        return middle * spread, spread

    def scale_chunk(r, _):
        rows = pl.ds(pl.multiple_of(r * 16, 16), 16)
        normed[c, x, rows] = scaled(rows)[0].astype(low)
        return 0

    lax.fori_loop(0, 8, scale_chunk, 0)
    loads[0].wait()
    for k in range(8):
        for i in range(6):
            col = (i // 2) * 2048 + (1 - i % 2) * 1024 + k * PAIR
            piece = stage[pl.ds(16, 16), pl.ds(col, PAIR)]
            wq_send[k, :, pl.ds(i * PAIR, PAIR)] = piece.astype(low)
    enter()

    def cast_dense():
        loads[1].wait()
        wd_own[...] = stage[pl.ds(16, 16), pl.ds(6144, 2048)].astype(low)

    def cast_expand():
        left16 = lax.broadcasted_iota(jnp.int32, (16, PAIR), 1) < HEAD
        loads[2].wait()
        for j in range(8):
            for k in range(4):
                first = stage[pl.ds(0, 16), pl.ds(j * 1024 + k * PAIR, PAIR)]
                second = stage[pl.ds(0, 16), pl.ds(j * 1024 + 512 + k * PAIR, PAIR)]
                even = jnp.where(left16, first, pltpu.roll(second, HEAD, 1))
                odd = jnp.where(left16, pltpu.roll(first, HEAD, 1), second)
                we_send[2 * k, :, pl.ds(j * PAIR, PAIR)] = even.astype(low)
                we_send[2 * k + 1, :, pl.ds(j * PAIR, PAIR)] = odd.astype(low)

    def cast_shrink():
        for k in range(4):
            loads[3 + k].wait()
            ws[z, y, pl.ds(16 * k, 16)] = stage[pl.ds(32, 16), pl.ds(2048 * k, 2048)].astype(low)

    works, stages, tasks, finished = {}, {}, {}, set()
    token_sends = []

    def finish(*names):
        for name in names:
            for _ in works[name]:
                pass
            finished.add(name)

    def advance(name):
        if name not in works:
            works[name], stages[name] = begin(name), 0
        stages[name] += 1
        if next(works[name], 0) == 0:
            finished.add(name)

    def reach(name, stage):
        while stages[name] < stage:
            advance(name)

    def begin(name):
        if name == "vec":
            return gather_vectors(copies, vec_group, vec_rows, wd.at[z, y, :, pl.ds(MODEL, 512)])
        if name == "to_q":
            return expand_to_group(copies, wq_send, wq, 768)
        if name == "to_e":
            cast_expand()
            return expand_to_group(copies, we_send, we, 1024)
        if name == "to_d":
            cast_dense()
            there = dense_partner()
            place = wd.at[there["z"], there["y"], :, pl.ds(0, MODEL)]
            return landed(copies.start(wd_own, place, there))
        if name == "q":
            finish("to_q")
            return gather_weights(copies, by_rows(wq, 128))
        if name == "d":
            finish("to_d", "vec")
            return gather_weights(copies, by_columns(wd, 2560))
        if name == "e":
            finish("to_e")
            return gather_weights(copies, by_rows(we, 128))
        if name == "s":
            cast_shrink()
            return gather_weights(copies, by_rows(ws, 64))
        if name == "cot":
            lax.fori_loop(0, 8, mask_chunk, 0)
            return gather_tokens(copies, d_out, [])
        if name == "tok":
            return gather_tokens(copies, normed, token_sends)
        if name == "sum_d":
            return scatter_weights(copies, by_columns(gd, 2048), wide_d, narrow_d, give_d)
        if name == "sum_q":
            return sum_q()
        if name in ("sum_e0", "sum_e1"):
            half = int(name[-1])
            cols = pl.ds(half * 512, 512)
            return scatter_weights(
                copies,
                by_rows(ge.at[:, :, :, cols], 128),
                wide_e.at[:, :, :, :, cols],
                narrow_e.at[:, :, :, cols],
                give_e(half),
            )
        if name in ("sum_s0", "sum_s1"):
            finish("sum_q")
            if "wide" not in finished:
                pl.semaphore_wait(wide_free, 4)
                finished.add("wide")
            half = int(name[-1])
            cols = pl.ds(half * 1024, 1024)
            return scatter_weights(
                copies,
                by_rows(gs.at[:, :, :, cols], 64),
                wide_s.at[:, :, :, :, cols],
                narrow_s.at[:, :, :, cols],
                give_s(half),
            )
        if name in ("n0", "n1", "o0", "o1"):
            half = int(name[-1])
            if name[0] == "o":
                finish("n" + name[1])
            cols = pl.ds(half * 1024, 1024)
            return scatter_tokens(
                copies,
                (normed if name[0] == "n" else d_out).at[:, :, :, cols],
                core_land.at[:, :, cols],
                ring_land.at[:, :, cols],
                (give_n if name[0] == "n" else give_o)(half),
                core_free.at[half],
                ring_free.at[half],
                name[0] == "n",
            )
        if name == "back_q":
            finish("sum_q")
            return return_to_group(copies, res_q, gq_out)
        if name == "back_e":
            finish("sum_e0", "sum_e1")
            return return_to_group(copies, res_e, ge_out)
        if name == "back_d":
            finish("sum_d")
            return landed(copies.start(res_d, gd_out, dense_partner()))
        return sum_vectors(copies, vec_part, vec_came, vec_mine, vec_zy, vec_out)

    def vec_task():
        finish("d")
        for i in range(16):
            block = wd[i // 4, i % 4, :, pl.ds(MODEL, PAIR)].astype(f32)
            vec_rows[pl.ds(11 * i, 11), :] = block[0:11]

    def norm_blocks(blocks):
        def chunk(r, _):
            rows = pl.ds(pl.multiple_of(r * 16, 16), 16)
            for core, chip in blocks:
                xhat = normed[core, chip, rows].astype(f32)
                whole = xhat * row_of(vec_rows, 0, 16) + row_of(vec_rows, 16, 16)
                normed[core, chip, rows] = whole.astype(low)
            return 0

        lax.fori_loop(0, 8, chunk, 0)

    def norm_own():
        reach("tok", 2)
        for copy in token_sends[0]:
            copy.leave()
        token_sends[0][2].arrive()
        norm_blocks([(c, x), (1 - c, x)])

    def norm_sides():
        reach("tok", 3)
        for copy in token_sends[1]:
            copy.leave()
        for copy in token_sends[1][2:]:
            copy.arrive()
        for way in (-1, 1):
            norm_blocks([(c, other("x", way)), (1 - c, other("x", way))])

    def norm_far():
        finish("tok")
        token_sends[2][0].leave()
        norm_blocks([(c, other("x", 2)), (1 - c, other("x", 2))])

    def qkv_tile(g, _):
        meta = vec_group[g, x, pl.ds(4, 1), :]
        projected = dot(normed[g].reshape(512, MODEL), wq[...].reshape(MODEL, 768))
        for p in range(6):
            bias = vec_rows[pl.ds(32 + (p // 2) * 16 + (1 - p % 2) * 8 + t, 1), :]
            for b in range(4):
                rows = pl.ds(b * BLOCK, BLOCK)
                part = projected[b * BLOCK : (b + 1) * BLOCK, p * PAIR : (p + 1) * PAIR] + bias
                if p < 4:
                    part = turned(part, table_of(meta, turn_ref, b), 1)
                part = part.astype(low)
                if p < 2:
                    part = part * jnp.asarray(SCALE, low)
                qkv[g, rows, pl.ds(p * PAIR, PAIR)] = part
        return 0

    def d_att_tile(g, _):
        dense = wd[:, :, :, pl.ds(0, MODEL)].reshape(256, MODEL)
        att[g] = dot_t(d_out[g].reshape(512, MODEL), dense).astype(low)
        return 0

    def d_att_task():
        finish("cot", "d")
        lax.fori_loop(0, 2, d_att_tile, 0)

    def qkv_task(g):
        def task():
            finish("tok", "q")
            lax.fori_loop(g, g + 1, qkv_tile, 0)

        return task

    def attend_tile(i, _):
        g, p = i // 2, lax.rem(i, 2)
        attend(vec_group[g, x, pl.ds(4, 1), :], turn_ref, qkv, att, g, p)
        return 0

    def dense_tile(n, _):
        cols = pl.ds(pl.multiple_of(n * 1024, 1024), 1024)
        term = cross(att[...].reshape(1024, 256), d_out[:, :, :, cols].reshape(1024, 1024))
        gd[:, :, :, cols] = term.astype(low).reshape(4, 4, 16, 1024)
        return 0

    def give_d(part, total):
        res_d[:, pl.ds(part * 512, 512)] = total.astype(low)

    def qkv_grad_tile(i, _):
        mine = normed[:, :, :, pl.ds(pl.multiple_of(i * 512, 512), 512)].reshape(1024, 512)
        term = cross(mine, qkv[...].reshape(1024, 768)).astype(low).reshape(4, BLOCK, 768)
        gq[i, :, :, pl.ds(0, 768)] = term[:, :64]
        gq[i, :, :, pl.ds(768, 768)] = term[:, 64:]
        return 0

    def give_q(part, total):
        res_q[part] = total[:, :768].astype(low)
        res_q[4 + part] = total[:, 768:].astype(low)

    def sum_q():
        short = pl.ds(0, 1536)
        yield from scatter_weights(
            copies,
            by_rows(gq, 64),
            wide_s.at[:, :, :, :, short],
            narrow_s.at[:, :, :, short],
            give_q,
        )
        for axis in ("y", "z"):
            for way in (1, -1):
                to = {axis: other(axis, way)}
                pl.semaphore_signal(wide_free, inc=1, device_id=to, device_id_type=MESH)

    def up_tile(i, _):
        g, n = i // 2, lax.rem(i, 2)
        cols = pl.ds(pl.multiple_of(n * 512, 512), 512)
        pre_term = dot(normed[g].reshape(512, MODEL), we[:, :, :, cols].reshape(MODEL, 512))
        for k in range(8):
            stage[:, pl.ds(k * 512, 512)] = pre_term[k * 64 : k * 64 + 64]
        act_term = dot_t(d_out[g].reshape(512, MODEL), ws[pl.ds(2 * n, 2)].reshape(512, MODEL))
        for k in range(8):
            stage[:, pl.ds(4096 + k * 512, 512)] = act_term[k * 64 : k * 64 + 64]

        def chunk(r, _):
            rows = pl.ds(pl.multiple_of(r * 16, 16), 16)
            at = pl.ds(pl.multiple_of(lax.rem(r, 4) * 16, 16), 16)
            across = r // 4
            pre = stage[at, pl.ds(pl.multiple_of(across * 512, 512), 512)]
            pre = pre + bias_e[pl.ds(0, 1), cols]
            square = pre * pre
            inner = jnp.tanh(GELU_A * (pre + GELU_B * (square * pre)))
            cover = 0.5 + 0.5 * inner
            act[g, rows, cols] = (pre * cover).astype(low)
            slope = cover + 0.5 * pre * (1.0 - inner * inner) * (
                GELU_A + (3.0 * GELU_A * GELU_B) * square
            )
            d_act = stage[at, pl.ds(pl.multiple_of(4096 + across * 512, 512), 512)]
            d_pre[g, rows, cols] = (d_act * slope).astype(low)
            return 0

        lax.fori_loop(0, 32, chunk, 0, unroll=4)
        return 0

    def up_bias():
        odd = lax.rem(t, 2) == 1
        half = t // 2
        left = lane < HEAD
        bias_e[...] = jnp.zeros_like(bias_e)
        for j in range(8):
            r0 = vec_rows[pl.ds(96 + 8 * j + half, 1), :]
            r1 = vec_rows[pl.ds(100 + 8 * j + half, 1), :]
            even_row = jnp.where(left, r0, pltpu.roll(r1, HEAD, 1))
            odd_row = jnp.where(left, pltpu.roll(r0, HEAD, 1), r1)
            bias_e[pl.ds(0, 1), pl.ds(j * PAIR, PAIR)] = jnp.where(odd, odd_row, even_row)

    def up_task(i):
        def task():
            finish("e", "s")
            if i == 0:
                up_bias()
            lax.fori_loop(i, i + 1, up_tile, 0)

        return task

    def expand_tile(half):
        cols = pl.ds(half * 512, 512)

        def body(i, _):
            mine = normed[:, :, :, pl.ds(pl.multiple_of(i * 1024, 1024), 1024)].reshape(1024, 1024)
            term = cross(mine, d_pre[:, :, cols].reshape(1024, 512))
            ge[pl.ds(2 * i, 2), :, :, cols] = term.astype(low).reshape(2, 4, BLOCK, 512)
            return 0

        return body

    def give_e(half):
        def give(part, total):
            cols = pl.ds(half * 512, 512)
            res_e[pl.ds(2 * part, 2), :, cols] = total.astype(low).reshape(2, 16, 512)

        return give

    def shrink_tile(half):
        cols = pl.ds(half * 1024, 1024)

        def body(j, _):
            mine = act[:, :, pl.ds(pl.multiple_of(j * 512, 512), 512)].reshape(1024, 512)
            term = cross(mine, d_out[:, :, :, cols].reshape(1024, 1024))
            gs[pl.ds(2 * j, 2), :, :, cols] = term.astype(low).reshape(2, 4, 64, 1024)
            return 0

        return body

    def give_s(half):
        def give(part, total):
            gs_out[pl.ds(part * 16, 16), pl.ds(half * 1024, 1024)] = total

        return give

    def down_task(g, half):
        def task():
            term = dot_t(qkv[g], wq[2 * half : 2 * half + 2].reshape(1024, 768)) + dot_t(
                d_pre[g], we[2 * half : 2 * half + 2].reshape(1024, 1024)
            )
            cols = pl.ds(half * 1024, 1024)
            normed[g, :, :, cols] = term.astype(low).reshape(4, BLOCK, 1024)

        return task

    def give_n(half):
        def give(high, r, total):
            at = pl.ds(pl.multiple_of(r * 16, 16), 16)
            stage[at, pl.ds(high * 2048 + half * 1024, 1024)] = total

        return give

    def out_task(g, half):
        def task():
            cols = pl.ds(half * 1024, 1024)
            term = dot(att[g], wd[:, :, :, cols].reshape(256, 1024)) + dot(
                act[g], ws[:, :, :, cols].reshape(1024, 1024)
            )
            d_out[g, :, :, cols] = term.astype(low).reshape(4, BLOCK, 1024)

        return task

    def give_o(half):
        def give(high, r, total):
            rows = pl.ds(pl.multiple_of(high * 64 + r * 16, 16), 16)
            cols = pl.ds(half * 1024, 1024)
            add_bias = row_of(vec_rows, 80 + half * 8, 8) + row_of(vec_rows, 160 + half * 8, 8)
            out_ref[rows, cols] = (tokens_ref[rows, cols].astype(f32) + (total + add_bias)).astype(low)

        return give

    def norm_back():
        finish("n0", "n1")
        gain = row_of(vec_rows, 0, 16)
        vec_sum[...] = jnp.zeros_like(vec_sum)

        def chunk(r, _):
            rows = pl.ds(pl.multiple_of(r * 16, 16), 16)
            at = pl.ds(pl.multiple_of(lax.rem(r, 4) * 16, 16), 16)
            total = stage[at, pl.ds(pl.multiple_of((r // 4) * 2048, 2048), 2048)]
            xhat, spread = scaled(rows)
            e = total * gain
            mean_e = jnp.mean(e, axis=1, keepdims=True)
            mean_x = jnp.mean(e * xhat, axis=1, keepdims=True)
            dy = d_out_rows(rows, r * 16)
            ig_ref[rows, :] = (dy + spread * (e - mean_e - xhat * mean_x)).astype(low)
            for i, value in enumerate((total * xhat, total, dy)):
                vec_sum[i] += value[0:8] + value[8:16]
            return 0

        lax.fori_loop(0, 8, chunk, 0)
        vec_part[...] = jnp.zeros_like(vec_part)
        for i in range(3):
            total = jnp.sum(vec_sum[i], axis=0, keepdims=True)
            for k in range(8):
                vec_part[k, pl.ds(i, 1), :] = total[:, k * 256 : k * 256 + 256]

    def column_sums():
        ones = jnp.ones((8, 1024), low)
        vec_mine[...] = jnp.zeros_like(vec_mine)
        qkv_sum = dot(ones, qkv[...].reshape(1024, 768))
        for i in range(6):
            vec_mine[pl.ds(6 + i, 1), :] = qkv_sum[0:1, i * PAIR : (i + 1) * PAIR]
        pre_sum = dot(ones, d_pre[...].reshape(1024, 1024))
        for i in range(8):
            vec_mine[pl.ds(12 + i, 1), :] = pre_sum[0:1, i * PAIR : (i + 1) * PAIR]

    def loop(first, last, tile):
        return lambda: lax.fori_loop(first, last, tile, 0)

    tasks = {
        "vec_rows": vec_task, "norm_own": norm_own, "norm_sides": norm_sides, "norm_far": norm_far,
        "d_att": d_att_task, "qkv0": qkv_task(0), "qkv1": qkv_task(1), "grad_d": loop(0, 2, dense_tile),
        "grad_q0": loop(0, 2, qkv_grad_tile), "grad_q1": loop(2, 4, qkv_grad_tile),
        "grad_e0": loop(0, 2, expand_tile(0)), "grad_e1": loop(0, 2, expand_tile(1)),
        "grad_s0": loop(0, 2, shrink_tile(0)), "grad_s1": loop(0, 2, shrink_tile(1)),
        "norm_back": norm_back, "col_sums": column_sums,
    }
    for i in range(4):
        tasks["att" + str(i)] = loop(i, i + 1, attend_tile)
        tasks["up" + str(i)] = up_task(i)
    for half in range(2):
        for at, g in (("a", 1 - c), ("b", c)):
            tasks["down" + at + str(half)] = down_task(g, half)
            tasks["out" + at + str(half)] = out_task(g, half)

    for name in SCHEDULE:
        if name in tasks:
            tasks[name]()
        else:
            advance(name)
    finish(*works)
    copies.finish()


def layer(tokens, cotangent, block_seq, seq_lengths, vectors, weights):
    low, f32 = jnp.bfloat16, jnp.float32
    vmem = pl.BlockSpec(memory_space=pltpu.VMEM)
    smem = pl.BlockSpec(memory_space=pltpu.SMEM)
    anywhere = pl.BlockSpec(memory_space=pl.ANY)
    turn = jnp.asarray(np.stack(rotary_constants())[:, : 3 * BLOCK])
    outs = [
        ((BLOCK, MODEL), low), ((BLOCK, MODEL), low), ((8, 16, 1024), low), ((8, 16, 768), low),
        ((16, MODEL), low), ((64, MODEL), f32), ((2, 4, 24, PAIR), f32),
    ]
    held = [
        ((4, 4, 128, 1024), low), ((4, 4, 128, 768), low), ((4, 4, 16, 2560), low),
        ((4, 4, 64, 2048), low), ((2, 4, 128, 2048), low), ((2, 4, 128, 2048), low),
        ((2, 512, 1024), low), ((2, 512, 1024), low), ((2, 512, 768), low), ((2, 512, 256), low),
        ((4, 4, 128, 1024), low), ((4, 4, 64, 1536), low), ((4, 4, 16, 2048), low),
        ((4, 4, 64, 2048), low), ((64, 8192), f32), ((8, 1024), f32),
        ((2, 4, 8, 128), f32), ((184, 128), f32),
        ((8, 16, 1024), low), ((8, 16, 768), low), ((16, 2048), low),
        ((2, 6, 4, 32, 1024), low), ((2, 6, 32, 1024), low),
        ((2, 6, 4, 16, 512), low), ((2, 6, 16, 512), low),
        ((2, 6, 4, 16, 2048), low), ((2, 6, 16, 2048), low),
        ((4, 128, 2048), low), ((6, 64, 2048), low),
        ((8, 16, 1024), low), ((8, 16, 768), low), ((16, 2048), low), ((8, 384), f32),
        ((3, 8, MODEL), f32), ((8, 8, 256), f32), ((8, 8, 256), f32), ((24, 128), f32),
        ((4, 4, 24, 128), f32),
    ]
    return pl.pallas_call(
        layer_kernel,
        in_specs=[vmem, vmem, smem, smem, vmem, vmem] + [anywhere] * 4,
        out_specs=[vmem] * 7,
        out_shape=[jax.ShapeDtypeStruct(s, k) for s, k in outs],
        scratch_shapes=[pltpu.VMEM(s, k) for s, k in held]
        + [
            pltpu.SemaphoreType.DMA((COPIES,)),
            pltpu.SemaphoreType.DMA((COPIES,)),
            pltpu.SemaphoreType.DMA((7,)),
            pltpu.SemaphoreType.REGULAR((2,)),
            pltpu.SemaphoreType.REGULAR((2,)),
            pltpu.SemaphoreType.REGULAR,
        ],
        compiler_params=pltpu.CompilerParams(
            collective_id=0, has_side_effects=True, vmem_limit_bytes=64 * 2**20
        ),
        name="layer",
    )(tokens, cotangent, block_seq, seq_lengths, vectors[None, :], turn, *weights)


def update_kernel(out_in, ig_in, ge, gq, gd, gs, vec, *refs):
    f32 = jnp.float32
    masters, moments, seconds = refs[0:5], refs[5:10], refs[10:15]
    out_ref, ig_ref = refs[15:17]
    results = [refs[17 + 3 * i : 20 + 3 * i] for i in range(5)]
    flat = refs[32]
    out_ref[...] = out_in[...]
    ig_ref[...] = ig_in[...]

    def update(i, at, gradient):
        grad_ref, state_ref, new_ref = results[i]
        grad_ref[at] = gradient
        state, new = adam_step(
            masters[i][at], moments[i][at], seconds[i][at], gradient, RATES[i], DECAYS[i]
        )
        state_ref[at] = state
        new_ref[at] = new

    every = slice(None)
    for s in range(3):
        for hi in range(2):
            for t in range(TPN):
                col = s * MODEL + hi * 1024 + t * PAIR
                piece = gq[t, :, pl.ds((2 * s + 1 - hi) * PAIR, PAIR)].astype(f32)
                update(0, (every, pl.ds(col, PAIR)), piece)
    for k in range(16):
        cols = (every, pl.ds(k * PAIR, PAIR))
        update(1, cols, gd[cols].astype(f32))
        for r in range(4):
            at = (pl.ds(16 * r, 16), pl.ds(k * PAIR, PAIR))
            update(3, at, gs[at])
    left = lax.broadcasted_iota(jnp.int32, (16, PAIR), 1) < HEAD
    for j in range(16):
        for k in range(4):
            first = ge[2 * k, :, pl.ds((j // 2) * PAIR, PAIR)].astype(f32)
            second = ge[2 * k + 1, :, pl.ds((j // 2) * PAIR, PAIR)].astype(f32)
            if j % 2 == 0:
                second = pltpu.roll(second, HEAD, 1)
            else:
                first = pltpu.roll(first, HEAD, 1)
            update(2, (every, pl.ds(j * 512 + k * PAIR, PAIR)), jnp.where(left, first, second))

    flat[...] = jnp.zeros_like(flat)
    left = lax.broadcasted_iota(jnp.int32, (1, PAIR), 1) < HEAD

    def line(t, row):
        return vec[t // 4, t % 4, pl.ds(row, 1), :]

    for t in range(TPN):
        for i in range(2):
            for row, base in ((0, 0), (1, 16), (2, 80), (2, 160)):
                flat[pl.ds(base + 2 * t + i, 1), :] = line(t, 2 * row + i)
        for s in range(3):
            for hi in range(2):
                at = 32 + s * 16 + hi * 8 + t
                flat[pl.ds(at, 1), :] = line(t, 6 + 2 * s + 1 - hi)
    for j in range(16):
        for k in range(4):
            first = line(2 * k, 12 + j // 2)
            second = line(2 * k + 1, 12 + j // 2)
            if j % 2 == 0:
                second = pltpu.roll(second, HEAD, 1)
            else:
                first = pltpu.roll(first, HEAD, 1)
            flat[pl.ds(96 + 4 * j + k, 1), :] = jnp.where(left, first, second)
    z, y, c, x = (lax.axis_index(a) for a in ALL)
    number = ((z * 4 + y) * 2 + c) * 4 + x
    first = (176 * number) // 128
    own = jnp.concatenate([flat[pl.ds(first + i, 1), :] for i in range(3)], axis=1)
    own = jnp.broadcast_to(own, (8, 3 * PAIR))
    own = pltpu.roll(own, lax.rem(3 * PAIR - 16 * lax.rem(3 * number, 8), 3 * PAIR), 1)
    update(4, (every, every), own[0:1, 0:176])


def update_all(parts, masters, moments, seconds):
    f32 = jnp.float32
    vmem = pl.BlockSpec(memory_space=pltpu.VMEM)
    shapes = [jax.ShapeDtypeStruct(p.shape, p.dtype) for p in parts[:2]]
    for w in masters:
        shapes += [jax.ShapeDtypeStruct(w.shape, f32)] * 3
    return pl.pallas_call(
        update_kernel,
        in_specs=[vmem] * 22,
        out_specs=[vmem] * 17,
        out_shape=shapes,
        scratch_shapes=[pltpu.VMEM((184, PAIR), f32)],
        compiler_params=pltpu.CompilerParams(vmem_limit_bytes=62 * 2**20),
        name="update",
    )(*parts, *masters, *moments, *seconds)


def adam_step(weight, moment, second, gradient, step_rate, step_decay):
    moment_new = BETA_ONE * moment + (1 - BETA_ONE) * gradient
    second_new = BETA_TWO * second + (1 - BETA_TWO) * gradient * gradient
    moment_hat = moment_new / (1 - BETA_ONE**STEP)
    second_hat = second_new / (1 - BETA_TWO**STEP)
    updated = weight - step_rate * (
        moment_hat / (jnp.sqrt(second_hat) + ADAM_EPS) + step_decay * weight
    )
    return (second_new, updated)


def shards(
    tokens, cotangent, block_seq, seq_lengths,
    qkv_weight, qkv_moment, qkv_second,
    dense_weight, dense_moment, dense_second,
    expand_weight, expand_moment, expand_second,
    shrink_weight, shrink_moment, shrink_second,
    vectors, vec_moment, vec_second,
):
    parts = layer(
        tokens,
        cotangent,
        block_seq,
        seq_lengths,
        vectors,
        (qkv_weight, dense_weight, expand_weight, shrink_weight),
    )
    masters = (qkv_weight, dense_weight, expand_weight, shrink_weight, vectors[None, :])
    moments = (qkv_moment, dense_moment, expand_moment, shrink_moment, vec_moment[None, :])
    seconds = (qkv_second, dense_second, expand_second, shrink_second, vec_second[None, :])
    results = update_all(parts, masters, moments, seconds)
    return (*results[:14], *(r[0] for r in results[14:]))


def solution(mesh):
    finer = Mesh(mesh.devices.reshape(*SIZES), ALL)
    whole, group = P(ALL, None), P(DP, None)
    return jax.shard_map(
        shards,
        mesh=finer,
        in_specs=(whole, whole, group, group, *[whole] * 12, *[P(ALL)] * 3),
        out_specs=(*[whole] * 14, *[P(ALL)] * 3),
        check_vma=False,
    )
```

```python
import functools

import jax
import jax.numpy as jnp
import numpy as np
from jax import lax
from jax.experimental import pallas as pl
from jax.experimental.pallas import tpu as pltpu
from jax.sharding import Mesh
from jax.sharding import PartitionSpec as P

HEAD = 64
ROT = 32
BLOCK = 128
STEP = 10
GROUP = 512
MODEL = 2048
FF = 8192
PAIR = 2 * HEAD
ALL = ("z", "y", "c", "x")
DP = ("z", "y", "c")
ZY = ("z", "y")
TP = ("c", "x")
SIZES = (4, 4, 2, 4)
TPN = 8
COPIES = 480
SCHEDULE = (
    "to_q", "s", "to_d", "tok", "vec", "d", "q", "to_e", "cot", "vec_rows", "q", "q", "e", "q",
    "norm_own", "q", "cot", "s", "norm_sides", "e", "norm_far", "qkv0", "d_att", "qkv1", "s",
    "e", "att0", "att1", "s", "att2", "att3", "e", "grad_q0", "e", "s", "grad_q1", "grad_d",
    "sum_d", "sum_q", "up0", "up1", "sum_d", "up2", "up3", "sum_q", "grad_e0", "grad_e1",
    "sum_e1", "downa1", "downa0", "n1", "sum_q", "sum_e0", "downb1", "n1", "n0", "grad_s0",
    "sum_q", "downb0", "sum_e1", "n0", "n1", "sum_e0", "grad_s1", "sum_d", "sum_s1", "outa1",
    "outb1", "n0", "sum_s0", "o1", "sum_d", "col_sums", "back_q", "outa0", "sum_s1", "o1",
    "norm_back", "back_d", "o0", "sum_e0", "outb0", "back_d", "vec_back", "sum_s0", "o0",
    "sum_s1", "sum_e1", "sum_s0", "o1", "sum_e1", "vec_back", "o0", "back_e", "sum_s0",
    "sum_s1", "vec_back", "sum_s1",
)
SCALE = HEAD ** (-0.5)

NORM_EPS = 1e-05
MASKED = -1e30
BETA_ONE = 0.9
BETA_TWO = 0.999
ADAM_EPS = 1e-08
RATES = (0.02, 0.1, 0.02, 0.01, 0.4)
DECAYS = (0.1, 0.1, 0.1, 0.1, 0.0)
GELU_A = float(np.sqrt(2.0 / np.pi))
GELU_B = 0.044715


def dot(a, b):
    return jnp.dot(a, b, preferred_element_type=jnp.float32)


def dot_t(a, b):
    return lax.dot_general(a, b, (((1,), (1,)), ((), ())), preferred_element_type=jnp.float32)


def cross(a, b):
    return lax.dot_general(a, b, (((0,), (0,)), ((), ())), preferred_element_type=jnp.float32)


def rotary_constants():
    half = np.arange(ROT // 2, dtype=np.float32)
    inverse = (10000.0 ** (-2.0 * half.astype(np.float64) / ROT)).astype(np.float32)
    angle = (np.arange(GROUP, dtype=np.float32)[:, None] * inverse[None, :]).astype(np.float64)
    cosine, sine = np.cos(angle).astype(np.float32), np.sin(angle).astype(np.float32)
    one = np.ones((GROUP, HEAD - ROT), np.float32)
    zero = np.zeros((GROUP, ROT // 2), np.float32)
    rest = np.zeros((GROUP, HEAD - ROT), np.float32)
    turn = np.concatenate([cosine, cosine, one], axis=1)
    ahead = np.concatenate([-sine, zero, rest], axis=1)
    behind = np.concatenate([zero, sine, rest], axis=1)
    return tuple(np.concatenate([a, a], axis=1) for a in (turn, ahead, behind))


MESH = pl.DeviceIdType.MESH


def other(axis, step):
    size = SIZES[ALL.index(axis)]
    return lax.rem(lax.axis_index(axis) + step + size, size)


class Copy:
    def __init__(self, copy):
        self.copy, self.here, self.gone = copy, False, False

    def arrive(self):
        if not self.here:
            self.copy.wait_recv()
        self.here = True

    def leave(self):
        if not self.gone:
            self.copy.wait_send()
        self.gone = True


class Copies:
    def __init__(self, send, recv):
        self.send, self.recv, self.all = send, recv, []

    def start(self, src, dst, to):
        at = len(self.all)
        copy = pltpu.make_async_remote_copy(
            src_ref=src,
            dst_ref=dst,
            send_sem=self.send.at[at],
            recv_sem=self.recv.at[at],
            device_id=to,
            device_id_type=MESH,
        )
        copy.start()
        self.all.append(Copy(copy))
        return self.all[-1]

    def finish(self):
        for copy in self.all:
            copy.leave()


def greet():
    barrier = pltpu.get_barrier_semaphore()
    for partner in token_partners() + weight_partners() + [dense_partner()]:
        pl.semaphore_signal(barrier, inc=1, device_id=partner, device_id_type=MESH)


def enter():
    pl.semaphore_wait(pltpu.get_barrier_semaphore(), 23)


def token_partners():
    return [{"c": other("c", i), "x": other("x", j)} for i in range(2) for j in range(4) if i + j]


def weight_partners():
    return [{"z": other("z", i), "y": other("y", j)} for i in range(4) for j in range(4) if i + j]


def dense_partner():
    z, y, c, x = (lax.axis_index(a) for a in ALL)
    return {"z": (1 - z // 2) * 2 + c, "y": x, "c": lax.rem(z, 2), "x": y}


def gather_weights(copies, view):
    z, y = lax.axis_index("z"), lax.axis_index("y")
    z_up, z_down, y_up, y_down = other("z", 1), other("z", -1), other("y", 1), other("y", -1)
    z_far, y_far = other("z", 2), other("y", 2)
    up, down, far, near = {"y": y_up}, {"y": y_down}, {"z": z_up}, {"z": z_down}

    def go(block, to):
        return copies.start(block, block, to)

    a_up, a_down = go(view(z, y, 4), up), go(view(z, y, 4), down)
    b_up, b_down = go(view(z, y, 5), far), go(view(z, y, 5), near)
    a_own = go(view(z, y, 4), far), go(view(z, y, 4), near)
    b_own = go(view(z, y, 5), up), go(view(z, y, 5), down)
    yield
    a_up.arrive()
    a_low = go(view(z, y_down, 0), up)
    b_up.arrive()
    b_low = go(view(z_down, y, 2), far)
    a_down.arrive()
    a_high = go(view(z, y_up, 1), down)
    b_down.arrive()
    b_high = go(view(z_up, y, 3), near)
    a_side = [(i, go(view(z, i, 4), far), go(view(z, i, 4), near)) for i in (y_down, y_up)]
    b_side = [(i, go(view(i, y, 5), up), go(view(i, y, 5), down)) for i in (z_down, z_up)]
    yield
    last = []
    a_own[0].arrive()
    last.append(go(view(z_down, y, 0), far))
    b_own[0].arrive()
    last.append(go(view(z, y_down, 2), up))
    a_own[1].arrive()
    last.append(go(view(z_up, y, 1), near))
    b_own[1].arrive()
    last.append(go(view(z, y_up, 3), down))
    a_low.arrive()
    a_high.arrive()
    a_side.append((y_far, go(view(z, y_far, 4), far), go(view(z, y_far, 4), near)))
    b_low.arrive()
    b_high.arrive()
    b_side.append((z_far, go(view(z_far, y, 5), up), go(view(z_far, y, 5), down)))
    for k in range(3):
        if k != 1:
            yield
        i, first, second = a_side[k]
        first.arrive()
        last.append(go(view(z_down, i, 0), far))
        second.arrive()
        last.append(go(view(z_up, i, 1), near))
        i, first, second = b_side[k]
        first.arrive()
        last.append(go(view(i, y_down, 2), up))
        second.arrive()
        last.append(go(view(i, y_up, 3), down))
    yield
    for copy in last:
        copy.arrive()


def gather_tokens(copies, ref, sent):
    c, x, across = lax.axis_index("c"), lax.axis_index("x"), other("c", 1)
    right, left = {"x": other("x", 1)}, {"x": other("x", -1)}

    def go(block, to):
        return copies.start(block, block, to)

    own = ref.at[c, x]
    sent.append([go(own, right), go(own, left), go(own, {"c": across})])
    yield
    sent[0][0].arrive()
    last = [go(ref.at[c, other("x", -1), pl.ds(0, 64)], right)]
    side = [go(ref.at[c, other("x", -1)], {"c": across})]
    sent[0][1].arrive()
    last.append(go(ref.at[c, other("x", 1), pl.ds(64, 64)], left))
    side.append(go(ref.at[c, other("x", 1)], {"c": across}))
    sent.append(last + side)
    yield
    for copy in last:
        copy.arrive()
    sent.append([go(ref.at[c, other("x", 2)], {"c": across})])
    yield
    for copies_of_stage in sent:
        for copy in copies_of_stage:
            copy.arrive()
            copy.leave()


def gather_vectors(copies, group, rows, place):
    c, x = lax.axis_index("c"), lax.axis_index("x")
    sent = [copies.start(group.at[c, x], group.at[c, x], to) for to in token_partners()]
    yield
    for copy in sent:
        copy.arrive()
    rows[pl.ds(0, 16), :] = jnp.zeros((16, PAIR), jnp.float32)
    for d in range(TPN):
        rows[pl.ds((176 * d) // PAIR, 3), :] += group[d // 4, d % 4, pl.ds(0, 3), :]
    place[:, pl.ds(0, PAIR)] = rows[pl.ds(0, 16), :].astype(jnp.bfloat16)
    place[:, pl.ds(PAIR, 3 * PAIR)] = jnp.zeros((16, 3 * PAIR), jnp.bfloat16)


def expand_to_group(copies, send, ref, width):
    z, y, c, x = (lax.axis_index(a) for a in ALL)
    rows = pl.ds(pl.multiple_of((c * 4 + x) * 16, 16), 16)
    sent = []
    for to in token_partners():
        sent.append(copies.start(send.at[to["c"] * 4 + to["x"]], ref.at[z, y, rows], to))
    ref[z, y, rows] = send[c * 4 + x]
    yield
    for copy in sent:
        copy.arrive()


def by_rows(ref, rows):
    quarter = rows // 4

    def view(z, y, part):
        start, size = (part * quarter, quarter) if part < 4 else ((part - 4) * 2 * quarter, 2 * quarter)
        return ref.at[z, y, pl.ds(start, size)]

    return view


def by_columns(ref, columns):
    quarter = columns // 4

    def view(z, y, part):
        start, size = (part * quarter, quarter) if part < 4 else ((part - 4) * 2 * quarter, 2 * quarter)
        return ref.at[z, y, :, pl.ds(start, size)]

    return view


def step(*works):
    for work in works:
        next(work, None)


def row_of(ref, first, count):
    return jnp.concatenate([ref[pl.ds(first + i, 1), :] for i in range(count)], axis=1)


def ring_sum(copies, axis, block, land, low_part, high_part):
    ahead, behind = other(axis, 1), other(axis, -1)
    up, down = {axis: ahead}, {axis: behind}
    far = other(axis, 2)
    t_low = copies.start(block(far, low_part), land.at[0], up)
    t_high = copies.start(block(far, high_part), land.at[1], down)
    d_high = copies.start(block(ahead, high_part), land.at[3], up)
    d_low = copies.start(block(behind, low_part), land.at[2], down)
    yield
    t_low.arrive()
    land[0] = land[0] + block(ahead, low_part)[...]
    p_low = copies.start(land.at[0], land.at[4], up)
    t_high.arrive()
    land[1] = land[1] + block(behind, high_part)[...]
    p_high = copies.start(land.at[1], land.at[5], down)
    yield
    for copy in (d_low, d_high, p_low, p_high):
        copy.arrive()
    for copy in (t_low, t_high, d_low, d_high, p_low, p_high):
        copy.leave()


def three(own, land, high, at=...):
    f32 = jnp.float32
    first, second = land.at[4 + high], land.at[2 + high]
    return own[at].astype(f32) + first[at].astype(f32) + second[at].astype(f32)


def both(first, second):
    while True:
        done = [next(first, 0), next(second, 0)]
        if 0 in done:
            return
        yield


def scatter_weights(copies, view, wide, narrow, give):
    z, y = lax.axis_index("z"), lax.axis_index("y")
    every = slice(None)
    low = jnp.bfloat16
    yield from both(
        ring_sum(copies, "y", lambda i, p: view(every, i, p), wide.at[0], 0, 1),
        ring_sum(copies, "z", lambda i, p: view(i, every, p), wide.at[1], 2, 3),
    )
    for high in range(2):
        own = view(every, y, high)
        for i in range(4):
            own[i] = three(own, wide.at[0], high, i).astype(low)
        own = view(z, every, 2 + high)
        for i in range(4):
            own[i] = three(own, wide.at[1], high, i).astype(low)
    yield from both(
        ring_sum(copies, "z", lambda i, p: view(i, y, p), narrow.at[0], 0, 1),
        ring_sum(copies, "y", lambda i, p: view(z, i, p), narrow.at[1], 2, 3),
    )
    for high in range(2):
        give(high, three(view(z, y, high), narrow.at[0], high))
        give(2 + high, three(view(z, y, 2 + high), narrow.at[1], high))


def scatter_tokens(copies, ref, core_land, land, give, core_free, ring_free, first):
    c, x, across = lax.axis_index("c"), lax.axis_index("x"), other("c", 1)
    if not first:
        pl.semaphore_wait(core_free, 1)
    came = copies.start(ref.at[across], core_land, {"c": across})
    yield
    came.arrive()
    for i in range(4):
        ref[c, i] = ref[c, i] + core_land[i]
    if first:
        pl.semaphore_signal(core_free, inc=1, device_id={"c": across}, device_id_type=MESH)
    else:
        pl.semaphore_wait(ring_free, 2)
    yield from ring_sum(copies, "x", lambda i, p: ref.at[c, i, pl.ds(p * 64, 64)], land, 0, 1)
    for high in range(2):
        own = ref.at[c, x, pl.ds(high * 64, 64)]

        def chunk(r, _):
            rows = pl.ds(pl.multiple_of(r * 16, 16), 16)
            give(high, r, three(own, land, high, rows))
            return 0

        lax.fori_loop(0, 4, chunk, 0)
    if first:
        for way in (1, -1):
            to = {"x": other("x", way)}
            pl.semaphore_signal(ring_free, inc=1, device_id=to, device_id_type=MESH)


def landed(copy):
    yield
    copy.arrive()


def sum_vectors(copies, part, came, mine, zy, out):
    z, y, c, x = (lax.axis_index(a) for a in ALL)
    t = c * 4 + x
    sent = [
        copies.start(part.at[to["c"] * 4 + to["x"]], came.at[t], to) for to in token_partners()
    ]
    came[t] = part[t]
    yield
    for copy in sent:
        copy.arrive()
    total = jnp.sum(came[...], axis=0)
    for i in range(6):
        mine[pl.ds(i, 1), :] = total[i // 2 : i // 2 + 1, (i % 2) * PAIR : (i % 2 + 1) * PAIR]
    zy[z, y] = mine[...]
    sent = [copies.start(mine, zy.at[z, y], to) for to in weight_partners()]
    yield
    for copy in sent:
        copy.arrive()
    out[c, x] = jnp.sum(zy[...].reshape(16, 24, PAIR), axis=0)
    sent = [copies.start(out.at[c, x], out.at[c, x], to) for to in token_partners()]
    yield
    for copy in sent:
        copy.arrive()


def return_to_group(copies, ref, out):
    c, x = lax.axis_index("c"), lax.axis_index("x")
    t = c * 4 + x
    sent = []
    for to in token_partners():
        sent.append(copies.start(ref.at[to["c"] * 4 + to["x"]], out.at[t], to))
    out[t] = ref[t]
    yield
    for copy in sent:
        copy.arrive()


def turned(values, table, sign):
    turn, ahead, behind = table
    up = pltpu.roll(values, PAIR - ROT // 2, 1)
    down = pltpu.roll(values, ROT // 2, 1)
    if sign > 0:
        return values * turn + up * ahead + down * behind
    return values * turn - up * ahead - down * behind


def attend(meta, turn_ref, qkv, att, g, p):
    low, f32 = jnp.bfloat16, jnp.float32
    lane = lax.broadcasted_iota(jnp.int32, (BLOCK, PAIR), 1)
    first = lane < HEAD
    zero = jnp.zeros((BLOCK, PAIR), low)
    row_at = lax.broadcasted_iota(jnp.int32, (BLOCK, BLOCK), 0)
    col_at = lax.broadcasted_iota(jnp.int32, (BLOCK, BLOCK), 1)
    cols = [pl.ds(pl.multiple_of(i * 2 * PAIR + p * PAIR, PAIR), PAIR) for i in range(3)]
    d_k = [jnp.zeros((BLOCK, PAIR), f32) for _ in range(4)]
    d_v = [jnp.zeros((BLOCK, PAIR), f32) for _ in range(4)]
    held = [qkv[g, :, cols[i]] for i in range(3)] + [att[g, :, cols[0]]]
    done = []
    for b in range(4):
        rows, width = slice(b * BLOCK, (b + 1) * BLOCK), (b + 1) * BLOCK
        base = meta[:, 4 + b : 5 + b] * BLOCK
        diagonal = (col_at <= row_at) & (col_at.astype(f32) + base < meta[:, 8 + b : 9 + b])
        bias = [
            jnp.where(meta[:, e : e + 1] == meta[:, b : b + 1], 0.0, MASKED)
            + jnp.zeros((BLOCK, BLOCK), f32)
            for e in range(b)
        ]
        bias.append(jnp.where(diagonal, 0.0, MASKED).astype(f32))
        bias = bias[0] if b == 0 else jnp.concatenate(bias, axis=1)
        q, da, k, v = held[0][rows], held[3][rows], held[1][:width], held[2][:width]
        qs = jnp.concatenate([jnp.where(first, q, zero), jnp.where(first, zero, q)], axis=0)
        das = jnp.concatenate([jnp.where(first, da, zero), jnp.where(first, zero, da)], axis=0)
        scores = dot_t(qs, k) + jnp.concatenate([bias, bias], axis=0)
        w = jnp.exp(scores - jnp.max(scores, axis=1, keepdims=True))
        prob = w * (1.0 / jnp.sum(w, axis=1, keepdims=True))
        prob_low = prob.astype(low)
        summed = dot(prob_low, v)
        dp = dot_t(das, v)
        ds = (prob * (dp - jnp.sum(prob * dp, axis=1, keepdims=True))).astype(low)
        dq = dot(ds, k)
        dq = jnp.where(first, dq[:BLOCK], dq[BLOCK:]) * SCALE
        dq = turned(dq, table_of(meta, turn_ref, b), -1).astype(low)
        done.append((jnp.where(first, summed[:BLOCK], summed[BLOCK:]).astype(low), dq))
        dk = cross(ds, qs)
        dv = cross(prob_low, das)
        for e in range(b + 1):
            d_k[e] = d_k[e] + dk[e * BLOCK : (e + 1) * BLOCK]
            d_v[e] = d_v[e] + dv[e * BLOCK : (e + 1) * BLOCK]
    for b in range(4):
        rows = pl.ds(b * BLOCK, BLOCK)
        att[g, rows, cols[0]], qkv[g, rows, cols[0]] = done[b]
        qkv[g, rows, cols[1]] = turned(d_k[b], table_of(meta, turn_ref, b), -1).astype(low)
        qkv[g, rows, cols[2]] = d_v[b].astype(low)


def table_of(meta, turn_ref, b):
    rank = meta[:, 4 + b : 5 + b]
    parts = [turn_ref[:, pl.ds(r * BLOCK, BLOCK), :] for r in range(3)]
    table = jnp.where((rank == 0.0)[None], parts[0], jnp.where((rank == 1.0)[None], parts[1], parts[2]))
    return table[0], table[1], table[2]


def layer_kernel(
    tokens_ref, cot_ref, seq_ref, length_ref, vec_ref, turn_ref, q_hbm, d_hbm, e_hbm, s_hbm,
    out_ref, ig_ref, ge_out, gq_out, gd_out, gs_out, vec_out,
    we, wq, wd, ws, normed, d_out, act, d_pre, qkv, att,
    ge, gq, gd, gs, stage, bias_e, vec_group, vec_rows, we_send, wq_send, wd_own,
    wide_e, narrow_e, wide_d, narrow_d, wide_s, narrow_s,
    core_land, ring_land, res_e, res_q, res_d,
    vec_line, vec_sum, vec_part, vec_came, vec_mine, vec_zy,
    send, recv, local, core_free, ring_free, wide_free,
):
    low, f32 = jnp.bfloat16, jnp.float32
    z, y, c, x = (lax.axis_index(a) for a in ALL)
    t = c * 4 + x
    copies = Copies(send, recv)
    greet()

    loads = [
        pltpu.make_async_copy(q_hbm, stage.at[pl.ds(16, 16), pl.ds(0, 6144)], local.at[0]),
        pltpu.make_async_copy(d_hbm, stage.at[pl.ds(16, 16), pl.ds(6144, 2048)], local.at[1]),
        pltpu.make_async_copy(e_hbm, stage.at[pl.ds(0, 16)], local.at[2]),
    ]
    for k in range(4):
        rows = pl.ds(16 * k, 16)
        place = stage.at[pl.ds(32, 16), pl.ds(2048 * k, 2048)]
        loads.append(pltpu.make_async_copy(s_hbm.at[rows], place, local.at[3 + k]))
    for load in loads:
        load.start()

    lane = lax.broadcasted_iota(jnp.int32, (1, PAIR), 1)
    seqs = [seq_ref[0, b] for b in range(4)]
    own_meta = jnp.zeros((1, PAIR), f32)
    own_rank, own_limit = jnp.zeros((1, 1), f32), jnp.zeros((1, 1), f32)
    for b in range(4):
        rank = jnp.int32(0)
        for e in range(b):
            rank = rank + jnp.where(seqs[e] == seqs[b], 1, 0)
        limit = jnp.where(seqs[b] == 0, length_ref[0, 0], length_ref[0, 1])
        for at, value in ((b, seqs[b]), (4 + b, rank), (8 + b, limit)):
            own_meta = jnp.where(lane == at, value.astype(f32), own_meta)
        own_rank = jnp.where(x == b, rank.astype(f32), own_rank)
        own_limit = jnp.where(x == b, limit.astype(f32), own_limit)
    vec_line[...] = jnp.zeros_like(vec_line)
    vec_line[pl.ds(0, 1), pl.ds(0, 176)] = vec_ref[...].astype(low).astype(f32)
    line = pltpu.roll(vec_line[...], 16 * lax.rem(3 * t + 24 * (z * 4 + y), 8), 1)
    vec_own = vec_group.at[c, x]
    vec_own[...] = jnp.zeros((8, PAIR), f32)
    for k in range(3):
        vec_own[pl.ds(k, 1), :] = line[0:1, k * PAIR : (k + 1) * PAIR]
    vec_own[pl.ds(4, 1), :] = own_meta

    def d_out_rows(rows, first):
        row_at = lax.broadcasted_iota(jnp.int32, (16, 1), 0) + first
        live = (row_at.astype(f32) + own_rank * BLOCK < own_limit).astype(f32)
        return cot_ref[rows, :].astype(f32) * live

    def mask_chunk(r, _):
        rows = pl.ds(pl.multiple_of(r * 16, 16), 16)
        d_out[c, x, rows] = d_out_rows(rows, r * 16).astype(low)
        return 0


    def scaled(rows):
        values = tokens_ref[rows, :].astype(f32)
        middle = values - jnp.mean(values, axis=1, keepdims=True)
        spread = lax.rsqrt(jnp.mean(middle * middle, axis=1, keepdims=True) + NORM_EPS)
        return middle * spread, spread

    def scale_chunk(r, _):
        rows = pl.ds(pl.multiple_of(r * 16, 16), 16)
        normed[c, x, rows] = scaled(rows)[0].astype(low)
        return 0

    lax.fori_loop(0, 8, scale_chunk, 0)
    loads[0].wait()
    for k in range(8):
        for i in range(6):
            col = (i // 2) * 2048 + (1 - i % 2) * 1024 + k * PAIR
            piece = stage[pl.ds(16, 16), pl.ds(col, PAIR)]
            wq_send[k, :, pl.ds(i * PAIR, PAIR)] = piece.astype(low)
    enter()

    def cast_dense():
        loads[1].wait()
        wd_own[...] = stage[pl.ds(16, 16), pl.ds(6144, 2048)].astype(low)

    def cast_expand():
        left16 = lax.broadcasted_iota(jnp.int32, (16, PAIR), 1) < HEAD
        loads[2].wait()
        for j in range(8):
            for k in range(4):
                first = stage[pl.ds(0, 16), pl.ds(j * 1024 + k * PAIR, PAIR)]
                second = stage[pl.ds(0, 16), pl.ds(j * 1024 + 512 + k * PAIR, PAIR)]
                even = jnp.where(left16, first, pltpu.roll(second, HEAD, 1))
                odd = jnp.where(left16, pltpu.roll(first, HEAD, 1), second)
                we_send[2 * k, :, pl.ds(j * PAIR, PAIR)] = even.astype(low)
                we_send[2 * k + 1, :, pl.ds(j * PAIR, PAIR)] = odd.astype(low)

    def cast_shrink():
        for k in range(4):
            loads[3 + k].wait()
            ws[z, y, pl.ds(16 * k, 16)] = stage[pl.ds(32, 16), pl.ds(2048 * k, 2048)].astype(low)

    works, stages, tasks, finished = {}, {}, {}, set()
    token_sends = []

    def finish(*names):
        for name in names:
            for _ in works[name]:
                pass
            finished.add(name)

    def advance(name):
        if name not in works:
            works[name], stages[name] = begin(name), 0
        stages[name] += 1
        if next(works[name], 0) == 0:
            finished.add(name)

    def reach(name, stage):
        while stages[name] < stage:
            advance(name)

    def begin(name):
        if name == "vec":
            return gather_vectors(copies, vec_group, vec_rows, wd.at[z, y, :, pl.ds(MODEL, 512)])
        if name == "to_q":
            return expand_to_group(copies, wq_send, wq, 768)
        if name == "to_e":
            cast_expand()
            return expand_to_group(copies, we_send, we, 1024)
        if name == "to_d":
            cast_dense()
            there = dense_partner()
            place = wd.at[there["z"], there["y"], :, pl.ds(0, MODEL)]
            return landed(copies.start(wd_own, place, there))
        if name == "q":
            finish("to_q")
            return gather_weights(copies, by_rows(wq, 128))
        if name == "d":
            finish("to_d", "vec")
            return gather_weights(copies, by_columns(wd, 2560))
        if name == "e":
            finish("to_e")
            return gather_weights(copies, by_rows(we, 128))
        if name == "s":
            cast_shrink()
            return gather_weights(copies, by_rows(ws, 64))
        if name == "cot":
            lax.fori_loop(0, 8, mask_chunk, 0)
            return gather_tokens(copies, d_out, [])
        if name == "tok":
            return gather_tokens(copies, normed, token_sends)
        if name == "sum_d":
            return scatter_weights(copies, by_columns(gd, 2048), wide_d, narrow_d, give_d)
        if name == "sum_q":
            return sum_q()
        if name in ("sum_e0", "sum_e1"):
            half = int(name[-1])
            cols = pl.ds(half * 512, 512)
            return scatter_weights(
                copies,
                by_rows(ge.at[:, :, :, cols], 128),
                wide_e.at[:, :, :, :, cols],
                narrow_e.at[:, :, :, cols],
                give_e(half),
            )
        if name in ("sum_s0", "sum_s1"):
            finish("sum_q")
            if "wide" not in finished:
                pl.semaphore_wait(wide_free, 4)
                finished.add("wide")
            half = int(name[-1])
            cols = pl.ds(half * 1024, 1024)
            return scatter_weights(
                copies,
                by_rows(gs.at[:, :, :, cols], 64),
                wide_s.at[:, :, :, :, cols],
                narrow_s.at[:, :, :, cols],
                give_s(half),
            )
        if name in ("n0", "n1", "o0", "o1"):
            half = int(name[-1])
            if name[0] == "o":
                finish("n" + name[1])
            cols = pl.ds(half * 1024, 1024)
            return scatter_tokens(
                copies,
                (normed if name[0] == "n" else d_out).at[:, :, :, cols],
                core_land.at[:, :, cols],
                ring_land.at[:, :, cols],
                (give_n if name[0] == "n" else give_o)(half),
                core_free.at[half],
                ring_free.at[half],
                name[0] == "n",
            )
        if name == "back_q":
            finish("sum_q")
            return return_to_group(copies, res_q, gq_out)
        if name == "back_e":
            finish("sum_e0", "sum_e1")
            return return_to_group(copies, res_e, ge_out)
        if name == "back_d":
            finish("sum_d")
            return landed(copies.start(res_d, gd_out, dense_partner()))
        return sum_vectors(copies, vec_part, vec_came, vec_mine, vec_zy, vec_out)

    def vec_task():
        finish("d")
        for i in range(16):
            block = wd[i // 4, i % 4, :, pl.ds(MODEL, PAIR)].astype(f32)
            vec_rows[pl.ds(11 * i, 11), :] = block[0:11]

    def norm_blocks(blocks):
        def chunk(r, _):
            rows = pl.ds(pl.multiple_of(r * 16, 16), 16)
            for core, chip in blocks:
                xhat = normed[core, chip, rows].astype(f32)
                whole = xhat * row_of(vec_rows, 0, 16) + row_of(vec_rows, 16, 16)
                normed[core, chip, rows] = whole.astype(low)
            return 0

        lax.fori_loop(0, 8, chunk, 0)

    def norm_own():
        reach("tok", 2)
        for copy in token_sends[0]:
            copy.leave()
        token_sends[0][2].arrive()
        norm_blocks([(c, x), (1 - c, x)])

    def norm_sides():
        reach("tok", 3)
        for copy in token_sends[1]:
            copy.leave()
        for copy in token_sends[1][2:]:
            copy.arrive()
        for way in (-1, 1):
            norm_blocks([(c, other("x", way)), (1 - c, other("x", way))])

    def norm_far():
        finish("tok")
        token_sends[2][0].leave()
        norm_blocks([(c, other("x", 2)), (1 - c, other("x", 2))])

    def qkv_tile(g, _):
        meta = vec_group[g, x, pl.ds(4, 1), :]
        projected = dot(normed[g].reshape(512, MODEL), wq[...].reshape(MODEL, 768))
        for p in range(6):
            bias = vec_rows[pl.ds(32 + (p // 2) * 16 + (1 - p % 2) * 8 + t, 1), :]
            for b in range(4):
                rows = pl.ds(b * BLOCK, BLOCK)
                part = projected[b * BLOCK : (b + 1) * BLOCK, p * PAIR : (p + 1) * PAIR] + bias
                if p < 4:
                    part = turned(part, table_of(meta, turn_ref, b), 1)
                part = part.astype(low)
                if p < 2:
                    part = part * jnp.asarray(SCALE, low)
                qkv[g, rows, pl.ds(p * PAIR, PAIR)] = part
        return 0

    def d_att_tile(g, _):
        dense = wd[:, :, :, pl.ds(0, MODEL)].reshape(256, MODEL)
        att[g] = dot_t(d_out[g].reshape(512, MODEL), dense).astype(low)
        return 0

    def d_att_task():
        finish("cot", "d")
        lax.fori_loop(0, 2, d_att_tile, 0)

    def qkv_task(g):
        def task():
            finish("tok", "q")
            lax.fori_loop(g, g + 1, qkv_tile, 0)

        return task

    def attend_tile(i, _):
        g, p = i // 2, lax.rem(i, 2)
        attend(vec_group[g, x, pl.ds(4, 1), :], turn_ref, qkv, att, g, p)
        return 0

    def dense_tile(n, _):
        cols = pl.ds(pl.multiple_of(n * 1024, 1024), 1024)
        term = cross(att[...].reshape(1024, 256), d_out[:, :, :, cols].reshape(1024, 1024))
        gd[:, :, :, cols] = term.astype(low).reshape(4, 4, 16, 1024)
        return 0

    def give_d(part, total):
        res_d[:, pl.ds(part * 512, 512)] = total.astype(low)

    def qkv_grad_tile(i, _):
        mine = normed[:, :, :, pl.ds(pl.multiple_of(i * 512, 512), 512)].reshape(1024, 512)
        term = cross(mine, qkv[...].reshape(1024, 768)).astype(low).reshape(4, BLOCK, 768)
        gq[i, :, :, pl.ds(0, 768)] = term[:, :64]
        gq[i, :, :, pl.ds(768, 768)] = term[:, 64:]
        return 0

    def give_q(part, total):
        res_q[part] = total[:, :768].astype(low)
        res_q[4 + part] = total[:, 768:].astype(low)

    def sum_q():
        short = pl.ds(0, 1536)
        yield from scatter_weights(
            copies,
            by_rows(gq, 64),
            wide_s.at[:, :, :, :, short],
            narrow_s.at[:, :, :, short],
            give_q,
        )
        for axis in ("y", "z"):
            for way in (1, -1):
                to = {axis: other(axis, way)}
                pl.semaphore_signal(wide_free, inc=1, device_id=to, device_id_type=MESH)

    def up_tile(i, _):
        g, n = i // 2, lax.rem(i, 2)
        cols = pl.ds(pl.multiple_of(n * 512, 512), 512)
        pre_term = dot(normed[g].reshape(512, MODEL), we[:, :, :, cols].reshape(MODEL, 512))
        for k in range(8):
            stage[:, pl.ds(k * 512, 512)] = pre_term[k * 64 : k * 64 + 64]
        act_term = dot_t(d_out[g].reshape(512, MODEL), ws[pl.ds(2 * n, 2)].reshape(512, MODEL))
        for k in range(8):
            stage[:, pl.ds(4096 + k * 512, 512)] = act_term[k * 64 : k * 64 + 64]

        def chunk(r, _):
            rows = pl.ds(pl.multiple_of(r * 16, 16), 16)
            at = pl.ds(pl.multiple_of(lax.rem(r, 4) * 16, 16), 16)
            across = r // 4
            pre = stage[at, pl.ds(pl.multiple_of(across * 512, 512), 512)]
            pre = pre + bias_e[pl.ds(0, 1), cols]
            square = pre * pre
            inner = jnp.tanh(GELU_A * (pre + GELU_B * (square * pre)))
            cover = 0.5 + 0.5 * inner
            act[g, rows, cols] = (pre * cover).astype(low)
            slope = cover + 0.5 * pre * (1.0 - inner * inner) * (
                GELU_A + (3.0 * GELU_A * GELU_B) * square
            )
            d_act = stage[at, pl.ds(pl.multiple_of(4096 + across * 512, 512), 512)]
            d_pre[g, rows, cols] = (d_act * slope).astype(low)
            return 0

        lax.fori_loop(0, 32, chunk, 0, unroll=4)
        return 0

    def up_bias():
        odd = lax.rem(t, 2) == 1
        half = t // 2
        left = lane < HEAD
        bias_e[...] = jnp.zeros_like(bias_e)
        for j in range(8):
            r0 = vec_rows[pl.ds(96 + 8 * j + half, 1), :]
            r1 = vec_rows[pl.ds(100 + 8 * j + half, 1), :]
            even_row = jnp.where(left, r0, pltpu.roll(r1, HEAD, 1))
            odd_row = jnp.where(left, pltpu.roll(r0, HEAD, 1), r1)
            bias_e[pl.ds(0, 1), pl.ds(j * PAIR, PAIR)] = jnp.where(odd, odd_row, even_row)

    def up_task(i):
        def task():
            finish("e", "s")
            if i == 0:
                up_bias()
            lax.fori_loop(i, i + 1, up_tile, 0)

        return task

    def expand_tile(half):
        cols = pl.ds(half * 512, 512)

        def body(i, _):
            mine = normed[:, :, :, pl.ds(pl.multiple_of(i * 1024, 1024), 1024)].reshape(1024, 1024)
            term = cross(mine, d_pre[:, :, cols].reshape(1024, 512))
            ge[pl.ds(2 * i, 2), :, :, cols] = term.astype(low).reshape(2, 4, BLOCK, 512)
            return 0

        return body

    def give_e(half):
        def give(part, total):
            cols = pl.ds(half * 512, 512)
            res_e[pl.ds(2 * part, 2), :, cols] = total.astype(low).reshape(2, 16, 512)

        return give

    def shrink_tile(half):
        cols = pl.ds(half * 1024, 1024)

        def body(j, _):
            mine = act[:, :, pl.ds(pl.multiple_of(j * 512, 512), 512)].reshape(1024, 512)
            term = cross(mine, d_out[:, :, :, cols].reshape(1024, 1024))
            gs[pl.ds(2 * j, 2), :, :, cols] = term.astype(low).reshape(2, 4, 64, 1024)
            return 0

        return body

    def give_s(half):
        def give(part, total):
            gs_out[pl.ds(part * 16, 16), pl.ds(half * 1024, 1024)] = total

        return give

    def down_task(g, half):
        def task():
            term = dot_t(qkv[g], wq[2 * half : 2 * half + 2].reshape(1024, 768)) + dot_t(
                d_pre[g], we[2 * half : 2 * half + 2].reshape(1024, 1024)
            )
            cols = pl.ds(half * 1024, 1024)
            normed[g, :, :, cols] = term.astype(low).reshape(4, BLOCK, 1024)

        return task

    def give_n(half):
        def give(high, r, total):
            at = pl.ds(pl.multiple_of(r * 16, 16), 16)
            stage[at, pl.ds(high * 2048 + half * 1024, 1024)] = total

        return give

    def out_task(g, half):
        def task():
            cols = pl.ds(half * 1024, 1024)
            term = dot(att[g], wd[:, :, :, cols].reshape(256, 1024)) + dot(
                act[g], ws[:, :, :, cols].reshape(1024, 1024)
            )
            d_out[g, :, :, cols] = term.astype(low).reshape(4, BLOCK, 1024)

        return task

    def give_o(half):
        def give(high, r, total):
            rows = pl.ds(pl.multiple_of(high * 64 + r * 16, 16), 16)
            cols = pl.ds(half * 1024, 1024)
            add_bias = row_of(vec_rows, 80 + half * 8, 8) + row_of(vec_rows, 160 + half * 8, 8)
            out_ref[rows, cols] = (tokens_ref[rows, cols].astype(f32) + (total + add_bias)).astype(low)

        return give

    def norm_back():
        finish("n0", "n1")
        gain = row_of(vec_rows, 0, 16)
        vec_sum[...] = jnp.zeros_like(vec_sum)

        def chunk(r, _):
            rows = pl.ds(pl.multiple_of(r * 16, 16), 16)
            at = pl.ds(pl.multiple_of(lax.rem(r, 4) * 16, 16), 16)
            total = stage[at, pl.ds(pl.multiple_of((r // 4) * 2048, 2048), 2048)]
            xhat, spread = scaled(rows)
            e = total * gain
            mean_e = jnp.mean(e, axis=1, keepdims=True)
            mean_x = jnp.mean(e * xhat, axis=1, keepdims=True)
            dy = d_out_rows(rows, r * 16)
            ig_ref[rows, :] = (dy + spread * (e - mean_e - xhat * mean_x)).astype(low)
            for i, value in enumerate((total * xhat, total, dy)):
                vec_sum[i] += value[0:8] + value[8:16]
            return 0

        lax.fori_loop(0, 8, chunk, 0)
        vec_part[...] = jnp.zeros_like(vec_part)
        for i in range(3):
            total = jnp.sum(vec_sum[i], axis=0, keepdims=True)
            for k in range(8):
                vec_part[k, pl.ds(i, 1), :] = total[:, k * 256 : k * 256 + 256]

    def column_sums():
        ones = jnp.ones((8, 1024), low)
        vec_mine[...] = jnp.zeros_like(vec_mine)
        qkv_sum = dot(ones, qkv[...].reshape(1024, 768))
        for i in range(6):
            vec_mine[pl.ds(6 + i, 1), :] = qkv_sum[0:1, i * PAIR : (i + 1) * PAIR]
        pre_sum = dot(ones, d_pre[...].reshape(1024, 1024))
        for i in range(8):
            vec_mine[pl.ds(12 + i, 1), :] = pre_sum[0:1, i * PAIR : (i + 1) * PAIR]

    def loop(first, last, tile):
        return lambda: lax.fori_loop(first, last, tile, 0)

    tasks = {
        "vec_rows": vec_task, "norm_own": norm_own, "norm_sides": norm_sides, "norm_far": norm_far,
        "d_att": d_att_task, "qkv0": qkv_task(0), "qkv1": qkv_task(1), "grad_d": loop(0, 2, dense_tile),
        "grad_q0": loop(0, 2, qkv_grad_tile), "grad_q1": loop(2, 4, qkv_grad_tile),
        "grad_e0": loop(0, 2, expand_tile(0)), "grad_e1": loop(0, 2, expand_tile(1)),
        "grad_s0": loop(0, 2, shrink_tile(0)), "grad_s1": loop(0, 2, shrink_tile(1)),
        "norm_back": norm_back, "col_sums": column_sums,
    }
    for i in range(4):
        tasks["att" + str(i)] = loop(i, i + 1, attend_tile)
        tasks["up" + str(i)] = up_task(i)
    for half in range(2):
        for at, g in (("a", 1 - c), ("b", c)):
            tasks["down" + at + str(half)] = down_task(g, half)
            tasks["out" + at + str(half)] = out_task(g, half)

    for name in SCHEDULE:
        if name in tasks:
            tasks[name]()
        else:
            advance(name)
    finish(*works)
    copies.finish()


def layer(tokens, cotangent, block_seq, seq_lengths, vectors, weights):
    low, f32 = jnp.bfloat16, jnp.float32
    vmem = pl.BlockSpec(memory_space=pltpu.VMEM)
    smem = pl.BlockSpec(memory_space=pltpu.SMEM)
    anywhere = pl.BlockSpec(memory_space=pl.ANY)
    turn = jnp.asarray(np.stack(rotary_constants())[:, : 3 * BLOCK])
    outs = [
        ((BLOCK, MODEL), low), ((BLOCK, MODEL), low), ((8, 16, 1024), low), ((8, 16, 768), low),
        ((16, MODEL), low), ((64, MODEL), f32), ((2, 4, 24, PAIR), f32),
    ]
    held = [
        ((4, 4, 128, 1024), low), ((4, 4, 128, 768), low), ((4, 4, 16, 2560), low),
        ((4, 4, 64, 2048), low), ((2, 4, 128, 2048), low), ((2, 4, 128, 2048), low),
        ((2, 512, 1024), low), ((2, 512, 1024), low), ((2, 512, 768), low), ((2, 512, 256), low),
        ((4, 4, 128, 1024), low), ((4, 4, 64, 1536), low), ((4, 4, 16, 2048), low),
        ((4, 4, 64, 2048), low), ((64, 8192), f32), ((8, 1024), f32),
        ((2, 4, 8, 128), f32), ((184, 128), f32),
        ((8, 16, 1024), low), ((8, 16, 768), low), ((16, 2048), low),
        ((2, 6, 4, 32, 1024), low), ((2, 6, 32, 1024), low),
        ((2, 6, 4, 16, 512), low), ((2, 6, 16, 512), low),
        ((2, 6, 4, 16, 2048), low), ((2, 6, 16, 2048), low),
        ((4, 128, 2048), low), ((6, 64, 2048), low),
        ((8, 16, 1024), low), ((8, 16, 768), low), ((16, 2048), low), ((8, 384), f32),
        ((3, 8, MODEL), f32), ((8, 8, 256), f32), ((8, 8, 256), f32), ((24, 128), f32),
        ((4, 4, 24, 128), f32),
    ]
    return pl.pallas_call(
        layer_kernel,
        in_specs=[vmem, vmem, smem, smem, vmem, vmem] + [anywhere] * 4,
        out_specs=[vmem] * 7,
        out_shape=[jax.ShapeDtypeStruct(s, k) for s, k in outs],
        scratch_shapes=[pltpu.VMEM(s, k) for s, k in held]
        + [
            pltpu.SemaphoreType.DMA((COPIES,)),
            pltpu.SemaphoreType.DMA((COPIES,)),
            pltpu.SemaphoreType.DMA((7,)),
            pltpu.SemaphoreType.REGULAR((2,)),
            pltpu.SemaphoreType.REGULAR((2,)),
            pltpu.SemaphoreType.REGULAR,
        ],
        compiler_params=pltpu.CompilerParams(
            collective_id=0, has_side_effects=True, vmem_limit_bytes=64 * 2**20
        ),
        name="layer",
    )(tokens, cotangent, block_seq, seq_lengths, vectors[None, :], turn, *weights)


def update_kernel(out_in, ig_in, ge, gq, gd, gs, vec, *refs):
    f32 = jnp.float32
    masters, moments, seconds = refs[0:5], refs[5:10], refs[10:15]
    out_ref, ig_ref = refs[15:17]
    results = [refs[17 + 3 * i : 20 + 3 * i] for i in range(5)]
    flat = refs[32]
    out_ref[...] = out_in[...]
    ig_ref[...] = ig_in[...]

    def update(i, at, gradient):
        grad_ref, state_ref, new_ref = results[i]
        grad_ref[at] = gradient
        state, new = adam_step(
            masters[i][at], moments[i][at], seconds[i][at], gradient, RATES[i], DECAYS[i]
        )
        state_ref[at] = state
        new_ref[at] = new

    every = slice(None)
    for s in range(3):
        for hi in range(2):
            for t in range(TPN):
                col = s * MODEL + hi * 1024 + t * PAIR
                piece = gq[t, :, pl.ds((2 * s + 1 - hi) * PAIR, PAIR)].astype(f32)
                update(0, (every, pl.ds(col, PAIR)), piece)
    for k in range(16):
        cols = (every, pl.ds(k * PAIR, PAIR))
        update(1, cols, gd[cols].astype(f32))
        for r in range(4):
            at = (pl.ds(16 * r, 16), pl.ds(k * PAIR, PAIR))
            update(3, at, gs[at])
    left = lax.broadcasted_iota(jnp.int32, (16, PAIR), 1) < HEAD
    for j in range(16):
        for k in range(4):
            first = ge[2 * k, :, pl.ds((j // 2) * PAIR, PAIR)].astype(f32)
            second = ge[2 * k + 1, :, pl.ds((j // 2) * PAIR, PAIR)].astype(f32)
            if j % 2 == 0:
                second = pltpu.roll(second, HEAD, 1)
            else:
                first = pltpu.roll(first, HEAD, 1)
            update(2, (every, pl.ds(j * 512 + k * PAIR, PAIR)), jnp.where(left, first, second))

    flat[...] = jnp.zeros_like(flat)
    left = lax.broadcasted_iota(jnp.int32, (1, PAIR), 1) < HEAD

    def line(t, row):
        return vec[t // 4, t % 4, pl.ds(row, 1), :]

    for t in range(TPN):
        for i in range(2):
            for row, base in ((0, 0), (1, 16), (2, 80), (2, 160)):
                flat[pl.ds(base + 2 * t + i, 1), :] = line(t, 2 * row + i)
        for s in range(3):
            for hi in range(2):
                at = 32 + s * 16 + hi * 8 + t
                flat[pl.ds(at, 1), :] = line(t, 6 + 2 * s + 1 - hi)
    for j in range(16):
        for k in range(4):
            first = line(2 * k, 12 + j // 2)
            second = line(2 * k + 1, 12 + j // 2)
            if j % 2 == 0:
                second = pltpu.roll(second, HEAD, 1)
            else:
                first = pltpu.roll(first, HEAD, 1)
            flat[pl.ds(96 + 4 * j + k, 1), :] = jnp.where(left, first, second)
    z, y, c, x = (lax.axis_index(a) for a in ALL)
    number = ((z * 4 + y) * 2 + c) * 4 + x
    first = (176 * number) // 128
    own = jnp.concatenate([flat[pl.ds(first + i, 1), :] for i in range(3)], axis=1)
    own = jnp.broadcast_to(own, (8, 3 * PAIR))
    own = pltpu.roll(own, lax.rem(3 * PAIR - 16 * lax.rem(3 * number, 8), 3 * PAIR), 1)
    update(4, (every, every), own[0:1, 0:176])


def update_all(parts, masters, moments, seconds):
    f32 = jnp.float32
    vmem = pl.BlockSpec(memory_space=pltpu.VMEM)
    shapes = [jax.ShapeDtypeStruct(p.shape, p.dtype) for p in parts[:2]]
    for w in masters:
        shapes += [jax.ShapeDtypeStruct(w.shape, f32)] * 3
    return pl.pallas_call(
        update_kernel,
        in_specs=[vmem] * 22,
        out_specs=[vmem] * 17,
        out_shape=shapes,
        scratch_shapes=[pltpu.VMEM((184, PAIR), f32)],
        compiler_params=pltpu.CompilerParams(vmem_limit_bytes=62 * 2**20),
        name="update",
    )(*parts, *masters, *moments, *seconds)


def adam_step(weight, moment, second, gradient, step_rate, step_decay):
    moment_new = BETA_ONE * moment + (1 - BETA_ONE) * gradient
    second_new = BETA_TWO * second + (1 - BETA_TWO) * gradient * gradient
    moment_hat = moment_new / (1 - BETA_ONE**STEP)
    second_hat = second_new / (1 - BETA_TWO**STEP)
    updated = weight - step_rate * (
        moment_hat / (jnp.sqrt(second_hat) + ADAM_EPS) + step_decay * weight
    )
    return (second_new, updated)


def shards(
    tokens, cotangent, block_seq, seq_lengths,
    qkv_weight, qkv_moment, qkv_second,
    dense_weight, dense_moment, dense_second,
    expand_weight, expand_moment, expand_second,
    shrink_weight, shrink_moment, shrink_second,
    vectors, vec_moment, vec_second,
):
    parts = layer(
        tokens,
        cotangent,
        block_seq,
        seq_lengths,
        vectors,
        (qkv_weight, dense_weight, expand_weight, shrink_weight),
    )
    masters = (qkv_weight, dense_weight, expand_weight, shrink_weight, vectors[None, :])
    moments = (qkv_moment, dense_moment, expand_moment, shrink_moment, vec_moment[None, :])
    seconds = (qkv_second, dense_second, expand_second, shrink_second, vec_second[None, :])
    results = update_all(parts, masters, moments, seconds)
    return (*results[:14], *(r[0] for r in results[14:]))


def solution(mesh):
    finer = Mesh(mesh.devices.reshape(*SIZES), ALL)
    whole, group = P(ALL, None), P(DP, None)
    return jax.shard_map(
        shards,
        mesh=finer,
        in_specs=(whole, whole, group, group, *[whole] * 12, *[P(ALL)] * 3),
        out_specs=(*[whole] * 14, *[P(ALL)] * 3),
        check_vma=False,
    )
```

```python
import functools

import jax
import jax.numpy as jnp
import numpy as np
from jax import lax
from jax.experimental import pallas as pl
from jax.experimental.pallas import tpu as pltpu
from jax.sharding import Mesh
from jax.sharding import PartitionSpec as P

HEAD = 64
ROT = 32
BLOCK = 128
STEP = 10
GROUP = 512
MODEL = 2048
FF = 8192
PAIR = 2 * HEAD
ALL = ("z", "y", "c", "x")
DP = ("z", "y", "c")
ZY = ("z", "y")
TP = ("c", "x")
SIZES = (4, 4, 2, 4)
TPN = 8
COPIES = 480
SCHEDULE = (
    "vec", "to_q", "s", "to_d", "d", "tok", "q", "s", "to_e", "cot", "vec_rows", "q", "e",
    "norm_own", "cot", "q", "norm_sides", "q", "norm_far", "q", "cot", "e", "d_att", "s",
    "qkv0", "e", "qkv1", "att0", "att1", "s", "att2", "e", "att3", "e", "s", "grad_q0",
    "grad_q1", "sum_q", "grad_d", "up0", "up1", "sum_d", "up2", "sum_q", "up3", "grad_e0",
    "sum_d", "grad_e1", "sum_e1", "downa1", "n1", "sum_q", "downa0", "n0", "sum_d", "sum_e0",
    "downb1", "n1", "downb0", "n0", "sum_q", "sum_e1", "grad_s0", "sum_d", "grad_s1", "sum_e0",
    "back_q", "outa1", "n1", "col_sums", "sum_s0", "sum_e1", "outb1", "back_d", "n0", "sum_e0",
    "sum_s1", "o1", "outa0", "sum_e1", "norm_back", "o1", "o0", "back_e", "sum_s1", "sum_s0",
    "vec_back", "outb0", "o0", "vec_back", "sum_s1", "o1", "sum_s0", "o0", "sum_s1", "sum_s0",
    "vec_back", "sum_s1",
)
SCALE = HEAD ** (-0.5)

NORM_EPS = 1e-05
MASKED = -1e30
BETA_ONE = 0.9
BETA_TWO = 0.999
ADAM_EPS = 1e-08
RATES = (0.02, 0.1, 0.02, 0.01, 0.4)
DECAYS = (0.1, 0.1, 0.1, 0.1, 0.0)
GELU_A = float(np.sqrt(2.0 / np.pi))
GELU_B = 0.044715


def dot(a, b):
    return jnp.dot(a, b, preferred_element_type=jnp.float32)


def dot_t(a, b):
    return lax.dot_general(a, b, (((1,), (1,)), ((), ())), preferred_element_type=jnp.float32)


def cross(a, b):
    return lax.dot_general(a, b, (((0,), (0,)), ((), ())), preferred_element_type=jnp.float32)


def rotary_constants():
    half = np.arange(ROT // 2, dtype=np.float32)
    inverse = (10000.0 ** (-2.0 * half.astype(np.float64) / ROT)).astype(np.float32)
    angle = (np.arange(GROUP, dtype=np.float32)[:, None] * inverse[None, :]).astype(np.float64)
    cosine, sine = np.cos(angle).astype(np.float32), np.sin(angle).astype(np.float32)
    one = np.ones((GROUP, HEAD - ROT), np.float32)
    zero = np.zeros((GROUP, ROT // 2), np.float32)
    rest = np.zeros((GROUP, HEAD - ROT), np.float32)
    turn = np.concatenate([cosine, cosine, one], axis=1)
    ahead = np.concatenate([-sine, zero, rest], axis=1)
    behind = np.concatenate([zero, sine, rest], axis=1)
    return tuple(np.concatenate([a, a], axis=1) for a in (turn, ahead, behind))


MESH = pl.DeviceIdType.MESH


def other(axis, step):
    size = SIZES[ALL.index(axis)]
    return lax.rem(lax.axis_index(axis) + step + size, size)


class Copy:
    def __init__(self, copy):
        self.copy, self.here, self.gone = copy, False, False

    def arrive(self):
        if not self.here:
            self.copy.wait_recv()
        self.here = True

    def leave(self):
        if not self.gone:
            self.copy.wait_send()
        self.gone = True


class Copies:
    def __init__(self, send, recv):
        self.send, self.recv, self.all = send, recv, []

    def start(self, src, dst, to):
        at = len(self.all)
        copy = pltpu.make_async_remote_copy(
            src_ref=src,
            dst_ref=dst,
            send_sem=self.send.at[at],
            recv_sem=self.recv.at[at],
            device_id=to,
            device_id_type=MESH,
        )
        copy.start()
        self.all.append(Copy(copy))
        return self.all[-1]

    def finish(self):
        for copy in self.all:
            copy.leave()


def greet():
    barrier = pltpu.get_barrier_semaphore()
    for partner in token_partners() + weight_partners() + [dense_partner()]:
        pl.semaphore_signal(barrier, inc=1, device_id=partner, device_id_type=MESH)


def enter():
    pl.semaphore_wait(pltpu.get_barrier_semaphore(), 23)


def token_partners():
    return [{"c": other("c", i), "x": other("x", j)} for i in range(2) for j in range(4) if i + j]


def weight_partners():
    return [{"z": other("z", i), "y": other("y", j)} for i in range(4) for j in range(4) if i + j]


def dense_partner():
    z, y, c, x = (lax.axis_index(a) for a in ALL)
    return {"z": (1 - z // 2) * 2 + c, "y": x, "c": lax.rem(z, 2), "x": y}


def gather_weights(copies, view):
    z, y = lax.axis_index("z"), lax.axis_index("y")
    z_up, z_down, y_up, y_down = other("z", 1), other("z", -1), other("y", 1), other("y", -1)
    z_far, y_far = other("z", 2), other("y", 2)
    up, down, far, near = {"y": y_up}, {"y": y_down}, {"z": z_up}, {"z": z_down}

    def go(block, to):
        return copies.start(block, block, to)

    a_up, a_down = go(view(z, y, 4), up), go(view(z, y, 4), down)
    b_up, b_down = go(view(z, y, 5), far), go(view(z, y, 5), near)
    a_own = go(view(z, y, 4), far), go(view(z, y, 4), near)
    b_own = go(view(z, y, 5), up), go(view(z, y, 5), down)
    yield
    a_up.arrive()
    a_low = go(view(z, y_down, 0), up)
    b_up.arrive()
    b_low = go(view(z_down, y, 2), far)
    a_down.arrive()
    a_high = go(view(z, y_up, 1), down)
    b_down.arrive()
    b_high = go(view(z_up, y, 3), near)
    a_side = [(i, go(view(z, i, 4), far), go(view(z, i, 4), near)) for i in (y_down, y_up)]
    b_side = [(i, go(view(i, y, 5), up), go(view(i, y, 5), down)) for i in (z_down, z_up)]
    yield
    last = []
    a_own[0].arrive()
    last.append(go(view(z_down, y, 0), far))
    b_own[0].arrive()
    last.append(go(view(z, y_down, 2), up))
    a_own[1].arrive()
    last.append(go(view(z_up, y, 1), near))
    b_own[1].arrive()
    last.append(go(view(z, y_up, 3), down))
    a_low.arrive()
    a_high.arrive()
    a_side.append((y_far, go(view(z, y_far, 4), far), go(view(z, y_far, 4), near)))
    b_low.arrive()
    b_high.arrive()
    b_side.append((z_far, go(view(z_far, y, 5), up), go(view(z_far, y, 5), down)))
    for k in range(3):
        if k != 1:
            yield
        i, first, second = a_side[k]
        first.arrive()
        last.append(go(view(z_down, i, 0), far))
        second.arrive()
        last.append(go(view(z_up, i, 1), near))
        i, first, second = b_side[k]
        first.arrive()
        last.append(go(view(i, y_down, 2), up))
        second.arrive()
        last.append(go(view(i, y_up, 3), down))
    yield
    for copy in last:
        copy.arrive()


def gather_tokens(copies, ref, sent):
    c, x, across = lax.axis_index("c"), lax.axis_index("x"), other("c", 1)
    right, left = {"x": other("x", 1)}, {"x": other("x", -1)}

    def go(block, to):
        return copies.start(block, block, to)

    own = ref.at[c, x]
    sent.append([go(own, right), go(own, left), go(own, {"c": across})])
    yield
    sent[0][0].arrive()
    last = [go(ref.at[c, other("x", -1), pl.ds(0, 64)], right)]
    side = [go(ref.at[c, other("x", -1)], {"c": across})]
    sent[0][1].arrive()
    last.append(go(ref.at[c, other("x", 1), pl.ds(64, 64)], left))
    side.append(go(ref.at[c, other("x", 1)], {"c": across}))
    sent.append(last + side)
    yield
    for copy in last:
        copy.arrive()
    sent.append([go(ref.at[c, other("x", 2)], {"c": across})])
    yield
    for copies_of_stage in sent:
        for copy in copies_of_stage:
            copy.arrive()
            copy.leave()


def gather_vectors(copies, group, rows, place):
    c, x = lax.axis_index("c"), lax.axis_index("x")
    sent = [copies.start(group.at[c, x], group.at[c, x], to) for to in token_partners()]
    yield
    for copy in sent:
        copy.arrive()
    rows[pl.ds(0, 16), :] = jnp.zeros((16, PAIR), jnp.float32)
    for d in range(TPN):
        rows[pl.ds((176 * d) // PAIR, 3), :] += group[d // 4, d % 4, pl.ds(0, 3), :]
    place[:, pl.ds(0, PAIR)] = rows[pl.ds(0, 16), :].astype(jnp.bfloat16)
    place[:, pl.ds(PAIR, 3 * PAIR)] = jnp.zeros((16, 3 * PAIR), jnp.bfloat16)


def expand_to_group(copies, send, ref, width):
    z, y, c, x = (lax.axis_index(a) for a in ALL)
    rows = pl.ds(pl.multiple_of((c * 4 + x) * 16, 16), 16)
    sent = []
    for to in token_partners():
        sent.append(copies.start(send.at[to["c"] * 4 + to["x"]], ref.at[z, y, rows], to))
    ref[z, y, rows] = send[c * 4 + x]
    yield
    for copy in sent:
        copy.arrive()


def by_rows(ref, rows):
    quarter = rows // 4

    def view(z, y, part):
        start, size = (part * quarter, quarter) if part < 4 else ((part - 4) * 2 * quarter, 2 * quarter)
        return ref.at[z, y, pl.ds(start, size)]

    return view


def by_columns(ref, columns):
    quarter = columns // 4

    def view(z, y, part):
        start, size = (part * quarter, quarter) if part < 4 else ((part - 4) * 2 * quarter, 2 * quarter)
        return ref.at[z, y, :, pl.ds(start, size)]

    return view


def step(*works):
    for work in works:
        next(work, None)


def row_of(ref, first, count):
    return jnp.concatenate([ref[pl.ds(first + i, 1), :] for i in range(count)], axis=1)


def ring_sum(copies, axis, block, land, low_part, high_part):
    ahead, behind = other(axis, 1), other(axis, -1)
    up, down = {axis: ahead}, {axis: behind}
    far = other(axis, 2)
    t_low = copies.start(block(far, low_part), land.at[0], up)
    t_high = copies.start(block(far, high_part), land.at[1], down)
    d_high = copies.start(block(ahead, high_part), land.at[3], up)
    d_low = copies.start(block(behind, low_part), land.at[2], down)
    yield
    t_low.arrive()
    land[0] = land[0] + block(ahead, low_part)[...]
    p_low = copies.start(land.at[0], land.at[4], up)
    t_high.arrive()
    land[1] = land[1] + block(behind, high_part)[...]
    p_high = copies.start(land.at[1], land.at[5], down)
    yield
    for copy in (d_low, d_high, p_low, p_high):
        copy.arrive()
    for copy in (t_low, t_high, d_low, d_high, p_low, p_high):
        copy.leave()


def three(own, land, high, at=...):
    f32 = jnp.float32
    first, second = land.at[4 + high], land.at[2 + high]
    return own[at].astype(f32) + first[at].astype(f32) + second[at].astype(f32)


def both(first, second):
    while True:
        done = [next(first, 0), next(second, 0)]
        if 0 in done:
            return
        yield


def scatter_weights(copies, view, wide, narrow, give):
    z, y = lax.axis_index("z"), lax.axis_index("y")
    every = slice(None)
    low = jnp.bfloat16
    yield from both(
        ring_sum(copies, "y", lambda i, p: view(every, i, p), wide.at[0], 0, 1),
        ring_sum(copies, "z", lambda i, p: view(i, every, p), wide.at[1], 2, 3),
    )
    for high in range(2):
        own = view(every, y, high)
        for i in range(4):
            own[i] = three(own, wide.at[0], high, i).astype(low)
        own = view(z, every, 2 + high)
        for i in range(4):
            own[i] = three(own, wide.at[1], high, i).astype(low)
    yield from both(
        ring_sum(copies, "z", lambda i, p: view(i, y, p), narrow.at[0], 0, 1),
        ring_sum(copies, "y", lambda i, p: view(z, i, p), narrow.at[1], 2, 3),
    )
    for high in range(2):
        give(high, three(view(z, y, high), narrow.at[0], high))
        give(2 + high, three(view(z, y, 2 + high), narrow.at[1], high))


def scatter_tokens(copies, ref, core_land, land, give, core_free, ring_free, first):
    c, x, across = lax.axis_index("c"), lax.axis_index("x"), other("c", 1)
    if not first:
        pl.semaphore_wait(core_free, 1)
    came = copies.start(ref.at[across], core_land, {"c": across})
    yield
    came.arrive()
    for i in range(4):
        ref[c, i] = ref[c, i] + core_land[i]
    if first:
        pl.semaphore_signal(core_free, inc=1, device_id={"c": across}, device_id_type=MESH)
    else:
        pl.semaphore_wait(ring_free, 2)
    yield from ring_sum(copies, "x", lambda i, p: ref.at[c, i, pl.ds(p * 64, 64)], land, 0, 1)
    for high in range(2):
        own = ref.at[c, x, pl.ds(high * 64, 64)]

        def chunk(r, _):
            rows = pl.ds(pl.multiple_of(r * 16, 16), 16)
            give(high, r, three(own, land, high, rows))
            return 0

        lax.fori_loop(0, 4, chunk, 0)
    if first:
        for way in (1, -1):
            to = {"x": other("x", way)}
            pl.semaphore_signal(ring_free, inc=1, device_id=to, device_id_type=MESH)


def landed(copy):
    yield
    copy.arrive()


def sum_vectors(copies, part, came, mine, zy, out):
    z, y, c, x = (lax.axis_index(a) for a in ALL)
    t = c * 4 + x
    sent = [
        copies.start(part.at[to["c"] * 4 + to["x"]], came.at[t], to) for to in token_partners()
    ]
    came[t] = part[t]
    yield
    for copy in sent:
        copy.arrive()
    total = jnp.sum(came[...], axis=0)
    for i in range(6):
        mine[pl.ds(i, 1), :] = total[i // 2 : i // 2 + 1, (i % 2) * PAIR : (i % 2 + 1) * PAIR]
    zy[z, y] = mine[...]
    sent = [copies.start(mine, zy.at[z, y], to) for to in weight_partners()]
    yield
    for copy in sent:
        copy.arrive()
    out[c, x] = jnp.sum(zy[...].reshape(16, 24, PAIR), axis=0)
    sent = [copies.start(out.at[c, x], out.at[c, x], to) for to in token_partners()]
    yield
    for copy in sent:
        copy.arrive()


def return_to_group(copies, ref, out):
    c, x = lax.axis_index("c"), lax.axis_index("x")
    t = c * 4 + x
    sent = []
    for to in token_partners():
        sent.append(copies.start(ref.at[to["c"] * 4 + to["x"]], out.at[t], to))
    out[t] = ref[t]
    yield
    for copy in sent:
        copy.arrive()


def turned(values, table, sign):
    turn, ahead, behind = table
    up = pltpu.roll(values, PAIR - ROT // 2, 1)
    down = pltpu.roll(values, ROT // 2, 1)
    if sign > 0:
        return values * turn + up * ahead + down * behind
    return values * turn - up * ahead - down * behind


def attend(meta, turn_ref, qkv, att, g, p):
    low, f32 = jnp.bfloat16, jnp.float32
    lane = lax.broadcasted_iota(jnp.int32, (BLOCK, PAIR), 1)
    first = lane < HEAD
    zero = jnp.zeros((BLOCK, PAIR), low)
    row_at = lax.broadcasted_iota(jnp.int32, (BLOCK, BLOCK), 0)
    col_at = lax.broadcasted_iota(jnp.int32, (BLOCK, BLOCK), 1)
    cols = [pl.ds(pl.multiple_of(i * 2 * PAIR + p * PAIR, PAIR), PAIR) for i in range(3)]
    d_k = [jnp.zeros((BLOCK, PAIR), f32) for _ in range(4)]
    d_v = [jnp.zeros((BLOCK, PAIR), f32) for _ in range(4)]
    held = [qkv[g, :, cols[i]] for i in range(3)] + [att[g, :, cols[0]]]
    done = []
    for b in range(4):
        rows, width = slice(b * BLOCK, (b + 1) * BLOCK), (b + 1) * BLOCK
        base = meta[:, 4 + b : 5 + b] * BLOCK
        diagonal = (col_at <= row_at) & (col_at.astype(f32) + base < meta[:, 8 + b : 9 + b])
        bias = [
            jnp.where(meta[:, e : e + 1] == meta[:, b : b + 1], 0.0, MASKED)
            + jnp.zeros((BLOCK, BLOCK), f32)
            for e in range(b)
        ]
        bias.append(jnp.where(diagonal, 0.0, MASKED).astype(f32))
        bias = bias[0] if b == 0 else jnp.concatenate(bias, axis=1)
        q, da, k, v = held[0][rows], held[3][rows], held[1][:width], held[2][:width]
        qs = jnp.concatenate([jnp.where(first, q, zero), jnp.where(first, zero, q)], axis=0)
        das = jnp.concatenate([jnp.where(first, da, zero), jnp.where(first, zero, da)], axis=0)
        scores = dot_t(qs, k) + jnp.concatenate([bias, bias], axis=0)
        w = jnp.exp(scores - jnp.max(scores, axis=1, keepdims=True))
        prob = w * (1.0 / jnp.sum(w, axis=1, keepdims=True))
        prob_low = prob.astype(low)
        summed = dot(prob_low, v)
        dp = dot_t(das, v)
        ds = (prob * (dp - jnp.sum(prob * dp, axis=1, keepdims=True))).astype(low)
        dq = dot(ds, k)
        dq = jnp.where(first, dq[:BLOCK], dq[BLOCK:]) * SCALE
        dq = turned(dq, table_of(meta, turn_ref, b), -1).astype(low)
        done.append((jnp.where(first, summed[:BLOCK], summed[BLOCK:]).astype(low), dq))
        dk = cross(ds, qs)
        dv = cross(prob_low, das)
        for e in range(b + 1):
            d_k[e] = d_k[e] + dk[e * BLOCK : (e + 1) * BLOCK]
            d_v[e] = d_v[e] + dv[e * BLOCK : (e + 1) * BLOCK]
    for b in range(4):
        rows = pl.ds(b * BLOCK, BLOCK)
        att[g, rows, cols[0]], qkv[g, rows, cols[0]] = done[b]
        qkv[g, rows, cols[1]] = turned(d_k[b], table_of(meta, turn_ref, b), -1).astype(low)
        qkv[g, rows, cols[2]] = d_v[b].astype(low)


def table_of(meta, turn_ref, b):
    rank = meta[:, 4 + b : 5 + b]
    parts = [turn_ref[:, pl.ds(r * BLOCK, BLOCK), :] for r in range(3)]
    table = jnp.where((rank == 0.0)[None], parts[0], jnp.where((rank == 1.0)[None], parts[1], parts[2]))
    return table[0], table[1], table[2]


def layer_kernel(
    tokens_ref, cot_ref, seq_ref, length_ref, vec_ref, turn_ref, q_hbm, d_hbm, e_hbm, s_hbm,
    out_ref, ig_ref, ge_out, gq_out, gd_out, gs_out, vec_out,
    we, wq, wd, ws, normed, d_out, act, d_pre, qkv, att,
    ge, gq, gd, gs, stage, bias_e, vec_group, vec_rows, we_send, wq_send, wd_own,
    wide_e, narrow_e, wide_d, narrow_d, wide_s, narrow_s,
    core_land, ring_land, res_e, res_q, res_d,
    vec_line, vec_sum, vec_part, vec_came, vec_mine, vec_zy,
    send, recv, local, core_free, ring_free, wide_free,
):
    low, f32 = jnp.bfloat16, jnp.float32
    z, y, c, x = (lax.axis_index(a) for a in ALL)
    t = c * 4 + x
    copies = Copies(send, recv)
    greet()

    loads = [
        pltpu.make_async_copy(q_hbm, stage.at[pl.ds(16, 16), pl.ds(0, 6144)], local.at[0]),
        pltpu.make_async_copy(d_hbm, stage.at[pl.ds(16, 16), pl.ds(6144, 2048)], local.at[1]),
        pltpu.make_async_copy(e_hbm, stage.at[pl.ds(0, 16)], local.at[2]),
    ]
    for k in range(4):
        rows = pl.ds(16 * k, 16)
        place = stage.at[pl.ds(32, 16), pl.ds(2048 * k, 2048)]
        loads.append(pltpu.make_async_copy(s_hbm.at[rows], place, local.at[3 + k]))
    for load in loads:
        load.start()

    lane = lax.broadcasted_iota(jnp.int32, (1, PAIR), 1)
    seqs = [seq_ref[0, b] for b in range(4)]
    own_meta = jnp.zeros((1, PAIR), f32)
    own_rank, own_limit = jnp.zeros((1, 1), f32), jnp.zeros((1, 1), f32)
    for b in range(4):
        rank = jnp.int32(0)
        for e in range(b):
            rank = rank + jnp.where(seqs[e] == seqs[b], 1, 0)
        limit = jnp.where(seqs[b] == 0, length_ref[0, 0], length_ref[0, 1])
        for at, value in ((b, seqs[b]), (4 + b, rank), (8 + b, limit)):
            own_meta = jnp.where(lane == at, value.astype(f32), own_meta)
        own_rank = jnp.where(x == b, rank.astype(f32), own_rank)
        own_limit = jnp.where(x == b, limit.astype(f32), own_limit)
    vec_line[...] = jnp.zeros_like(vec_line)
    vec_line[pl.ds(0, 1), pl.ds(0, 176)] = vec_ref[...].astype(low).astype(f32)
    line = pltpu.roll(vec_line[...], 16 * lax.rem(3 * t + 24 * (z * 4 + y), 8), 1)
    vec_own = vec_group.at[c, x]
    vec_own[...] = jnp.zeros((8, PAIR), f32)
    for k in range(3):
        vec_own[pl.ds(k, 1), :] = line[0:1, k * PAIR : (k + 1) * PAIR]
    vec_own[pl.ds(4, 1), :] = own_meta

    def d_out_rows(rows, first):
        row_at = lax.broadcasted_iota(jnp.int32, (16, 1), 0) + first
        live = (row_at.astype(f32) + own_rank * BLOCK < own_limit).astype(f32)
        return cot_ref[rows, :].astype(f32) * live

    def mask_chunk(r, _):
        rows = pl.ds(pl.multiple_of(r * 16, 16), 16)
        d_out[c, x, rows] = d_out_rows(rows, r * 16).astype(low)
        return 0


    def scaled(rows):
        values = tokens_ref[rows, :].astype(f32)
        middle = values - jnp.mean(values, axis=1, keepdims=True)
        spread = lax.rsqrt(jnp.mean(middle * middle, axis=1, keepdims=True) + NORM_EPS)
        return middle * spread, spread

    def scale_chunk(r, _):
        rows = pl.ds(pl.multiple_of(r * 16, 16), 16)
        normed[c, x, rows] = scaled(rows)[0].astype(low)
        return 0

    lax.fori_loop(0, 8, scale_chunk, 0)
    loads[0].wait()
    for k in range(8):
        for i in range(6):
            col = (i // 2) * 2048 + (1 - i % 2) * 1024 + k * PAIR
            piece = stage[pl.ds(16, 16), pl.ds(col, PAIR)]
            wq_send[k, :, pl.ds(i * PAIR, PAIR)] = piece.astype(low)
    enter()

    def cast_dense():
        loads[1].wait()
        wd_own[...] = stage[pl.ds(16, 16), pl.ds(6144, 2048)].astype(low)

    def cast_expand():
        left16 = lax.broadcasted_iota(jnp.int32, (16, PAIR), 1) < HEAD
        loads[2].wait()
        for j in range(8):
            for k in range(4):
                first = stage[pl.ds(0, 16), pl.ds(j * 1024 + k * PAIR, PAIR)]
                second = stage[pl.ds(0, 16), pl.ds(j * 1024 + 512 + k * PAIR, PAIR)]
                even = jnp.where(left16, first, pltpu.roll(second, HEAD, 1))
                odd = jnp.where(left16, pltpu.roll(first, HEAD, 1), second)
                we_send[2 * k, :, pl.ds(j * PAIR, PAIR)] = even.astype(low)
                we_send[2 * k + 1, :, pl.ds(j * PAIR, PAIR)] = odd.astype(low)

    def cast_shrink():
        for k in range(4):
            loads[3 + k].wait()
            ws[z, y, pl.ds(16 * k, 16)] = stage[pl.ds(32, 16), pl.ds(2048 * k, 2048)].astype(low)

    works, stages, tasks, finished = {}, {}, {}, set()
    token_sends = []

    def finish(*names):
        for name in names:
            for _ in works[name]:
                pass
            finished.add(name)

    def advance(name):
        if name not in works:
            works[name], stages[name] = begin(name), 0
        stages[name] += 1
        if next(works[name], 0) == 0:
            finished.add(name)

    def reach(name, stage):
        while stages[name] < stage:
            advance(name)

    def begin(name):
        if name == "vec":
            return gather_vectors(copies, vec_group, vec_rows, wd.at[z, y, :, pl.ds(MODEL, 512)])
        if name == "to_q":
            return expand_to_group(copies, wq_send, wq, 768)
        if name == "to_e":
            cast_expand()
            return expand_to_group(copies, we_send, we, 1024)
        if name == "to_d":
            cast_dense()
            there = dense_partner()
            place = wd.at[there["z"], there["y"], :, pl.ds(0, MODEL)]
            return landed(copies.start(wd_own, place, there))
        if name == "q":
            finish("to_q")
            return gather_weights(copies, by_rows(wq, 128))
        if name == "d":
            finish("to_d", "vec")
            return gather_weights(copies, by_columns(wd, 2560))
        if name == "e":
            finish("to_e")
            return gather_weights(copies, by_rows(we, 128))
        if name == "s":
            cast_shrink()
            return gather_weights(copies, by_rows(ws, 64))
        if name == "cot":
            lax.fori_loop(0, 8, mask_chunk, 0)
            return gather_tokens(copies, d_out, [])
        if name == "tok":
            return gather_tokens(copies, normed, token_sends)
        if name == "sum_d":
            return scatter_weights(copies, by_columns(gd, 2048), wide_d, narrow_d, give_d)
        if name == "sum_q":
            return sum_q()
        if name in ("sum_e0", "sum_e1"):
            half = int(name[-1])
            cols = pl.ds(half * 512, 512)
            return scatter_weights(
                copies,
                by_rows(ge.at[:, :, :, cols], 128),
                wide_e.at[:, :, :, :, cols],
                narrow_e.at[:, :, :, cols],
                give_e(half),
            )
        if name in ("sum_s0", "sum_s1"):
            finish("sum_q")
            if "wide" not in finished:
                pl.semaphore_wait(wide_free, 4)
                finished.add("wide")
            half = int(name[-1])
            cols = pl.ds(half * 1024, 1024)
            return scatter_weights(
                copies,
                by_rows(gs.at[:, :, :, cols], 64),
                wide_s.at[:, :, :, :, cols],
                narrow_s.at[:, :, :, cols],
                give_s(half),
            )
        if name in ("n0", "n1", "o0", "o1"):
            half = int(name[-1])
            if name[0] == "o":
                finish("n" + name[1])
            cols = pl.ds(half * 1024, 1024)
            return scatter_tokens(
                copies,
                (normed if name[0] == "n" else d_out).at[:, :, :, cols],
                core_land.at[:, :, cols],
                ring_land.at[:, :, cols],
                (give_n if name[0] == "n" else give_o)(half),
                core_free.at[half],
                ring_free.at[half],
                name[0] == "n",
            )
        if name == "back_q":
            finish("sum_q")
            return return_to_group(copies, res_q, gq_out)
        if name == "back_e":
            finish("sum_e0", "sum_e1")
            return return_to_group(copies, res_e, ge_out)
        if name == "back_d":
            finish("sum_d")
            return landed(copies.start(res_d, gd_out, dense_partner()))
        return sum_vectors(copies, vec_part, vec_came, vec_mine, vec_zy, vec_out)

    def vec_task():
        finish("d")
        for i in range(16):
            block = wd[i // 4, i % 4, :, pl.ds(MODEL, PAIR)].astype(f32)
            vec_rows[pl.ds(11 * i, 11), :] = block[0:11]

    def norm_blocks(blocks):
        def chunk(r, _):
            rows = pl.ds(pl.multiple_of(r * 16, 16), 16)
            for core, chip in blocks:
                xhat = normed[core, chip, rows].astype(f32)
                whole = xhat * row_of(vec_rows, 0, 16) + row_of(vec_rows, 16, 16)
                normed[core, chip, rows] = whole.astype(low)
            return 0

        lax.fori_loop(0, 8, chunk, 0)

    def norm_own():
        reach("tok", 2)
        for copy in token_sends[0]:
            copy.leave()
        token_sends[0][2].arrive()
        norm_blocks([(c, x), (1 - c, x)])

    def norm_sides():
        reach("tok", 3)
        for copy in token_sends[1]:
            copy.leave()
        for copy in token_sends[1][2:]:
            copy.arrive()
        for way in (-1, 1):
            norm_blocks([(c, other("x", way)), (1 - c, other("x", way))])

    def norm_far():
        finish("tok")
        token_sends[2][0].leave()
        norm_blocks([(c, other("x", 2)), (1 - c, other("x", 2))])

    def qkv_tile(g, _):
        meta = vec_group[g, x, pl.ds(4, 1), :]
        projected = dot(normed[g].reshape(512, MODEL), wq[...].reshape(MODEL, 768))
        for p in range(6):
            bias = vec_rows[pl.ds(32 + (p // 2) * 16 + (1 - p % 2) * 8 + t, 1), :]
            for b in range(4):
                rows = pl.ds(b * BLOCK, BLOCK)
                part = projected[b * BLOCK : (b + 1) * BLOCK, p * PAIR : (p + 1) * PAIR] + bias
                if p < 4:
                    part = turned(part, table_of(meta, turn_ref, b), 1)
                part = part.astype(low)
                if p < 2:
                    part = part * jnp.asarray(SCALE, low)
                qkv[g, rows, pl.ds(p * PAIR, PAIR)] = part
        return 0

    def d_att_tile(g, _):
        dense = wd[:, :, :, pl.ds(0, MODEL)].reshape(256, MODEL)
        att[g] = dot_t(d_out[g].reshape(512, MODEL), dense).astype(low)
        return 0

    def d_att_task():
        finish("cot", "d")
        lax.fori_loop(0, 2, d_att_tile, 0)

    def qkv_task(g):
        def task():
            finish("tok", "q")
            lax.fori_loop(g, g + 1, qkv_tile, 0)

        return task

    def attend_tile(i, _):
        g, p = i // 2, lax.rem(i, 2)
        attend(vec_group[g, x, pl.ds(4, 1), :], turn_ref, qkv, att, g, p)
        return 0

    def dense_tile(n, _):
        cols = pl.ds(pl.multiple_of(n * 1024, 1024), 1024)
        term = cross(att[...].reshape(1024, 256), d_out[:, :, :, cols].reshape(1024, 1024))
        gd[:, :, :, cols] = term.astype(low).reshape(4, 4, 16, 1024)
        return 0

    def give_d(part, total):
        res_d[:, pl.ds(part * 512, 512)] = total.astype(low)

    def qkv_grad_tile(i, _):
        mine = normed[:, :, :, pl.ds(pl.multiple_of(i * 512, 512), 512)].reshape(1024, 512)
        term = cross(mine, qkv[...].reshape(1024, 768)).astype(low).reshape(4, BLOCK, 768)
        gq[i, :, :, pl.ds(0, 768)] = term[:, :64]
        gq[i, :, :, pl.ds(768, 768)] = term[:, 64:]
        return 0

    def give_q(part, total):
        res_q[part] = total[:, :768].astype(low)
        res_q[4 + part] = total[:, 768:].astype(low)

    def sum_q():
        short = pl.ds(0, 1536)
        yield from scatter_weights(
            copies,
            by_rows(gq, 64),
            wide_s.at[:, :, :, :, short],
            narrow_s.at[:, :, :, short],
            give_q,
        )
        for axis in ("y", "z"):
            for way in (1, -1):
                to = {axis: other(axis, way)}
                pl.semaphore_signal(wide_free, inc=1, device_id=to, device_id_type=MESH)

    def up_tile(i, _):
        g, n = i // 2, lax.rem(i, 2)
        cols = pl.ds(pl.multiple_of(n * 512, 512), 512)
        pre_term = dot(normed[g].reshape(512, MODEL), we[:, :, :, cols].reshape(MODEL, 512))
        for k in range(8):
            stage[:, pl.ds(k * 512, 512)] = pre_term[k * 64 : k * 64 + 64]
        act_term = dot_t(d_out[g].reshape(512, MODEL), ws[pl.ds(2 * n, 2)].reshape(512, MODEL))
        for k in range(8):
            stage[:, pl.ds(4096 + k * 512, 512)] = act_term[k * 64 : k * 64 + 64]

        def chunk(r, _):
            rows = pl.ds(pl.multiple_of(r * 16, 16), 16)
            at = pl.ds(pl.multiple_of(lax.rem(r, 4) * 16, 16), 16)
            across = r // 4
            pre = stage[at, pl.ds(pl.multiple_of(across * 512, 512), 512)]
            pre = pre + bias_e[pl.ds(0, 1), cols]
            square = pre * pre
            inner = jnp.tanh(GELU_A * (pre + GELU_B * (square * pre)))
            cover = 0.5 + 0.5 * inner
            act[g, rows, cols] = (pre * cover).astype(low)
            slope = cover + 0.5 * pre * (1.0 - inner * inner) * (
                GELU_A + (3.0 * GELU_A * GELU_B) * square
            )
            d_act = stage[at, pl.ds(pl.multiple_of(4096 + across * 512, 512), 512)]
            d_pre[g, rows, cols] = (d_act * slope).astype(low)
            return 0

        lax.fori_loop(0, 32, chunk, 0, unroll=4)
        return 0

    def up_bias():
        odd = lax.rem(t, 2) == 1
        half = t // 2
        left = lane < HEAD
        bias_e[...] = jnp.zeros_like(bias_e)
        for j in range(8):
            r0 = vec_rows[pl.ds(96 + 8 * j + half, 1), :]
            r1 = vec_rows[pl.ds(100 + 8 * j + half, 1), :]
            even_row = jnp.where(left, r0, pltpu.roll(r1, HEAD, 1))
            odd_row = jnp.where(left, pltpu.roll(r0, HEAD, 1), r1)
            bias_e[pl.ds(0, 1), pl.ds(j * PAIR, PAIR)] = jnp.where(odd, odd_row, even_row)

    def up_task(i):
        def task():
            finish("e", "s")
            if i == 0:
                up_bias()
            lax.fori_loop(i, i + 1, up_tile, 0)

        return task

    def expand_tile(half):
        cols = pl.ds(half * 512, 512)

        def body(i, _):
            mine = normed[:, :, :, pl.ds(pl.multiple_of(i * 1024, 1024), 1024)].reshape(1024, 1024)
            term = cross(mine, d_pre[:, :, cols].reshape(1024, 512))
            ge[pl.ds(2 * i, 2), :, :, cols] = term.astype(low).reshape(2, 4, BLOCK, 512)
            return 0

        return body

    def give_e(half):
        def give(part, total):
            cols = pl.ds(half * 512, 512)
            res_e[pl.ds(2 * part, 2), :, cols] = total.astype(low).reshape(2, 16, 512)

        return give

    def shrink_tile(half):
        cols = pl.ds(half * 1024, 1024)

        def body(j, _):
            mine = act[:, :, pl.ds(pl.multiple_of(j * 512, 512), 512)].reshape(1024, 512)
            term = cross(mine, d_out[:, :, :, cols].reshape(1024, 1024))
            gs[pl.ds(2 * j, 2), :, :, cols] = term.astype(low).reshape(2, 4, 64, 1024)
            return 0

        return body

    def give_s(half):
        def give(part, total):
            gs_out[pl.ds(part * 16, 16), pl.ds(half * 1024, 1024)] = total

        return give

    def down_task(g, half):
        def task():
            term = dot_t(qkv[g], wq[2 * half : 2 * half + 2].reshape(1024, 768)) + dot_t(
                d_pre[g], we[2 * half : 2 * half + 2].reshape(1024, 1024)
            )
            cols = pl.ds(half * 1024, 1024)
            normed[g, :, :, cols] = term.astype(low).reshape(4, BLOCK, 1024)

        return task

    def give_n(half):
        def give(high, r, total):
            at = pl.ds(pl.multiple_of(r * 16, 16), 16)
            stage[at, pl.ds(high * 2048 + half * 1024, 1024)] = total

        return give

    def out_task(g, half):
        def task():
            cols = pl.ds(half * 1024, 1024)
            term = dot(att[g], wd[:, :, :, cols].reshape(256, 1024)) + dot(
                act[g], ws[:, :, :, cols].reshape(1024, 1024)
            )
            d_out[g, :, :, cols] = term.astype(low).reshape(4, BLOCK, 1024)

        return task

    def give_o(half):
        def give(high, r, total):
            rows = pl.ds(pl.multiple_of(high * 64 + r * 16, 16), 16)
            cols = pl.ds(half * 1024, 1024)
            add_bias = row_of(vec_rows, 80 + half * 8, 8) + row_of(vec_rows, 160 + half * 8, 8)
            out_ref[rows, cols] = (tokens_ref[rows, cols].astype(f32) + (total + add_bias)).astype(low)

        return give

    def norm_back():
        finish("n0", "n1")
        gain = row_of(vec_rows, 0, 16)
        vec_sum[...] = jnp.zeros_like(vec_sum)

        def chunk(r, _):
            rows = pl.ds(pl.multiple_of(r * 16, 16), 16)
            at = pl.ds(pl.multiple_of(lax.rem(r, 4) * 16, 16), 16)
            total = stage[at, pl.ds(pl.multiple_of((r // 4) * 2048, 2048), 2048)]
            xhat, spread = scaled(rows)
            e = total * gain
            mean_e = jnp.mean(e, axis=1, keepdims=True)
            mean_x = jnp.mean(e * xhat, axis=1, keepdims=True)
            dy = d_out_rows(rows, r * 16)
            ig_ref[rows, :] = (dy + spread * (e - mean_e - xhat * mean_x)).astype(low)
            for i, value in enumerate((total * xhat, total, dy)):
                vec_sum[i] += value[0:8] + value[8:16]
            return 0

        lax.fori_loop(0, 8, chunk, 0)
        vec_part[...] = jnp.zeros_like(vec_part)
        for i in range(3):
            total = jnp.sum(vec_sum[i], axis=0, keepdims=True)
            for k in range(8):
                vec_part[k, pl.ds(i, 1), :] = total[:, k * 256 : k * 256 + 256]

    def column_sums():
        ones = jnp.ones((8, 1024), low)
        vec_mine[...] = jnp.zeros_like(vec_mine)
        qkv_sum = dot(ones, qkv[...].reshape(1024, 768))
        for i in range(6):
            vec_mine[pl.ds(6 + i, 1), :] = qkv_sum[0:1, i * PAIR : (i + 1) * PAIR]
        pre_sum = dot(ones, d_pre[...].reshape(1024, 1024))
        for i in range(8):
            vec_mine[pl.ds(12 + i, 1), :] = pre_sum[0:1, i * PAIR : (i + 1) * PAIR]

    def loop(first, last, tile):
        return lambda: lax.fori_loop(first, last, tile, 0)

    tasks = {
        "vec_rows": vec_task, "norm_own": norm_own, "norm_sides": norm_sides, "norm_far": norm_far,
        "d_att": d_att_task, "qkv0": qkv_task(0), "qkv1": qkv_task(1), "grad_d": loop(0, 2, dense_tile),
        "grad_q0": loop(0, 2, qkv_grad_tile), "grad_q1": loop(2, 4, qkv_grad_tile),
        "grad_e0": loop(0, 2, expand_tile(0)), "grad_e1": loop(0, 2, expand_tile(1)),
        "grad_s0": loop(0, 2, shrink_tile(0)), "grad_s1": loop(0, 2, shrink_tile(1)),
        "norm_back": norm_back, "col_sums": column_sums,
    }
    for i in range(4):
        tasks["att" + str(i)] = loop(i, i + 1, attend_tile)
        tasks["up" + str(i)] = up_task(i)
    for half in range(2):
        for at, g in (("a", 1 - c), ("b", c)):
            tasks["down" + at + str(half)] = down_task(g, half)
            tasks["out" + at + str(half)] = out_task(g, half)

    for name in SCHEDULE:
        if name in tasks:
            tasks[name]()
        else:
            advance(name)
    finish(*works)
    copies.finish()


def layer(tokens, cotangent, block_seq, seq_lengths, vectors, weights):
    low, f32 = jnp.bfloat16, jnp.float32
    vmem = pl.BlockSpec(memory_space=pltpu.VMEM)
    smem = pl.BlockSpec(memory_space=pltpu.SMEM)
    anywhere = pl.BlockSpec(memory_space=pl.ANY)
    turn = jnp.asarray(np.stack(rotary_constants())[:, : 3 * BLOCK])
    outs = [
        ((BLOCK, MODEL), low), ((BLOCK, MODEL), low), ((8, 16, 1024), low), ((8, 16, 768), low),
        ((16, MODEL), low), ((64, MODEL), f32), ((2, 4, 24, PAIR), f32),
    ]
    held = [
        ((4, 4, 128, 1024), low), ((4, 4, 128, 768), low), ((4, 4, 16, 2560), low),
        ((4, 4, 64, 2048), low), ((2, 4, 128, 2048), low), ((2, 4, 128, 2048), low),
        ((2, 512, 1024), low), ((2, 512, 1024), low), ((2, 512, 768), low), ((2, 512, 256), low),
        ((4, 4, 128, 1024), low), ((4, 4, 64, 1536), low), ((4, 4, 16, 2048), low),
        ((4, 4, 64, 2048), low), ((64, 8192), f32), ((8, 1024), f32),
        ((2, 4, 8, 128), f32), ((184, 128), f32),
        ((8, 16, 1024), low), ((8, 16, 768), low), ((16, 2048), low),
        ((2, 6, 4, 32, 1024), low), ((2, 6, 32, 1024), low),
        ((2, 6, 4, 16, 512), low), ((2, 6, 16, 512), low),
        ((2, 6, 4, 16, 2048), low), ((2, 6, 16, 2048), low),
        ((4, 128, 2048), low), ((6, 64, 2048), low),
        ((8, 16, 1024), low), ((8, 16, 768), low), ((16, 2048), low), ((8, 384), f32),
        ((3, 8, MODEL), f32), ((8, 8, 256), f32), ((8, 8, 256), f32), ((24, 128), f32),
        ((4, 4, 24, 128), f32),
    ]
    return pl.pallas_call(
        layer_kernel,
        in_specs=[vmem, vmem, smem, smem, vmem, vmem] + [anywhere] * 4,
        out_specs=[vmem] * 7,
        out_shape=[jax.ShapeDtypeStruct(s, k) for s, k in outs],
        scratch_shapes=[pltpu.VMEM(s, k) for s, k in held]
        + [
            pltpu.SemaphoreType.DMA((COPIES,)),
            pltpu.SemaphoreType.DMA((COPIES,)),
            pltpu.SemaphoreType.DMA((7,)),
            pltpu.SemaphoreType.REGULAR((2,)),
            pltpu.SemaphoreType.REGULAR((2,)),
            pltpu.SemaphoreType.REGULAR,
        ],
        compiler_params=pltpu.CompilerParams(
            collective_id=0, has_side_effects=True, vmem_limit_bytes=64 * 2**20
        ),
        name="layer",
    )(tokens, cotangent, block_seq, seq_lengths, vectors[None, :], turn, *weights)


def update_kernel(out_in, ig_in, ge, gq, gd, gs, vec, *refs):
    f32 = jnp.float32
    masters, moments, seconds = refs[0:5], refs[5:10], refs[10:15]
    out_ref, ig_ref = refs[15:17]
    results = [refs[17 + 3 * i : 20 + 3 * i] for i in range(5)]
    flat = refs[32]
    out_ref[...] = out_in[...]
    ig_ref[...] = ig_in[...]

    def update(i, at, gradient):
        grad_ref, state_ref, new_ref = results[i]
        grad_ref[at] = gradient
        state, new = adam_step(
            masters[i][at], moments[i][at], seconds[i][at], gradient, RATES[i], DECAYS[i]
        )
        state_ref[at] = state
        new_ref[at] = new

    every = slice(None)
    for s in range(3):
        for hi in range(2):
            for t in range(TPN):
                col = s * MODEL + hi * 1024 + t * PAIR
                piece = gq[t, :, pl.ds((2 * s + 1 - hi) * PAIR, PAIR)].astype(f32)
                update(0, (every, pl.ds(col, PAIR)), piece)
    for k in range(16):
        cols = (every, pl.ds(k * PAIR, PAIR))
        update(1, cols, gd[cols].astype(f32))
        for r in range(4):
            at = (pl.ds(16 * r, 16), pl.ds(k * PAIR, PAIR))
            update(3, at, gs[at])
    left = lax.broadcasted_iota(jnp.int32, (16, PAIR), 1) < HEAD
    for j in range(16):
        for k in range(4):
            first = ge[2 * k, :, pl.ds((j // 2) * PAIR, PAIR)].astype(f32)
            second = ge[2 * k + 1, :, pl.ds((j // 2) * PAIR, PAIR)].astype(f32)
            if j % 2 == 0:
                second = pltpu.roll(second, HEAD, 1)
            else:
                first = pltpu.roll(first, HEAD, 1)
            update(2, (every, pl.ds(j * 512 + k * PAIR, PAIR)), jnp.where(left, first, second))

    flat[...] = jnp.zeros_like(flat)
    left = lax.broadcasted_iota(jnp.int32, (1, PAIR), 1) < HEAD

    def line(t, row):
        return vec[t // 4, t % 4, pl.ds(row, 1), :]

    for t in range(TPN):
        for i in range(2):
            for row, base in ((0, 0), (1, 16), (2, 80), (2, 160)):
                flat[pl.ds(base + 2 * t + i, 1), :] = line(t, 2 * row + i)
        for s in range(3):
            for hi in range(2):
                at = 32 + s * 16 + hi * 8 + t
                flat[pl.ds(at, 1), :] = line(t, 6 + 2 * s + 1 - hi)
    for j in range(16):
        for k in range(4):
            first = line(2 * k, 12 + j // 2)
            second = line(2 * k + 1, 12 + j // 2)
            if j % 2 == 0:
                second = pltpu.roll(second, HEAD, 1)
            else:
                first = pltpu.roll(first, HEAD, 1)
            flat[pl.ds(96 + 4 * j + k, 1), :] = jnp.where(left, first, second)
    z, y, c, x = (lax.axis_index(a) for a in ALL)
    number = ((z * 4 + y) * 2 + c) * 4 + x
    first = (176 * number) // 128
    own = jnp.concatenate([flat[pl.ds(first + i, 1), :] for i in range(3)], axis=1)
    own = jnp.broadcast_to(own, (8, 3 * PAIR))
    own = pltpu.roll(own, lax.rem(3 * PAIR - 16 * lax.rem(3 * number, 8), 3 * PAIR), 1)
    update(4, (every, every), own[0:1, 0:176])


def update_all(parts, masters, moments, seconds):
    f32 = jnp.float32
    vmem = pl.BlockSpec(memory_space=pltpu.VMEM)
    shapes = [jax.ShapeDtypeStruct(p.shape, p.dtype) for p in parts[:2]]
    for w in masters:
        shapes += [jax.ShapeDtypeStruct(w.shape, f32)] * 3
    return pl.pallas_call(
        update_kernel,
        in_specs=[vmem] * 22,
        out_specs=[vmem] * 17,
        out_shape=shapes,
        scratch_shapes=[pltpu.VMEM((184, PAIR), f32)],
        compiler_params=pltpu.CompilerParams(vmem_limit_bytes=62 * 2**20),
        name="update",
    )(*parts, *masters, *moments, *seconds)


def adam_step(weight, moment, second, gradient, step_rate, step_decay):
    moment_new = BETA_ONE * moment + (1 - BETA_ONE) * gradient
    second_new = BETA_TWO * second + (1 - BETA_TWO) * gradient * gradient
    moment_hat = moment_new / (1 - BETA_ONE**STEP)
    second_hat = second_new / (1 - BETA_TWO**STEP)
    updated = weight - step_rate * (
        moment_hat / (jnp.sqrt(second_hat) + ADAM_EPS) + step_decay * weight
    )
    return (second_new, updated)


def shards(
    tokens, cotangent, block_seq, seq_lengths,
    qkv_weight, qkv_moment, qkv_second,
    dense_weight, dense_moment, dense_second,
    expand_weight, expand_moment, expand_second,
    shrink_weight, shrink_moment, shrink_second,
    vectors, vec_moment, vec_second,
):
    parts = layer(
        tokens,
        cotangent,
        block_seq,
        seq_lengths,
        vectors,
        (qkv_weight, dense_weight, expand_weight, shrink_weight),
    )
    masters = (qkv_weight, dense_weight, expand_weight, shrink_weight, vectors[None, :])
    moments = (qkv_moment, dense_moment, expand_moment, shrink_moment, vec_moment[None, :])
    seconds = (qkv_second, dense_second, expand_second, shrink_second, vec_second[None, :])
    results = update_all(parts, masters, moments, seconds)
    return (*results[:14], *(r[0] for r in results[14:]))


def solution(mesh):
    finer = Mesh(mesh.devices.reshape(*SIZES), ALL)
    whole, group = P(ALL, None), P(DP, None)
    return jax.shard_map(
        shards,
        mesh=finer,
        in_specs=(whole, whole, group, group, *[whole] * 12, *[P(ALL)] * 3),
        out_specs=(*[whole] * 14, *[P(ALL)] * 3),
        check_vma=False,
    )
```
